32 devices in a mesh: dp: 8 (over z, y), tensor: 4 (over x, core).
Axes of the slice: x: 2, y: 2, z: 4, core: 2. Of those that a mesh axis runs over, the one named last changes fastest.
Arguments:
- hidden_in: float32 [8192, 1536], P(('dp', 'tensor')), may hold values from -6 to 6
- norm_gain: float32 [1536], replicated, may hold values from 0.5 to 1.5
- gate_value_weight: bfloat16 [1536, 2, 3072], P('dp', None, 'tensor'), may hold values from -0.15625 to 0.15625
- state_proj_weight: bfloat16 [1536, 256], P('dp'), may hold values from -0.15625 to 0.15625
- step_weight: bfloat16 [1536, 48], P('dp', 'tensor'), may hold values from -0.15625 to 0.15625
- conv_value_kernel: float32 [3072, 4], P('tensor'), may hold values from -3 to 3
- conv_value_bias: float32 [3072], P('tensor'), may hold values from -3 to 3
- conv_state_kernel: float32 [256, 4], replicated, may hold values from -3 to 3
- conv_state_bias: float32 [256], replicated, may hold values from -3 to 3
- step_bias: float32 [48], P('tensor'), may hold values from -6 to -1
- decay_log: float32 [48], P('tensor'), may hold values from -3 to 2
- skip_scale: float32 [48], P('tensor'), may hold values from 0.5 to 1.5
- gate_norm_gain: float32 [3072], P('tensor'), may hold values from 0.5 to 1.5
- out_weight: bfloat16 [1536, 3072], P('dp', 'tensor'), may hold values from -0.109375 to 0.109375
- out_cotangent: float32 [8192, 1536], P(('dp', 'tensor')), may hold values from -6 to 6
- seq_lengths: int32 [32], replicated, may hold values from 0 to 1024, as said below
- seq_device: int32 [32], replicated, may hold values from 0 to 7, as said below
- seq_offset: int32 [32], replicated, may hold values from 0 to 3, as said below
Outputs:
- output: float32 [8192, 1536], P(('dp', 'tensor'))
- hidden_gradient: float32 [8192, 1536], P(('dp', 'tensor'))
- norm_gain_gradient: float32 [1536], P(('dp', 'tensor'))
- gate_value_weight_gradient: float32 [1536, 2, 3072], P('dp', None, 'tensor')
- state_proj_weight_gradient: float32 [1536, 256], P(('dp', 'tensor'))
- step_weight_gradient: float32 [1536, 48], P('dp', 'tensor')
- conv_value_kernel_gradient: float32 [3072, 4], P('tensor')
- conv_value_bias_gradient: float32 [3072], P('tensor')
- conv_state_kernel_gradient: float32 [256, 4], P(('dp', 'tensor'))
- conv_state_bias_gradient: float32 [256], P(('dp', 'tensor'))
- step_bias_gradient: float32 [48], P('tensor')
- decay_log_gradient: float32 [48], P('tensor')
- skip_scale_gradient: float32 [48], P('tensor')
- gate_norm_gain_gradient: float32 [3072], P('tensor')
- out_weight_gradient: float32 [1536, 3072], P('dp', 'tensor')
The draws below stay inside these ranges and needn't reach their ends.
Inputs may be any that keep to these rules, and one draw needn't show every extreme that they name: A slot with seq_lengths > 0 is a sequence that occupies spans seq_offset to seq_offset + ceil(seq_lengths / 256) - 1 of the 4 spans of dp index seq_device; sequences of one dp index never share a span; a slot of length 0 occupies nothing. Some sequence has length 1024, and some slot is empty. `seq_device`: each dp index is named by 4 slots. `seq_offset`: some sequence begins at the last span of its dp index.
All inputs are finite; a program needn't handle non-finite values.
Results may differ from the reference program's by a relative error of at most 0.011.
Values may be sent and summed in bfloat16 or wider, within the bound.
No kernel may reach another device: no remote copies, remote signals or barrier semaphores. Data moves between devices by JAX's collectives and lax.ppermute only.
A program may use at most 192 MiB of HBM per device.

```python
from functools import partial
import jax
import jax.numpy as jnp
from jax import lax

D = 1536
H = 48
N = 128
KCONV = 4
SPAN = 256
E = 3072
TOK_DEV = 1024
SEQ_DEV = 4
SEQS = 32
TOKENS = 8192
GROUPS = 4
N_DP = 8


def seq_layout(key):
    folded = jax.random.fold_in(key, 11)
    key_count, key_fill, key_full, key_tail, key_order = jax.random.split(folded, 5)
    devices = SEQS // SEQ_DEV
    counts = jax.random.randint(key_count, (devices, SEQ_DEV), 1, SEQ_DEV + 1)
    filled = jax.random.randint(key_fill, (devices,), 1, SEQ_DEV + 1)
    chosen = jax.random.randint(key_full, (), 0, devices)
    second = (chosen + 1) % devices
    device_index = jnp.arange(devices)[:, None]
    slot_index = jnp.arange(SEQ_DEV)[None, :]
    full_slot = (device_index == chosen) & (slot_index == 0)
    counts = jnp.where(full_slot, SEQ_DEV, counts)
    counts = jnp.where(device_index == second, 1, counts)
    filled = jnp.where(jnp.arange(devices) == chosen, SEQ_DEV, filled)
    filled = jnp.where(jnp.arange(devices) == second, SEQ_DEV, filled)
    filled = jnp.maximum(filled, counts[:, 0])
    finish = jnp.cumsum(counts, axis=1)
    occupied = finish <= filled[:, None]
    last_rows = jax.random.randint(key_tail, (devices, SEQ_DEV), 1, SPAN + 1)
    last_rows = jnp.where(full_slot, SPAN, last_rows)
    lengths = jnp.where(occupied, (counts - 1) * SPAN + last_rows, 0)
    offsets = jnp.where(occupied, finish - counts, 0)
    owners = jnp.broadcast_to(device_index, (devices, SEQ_DEV))
    shuffle = jax.random.permutation(key_order, SEQS)
    return (lengths.reshape(-1)[shuffle].astype(jnp.int32), owners.reshape(-1)[shuffle].astype(jnp.int32), offsets.reshape(-1)[shuffle].astype(jnp.int32))


def draw_seq_lengths(key, part):
    return seq_layout(key)[0]


def draw_seq_device(key, part):
    return seq_layout(key)[1]


def draw_seq_offset(key, part):
    return seq_layout(key)[2]


def levels(rng, dims, cuts, low, high):
    loudness, own = 1.0, jax.random.fold_in(rng, 6)
    for axis_at, parts in cuts:
        draws = jnp.exp(jax.random.uniform(jax.random.fold_in(own, axis_at), (parts,), jnp.float32, low / len(cuts), high / len(cuts)))
        loudness = loudness * jnp.repeat(draws, dims[axis_at] // parts).reshape([-1 if axis == axis_at else 1 for axis in range(len(dims))])
    return loudness


def noise(own_key, dims, deviation, bound, cuts=(), kind=jnp.bfloat16):
    drawn = deviation * jax.random.normal(own_key, dims, jnp.float32)
    if cuts:
        drawn = drawn * levels(own_key, dims, cuts, -0.22, 0.18)
    return jnp.clip(drawn, -bound, bound).astype(kind)


def setup_inputs(seed: int = 0) -> dict:
    arg_keys = jax.random.split(jax.random.key(seed), 19)
    return {
        "hidden_in": noise(arg_keys[0], (TOKENS, D), 1.0, 6.0, ((0, 32),), jnp.float32),
        "norm_gain": jnp.clip(1.0 + 0.1 * jax.random.normal(arg_keys[1], (D,), jnp.float32), 0.5, 1.5),
        "gate_value_weight": noise(arg_keys[2], (D, 2, E), D ** -0.5, 0.15625, ((0, 8), (2, 4))),
        "state_proj_weight": noise(arg_keys[3], (D, 2 * N), D ** -0.5, 0.15625, ((0, 8),)),
        "step_weight": noise(arg_keys[4], (D, H), D ** -0.5, 0.15625, ((0, 8), (1, 4))),
        "conv_value_kernel": noise(arg_keys[5], (E, KCONV), KCONV ** -0.5, 3.0, ((0, 4),), jnp.float32),
        "conv_value_bias": noise(arg_keys[6], (E,), 0.5, 3.0, ((0, 4),), jnp.float32),
        "conv_state_kernel": noise(arg_keys[7], (2 * N, KCONV), KCONV ** -0.5, 3.0, (), jnp.float32),
        "conv_state_bias": noise(arg_keys[8], (2 * N,), 0.5, 3.0, (), jnp.float32),
        "step_bias": jnp.clip(-6.0 + 5.0 * jax.random.uniform(arg_keys[9], (H,), jnp.float32) ** levels(arg_keys[9], (H,), ((0, 4),), -0.2, 0.2), -6.0, -1.0),
        "decay_log": jnp.clip(-3.0 + 5.0 * jax.random.uniform(arg_keys[10], (H,), jnp.float32) ** levels(arg_keys[10], (H,), ((0, 4),), -0.2, 0.2), -3.0, 2.0),
        "skip_scale": jnp.clip(0.5 + 1.0 * jax.random.uniform(arg_keys[11], (H,), jnp.float32) ** levels(arg_keys[11], (H,), ((0, 4),), -0.2, 0.2), 0.5, 1.5),
        "gate_norm_gain": jnp.clip(1.0 + 0.1 * jax.random.normal(arg_keys[12], (E,), jnp.float32), 0.5, 1.5),
        "out_weight": noise(arg_keys[13], (D, E), E ** -0.5, 0.109375, ((0, 8), (1, 4))),
        "out_cotangent": noise(arg_keys[14], (TOKENS, D), 1.0, 6.0, ((0, 32),), jnp.float32),
        "seq_lengths": draw_seq_lengths(jax.random.fold_in(arg_keys[18], 71), 0),
        "seq_device": draw_seq_device(jax.random.fold_in(arg_keys[18], 71), 0),
        "seq_offset": draw_seq_offset(jax.random.fold_in(arg_keys[18], 71), 0),
    }


EPSILON = 1e-05
HIGHEST = lax.Precision.HIGHEST

def span_layout(seq_lengths, seq_device, seq_offset, device):
    span_index = jnp.arange(SEQ_DEV, dtype=jnp.int32)
    needed = (seq_lengths + SPAN - 1) // SPAN
    owned_seq = (seq_device == device) & (seq_lengths > 0)
    relative = span_index[None, :] - seq_offset[:, None]
    inside = owned_seq[:, None] & (relative >= 0) & (relative < needed[:, None])
    live_rows = lax.optimization_barrier(jnp.sum(jnp.where(inside, jnp.clip(seq_lengths[:, None] - relative * SPAN, 0, SPAN), 0), axis=0))
    seq_first = jnp.any(inside & (relative == 0), axis=0)
    position = jnp.arange(TOK_DEV, dtype=jnp.int32) % SPAN
    row_mask = jnp.where(position < jnp.repeat(live_rows, SPAN), 1.0, 0.0).astype(jnp.float32)
    first_rows = jnp.repeat(seq_first, SPAN)
    keep_mask = jnp.stack([jnp.logical_not(first_rows & (position < shift_by)) for shift_by in range(KCONV)])
    return (row_mask, seq_first, keep_mask)

def causal_conv(values, kernel, offset_bias, keep_mask):
    row_count = values.shape[0]
    tap_count = kernel.shape[1]
    result = offset_bias[None, :] + kernel[:, tap_count - 1][None, :] * values
    for shift_by in range(1, tap_count):
        shifted = jnp.concatenate([jnp.zeros((shift_by, values.shape[1]), values.dtype), values[:row_count - shift_by]], axis=0)
        shifted = jnp.where(keep_mask[shift_by][:, None], shifted, 0.0)
        result = result + kernel[:, tap_count - 1 - shift_by][None, :] * shifted
    return result

def ssd_scan(values, b_state, c_state, step, decay_log, skip_scale, seq_first):
    row_count, head_count = step.shape
    head_width = values.shape[1] // head_count
    state_width = b_state.shape[1]
    span_count = row_count // SPAN
    log_decay = step * (-jnp.exp(decay_log))[None, :]
    lower_mask = jnp.arange(SPAN)[:, None] >= jnp.arange(SPAN)[None, :]
    scanned = (values.reshape(span_count, SPAN, head_count, head_width), b_state.reshape(span_count, SPAN, state_width), c_state.reshape(span_count, SPAN, state_width), step.reshape(span_count, SPAN, head_count), log_decay.reshape(span_count, SPAN, head_count), seq_first)

    def span_step(carried, block_data):
        value_blk, b_blk, c_blk, step_blk, decay_blk, starts = block_data
        carried = jnp.where(starts, jnp.zeros_like(carried), carried)
        cum_decay = jnp.cumsum(decay_blk, axis=0)
        scores_bc = jnp.dot(c_blk, b_blk.T, precision=HIGHEST)
        gap_log = jnp.where(lower_mask[:, :, None], cum_decay[:, None, :] - cum_decay[None, :, :], 0.0)
        weights = jnp.where(lower_mask[:, :, None], jnp.exp(gap_log), 0.0) * scores_bc[:, :, None] * step_blk[None, :, :]
        diag_part = jnp.einsum('tsh,shp->thp', weights, value_blk, precision=HIGHEST)
        carry_part = jnp.einsum('tn,hnp->thp', c_blk, carried, precision=HIGHEST) * jnp.exp(cum_decay)[:, :, None]
        tail_weight = jnp.exp(cum_decay[-1][None, :] - cum_decay) * step_blk
        updated = jnp.exp(cum_decay[-1])[:, None, None] * carried + jnp.einsum('sn,shp->hnp', b_blk, value_blk * tail_weight[:, :, None], precision=HIGHEST)
        result = diag_part + carry_part + skip_scale[None, :, None] * value_blk
        return (updated, result)
    zero_state = jnp.zeros((head_count, state_width, head_width), jnp.float32)
    _, outputs = lax.scan(jax.checkpoint(span_step), zero_state, scanned)
    return outputs.reshape(row_count, head_count * head_width)

def mixer_core(seq_first, keep_mask, gate_raw, value_raw, bc_raw, step_raw, conv_value_kernel, conv_value_bias, conv_state_kernel, conv_state_bias, step_bias, decay_log, skip_scale):
    values = jax.nn.silu(causal_conv(value_raw, conv_value_kernel, conv_value_bias, keep_mask))
    bc_conv = jax.nn.silu(causal_conv(bc_raw, conv_state_kernel, conv_state_bias, keep_mask))
    state_width = bc_raw.shape[1] // 2
    step = jax.nn.softplus(step_raw + step_bias[None, :])
    mixed = ssd_scan(values, bc_conv[:, :state_width], bc_conv[:, state_width:], step, decay_log, skip_scale, seq_first)
    return mixed * jax.nn.silu(gate_raw)

def reference(hidden_in, norm_gain, gate_value_weight, state_proj_weight, step_weight, conv_value_kernel, conv_value_bias, conv_state_kernel, conv_state_bias, step_bias, decay_log, skip_scale, gate_norm_gain, out_weight, out_cotangent, seq_lengths, seq_device, seq_offset):
    group_width = E // GROUPS
    group_heads = H // GROUPS
    value_flat = gate_value_weight.reshape(D, 2 * E)

    def block_pass(totals, block_data):
        hidden, cotangent, device = block_data
        row_mask, seq_first, keep_mask = span_layout(seq_lengths, seq_device, seq_offset, device)
        inv_rms = lax.rsqrt(lax.optimization_barrier(jnp.mean(hidden * hidden, axis=-1)) + EPSILON)
        scaled = hidden * inv_rms[:, None]
        normed = (scaled * norm_gain[None, :]).astype(jnp.bfloat16)
        gate_value = jnp.dot(normed, value_flat, preferred_element_type=jnp.float32).reshape(TOK_DEV, 2, E)
        bc_raw = jnp.dot(normed, state_proj_weight, preferred_element_type=jnp.float32)
        step_raw = jnp.dot(normed, step_weight, preferred_element_type=jnp.float32)
        pieces = []
        pullbacks = []
        for group_index in range(GROUPS):
            columns = slice(group_index * group_width, (group_index + 1) * group_width)
            head_range = slice(group_index * group_heads, (group_index + 1) * group_heads)
            gated_part, pullback = jax.vjp(partial(mixer_core, seq_first, keep_mask), gate_value[:, 0, columns], gate_value[:, 1, columns], bc_raw, step_raw[:, head_range], conv_value_kernel[columns], conv_value_bias[columns], conv_state_kernel, conv_state_bias, step_bias[head_range], decay_log[head_range], skip_scale[head_range])
            pieces.append(gated_part)
            pullbacks.append(pullback)
        gated = jnp.concatenate(pieces, axis=1)
        gate_inv = lax.rsqrt(lax.optimization_barrier(jnp.mean(gated * gated, axis=-1)) + EPSILON)
        unit_norm = gated * gate_inv[:, None]
        normed_y = (unit_norm * gate_norm_gain[None, :]).astype(jnp.bfloat16)
        mixer_rows = jnp.dot(normed_y, out_weight.T, preferred_element_type=jnp.float32)
        result = hidden + row_mask[:, None] * mixer_rows
        back_mix = (row_mask[:, None] * cotangent).astype(jnp.bfloat16)
        out_weight_grad = jnp.dot(back_mix.T, normed_y, preferred_element_type=jnp.float32)
        back_y = jnp.dot(back_mix, out_weight, preferred_element_type=jnp.float32)
        gate_gain_grad = lax.optimization_barrier(jnp.sum(back_y * unit_norm, axis=0))
        weighted = back_y * gate_norm_gain[None, :]
        back_gated = gate_inv[:, None] * (weighted - unit_norm * lax.optimization_barrier(jnp.mean(weighted * unit_norm, axis=-1))[:, None])
        gate_list, value_list, step_list, state_list = ([], [], [], [])
        kernel_list, bias_list, stepb_list, decay_list, skip_list = ([], [], [], [], [])
        state_kernel_grad = jnp.zeros_like(conv_state_kernel)
        state_bias_grad = jnp.zeros_like(conv_state_bias)
        for group_index in range(GROUPS):
            columns = slice(group_index * group_width, (group_index + 1) * group_width)
            pulled = pullbacks[group_index](back_gated[:, columns])
            gate_list.append(pulled[0])
            value_list.append(pulled[1])
            state_list.append(pulled[2].astype(jnp.bfloat16))
            step_list.append(pulled[3])
            kernel_list.append(pulled[4])
            bias_list.append(pulled[5])
            state_kernel_grad = state_kernel_grad + pulled[6]
            state_bias_grad = state_bias_grad + pulled[7]
            stepb_list.append(pulled[8])
            decay_list.append(pulled[9])
            skip_list.append(pulled[10])
        back_gv = jnp.stack([jnp.concatenate(gate_list, axis=1), jnp.concatenate(value_list, axis=1)], axis=1).astype(jnp.bfloat16).reshape(TOK_DEV, 2 * E)
        back_step = jnp.concatenate(step_list, axis=1).astype(jnp.bfloat16)
        gv_grad = jnp.dot(normed.T, back_gv, preferred_element_type=jnp.float32).reshape(D, 2, E)
        step_grad = jnp.dot(normed.T, back_step, preferred_element_type=jnp.float32)
        back_normed = jnp.dot(back_gv, value_flat.T, preferred_element_type=jnp.float32) + jnp.dot(back_step, step_weight.T, preferred_element_type=jnp.float32)
        bc_grad = jnp.zeros((D, 2 * N), jnp.float32)
        for state_piece in state_list:
            bc_grad = bc_grad + jnp.dot(normed.T, state_piece, preferred_element_type=jnp.float32)
            back_normed = back_normed + jnp.dot(state_piece, state_proj_weight.T, preferred_element_type=jnp.float32)
        norm_grad = lax.optimization_barrier(jnp.sum(back_normed * scaled, axis=0))
        back_scaled = back_normed * norm_gain[None, :]
        hidden_grad = cotangent + inv_rms[:, None] * (back_scaled - scaled * lax.optimization_barrier(jnp.mean(back_scaled * scaled, axis=-1))[:, None])
        terms = (norm_grad, gv_grad, bc_grad, step_grad, jnp.concatenate(kernel_list, axis=0), jnp.concatenate(bias_list, axis=0), state_kernel_grad, state_bias_grad, jnp.concatenate(stepb_list, axis=0), jnp.concatenate(decay_list, axis=0), jnp.concatenate(skip_list, axis=0), gate_gain_grad, out_weight_grad)
        totals = tuple((total + term for total, term in zip(totals, terms)))
        return (totals, (result, hidden_grad))
    initial = (jnp.zeros((D,), jnp.float32), jnp.zeros((D, 2, E), jnp.float32), jnp.zeros((D, 2 * N), jnp.float32), jnp.zeros((D, H), jnp.float32), jnp.zeros((E, KCONV), jnp.float32), jnp.zeros((E,), jnp.float32), jnp.zeros((2 * N, KCONV), jnp.float32), jnp.zeros((2 * N,), jnp.float32), jnp.zeros((H,), jnp.float32), jnp.zeros((H,), jnp.float32), jnp.zeros((H,), jnp.float32), jnp.zeros((E,), jnp.float32), jnp.zeros((D, E), jnp.float32))
    blocks = (hidden_in.reshape(N_DP, TOK_DEV, D), out_cotangent.reshape(N_DP, TOK_DEV, D), jnp.arange(N_DP, dtype=jnp.int32))
    totals, (results, hidden_grads) = lax.scan(block_pass, initial, blocks)
    return (results.reshape(TOKENS, D), hidden_grads.reshape(TOKENS, D), totals[0], totals[1], totals[2], totals[3], totals[4], totals[5], totals[6], totals[7], totals[8], totals[9], totals[10], totals[11], totals[12])
```

```python
from functools import partial

import jax, jax.numpy as jnp
from jax import lax
from jax.experimental import pallas as pl
from jax.experimental.pallas import tpu as pltpu
from jax.sharding import PartitionSpec as P
f32=jnp.float32; bf16=jnp.bfloat16
Q=128
NS=128
VW=768
HW=64
CW=1024
RW=1152
SPAN=256
NEG=-1e30

def mm(a,b,ca=1,cb=0):
    return lax.dot_general(a,b,(((ca,),(cb,)),((),())),preferred_element_type=f32)

def split2(x):
    hi=x.astype(bf16); return hi,(x-hi.astype(f32)).astype(bf16)

def split3(x):
    hi=x.astype(bf16); r=x-hi.astype(f32); mid=r.astype(bf16); return hi,mid,(r-mid.astype(f32)).astype(bf16)

def tri_sum(tri,x):
    a,b,c=split3(x); w=x.shape[1]
    p=mm(tri,jnp.concatenate([a,b,c],axis=1))
    return p[:,:w]+p[:,w:2*w]+p[:,2*w:]

def spread(x,ee):
    a,b=split2(x)
    return mm(jnp.concatenate([a,b],axis=1),ee)

def head_sum(x,hh):
    a,b=split2(x)
    return mm(jnp.concatenate([a,b],axis=1),hh)

def iotas():
    return lax.broadcasted_iota(jnp.int32,(Q,Q),0),lax.broadcasted_iota(jnp.int32,(Q,Q),1)

def softplus(z):
    return jnp.maximum(z,0.0)+jnp.log(1.0+jnp.exp(-jnp.abs(z)))

def sig(z):
    return 1.0/(1.0+jnp.exp(-z))

def halves(x):
    lane=lax.broadcasted_iota(jnp.int32,x.shape,1)
    lo=jnp.where(lane<HW,x,0.0); hi=jnp.where(lane<HW,0.0,x)
    return jnp.concatenate([lo.astype(bf16),hi.astype(bf16)],axis=0)

def fwd_kernel(c0,nc,first_ref,raw_ref,ck_ref,cb_ref,sb_ref,dl_ref,ee_ref,s_in,t_in,y_ref,pre_ref,sp_ref,s_ref,t_ref,ext):
    i=pl.program_id(0)
    @pl.when(i==0)
    def _():
        s_ref[...]=s_in[...]; t_ref[...]=t_in[...]
    c=c0+i
    start=(first_ref[c//(SPAN//Q)]==1)&(c%(SPAN//Q)==0)
    @pl.when(start)
    def _():
        s_ref[...]=jnp.zeros_like(s_ref); t_ref[...]=jnp.zeros_like(t_ref)
    ext[0:8,:]=t_ref[...]
    x=raw_ref[:,:CW]
    ext[8:8+Q,:]=x
    t_ref[...]=raw_ref[Q-8:Q,:CW]
    pre=cb_ref[...]+ck_ref[3:4,:]*x
    for j in (1,2,3):
        pre=pre+ck_ref[3-j:4-j,:]*ext[8-j:8-j+Q,:]
    pre_ref[...]=pre
    act=pre*sig(pre)
    v=act[:,:VW]; b=act[:,VW:VW+NS].astype(bf16); cc=act[:,VW+NS:].astype(bf16)
    dt=softplus(raw_ref[:,CW:]+sb_ref[...])
    a=-dt*jnp.exp(dl_ref[...])
    row,col=iotas()
    low=row>=col
    tri=jnp.where(low,1.0,0.0).astype(bf16)
    cum=tri_sum(tri,a)
    cum_t=cum.T
    last=cum[Q-1:Q,:]
    ee=ee_ref[...]
    sprd=spread(jnp.concatenate([dt,jnp.exp(cum),jnp.exp(last-cum)],axis=0),ee)
    dte,ecum,etail=sprd[:Q],sprd[Q:2*Q],sprd[2*Q:]
    x=v*dte
    g=mm(cc,b,1,1)
    parts=[]
    for p in range(VW//128):
        ws=[]
        for h in (2*p,2*p+1):
            d=jnp.where(low,cum[:,h:h+1]-cum_t[h:h+1,:],NEG)
            ws.append((jnp.exp(d)*g).astype(bf16))
        parts.append(mm(jnp.concatenate(ws,axis=1),halves(x[:,128*p:128*p+128])))
    s=s_ref[...]
    sp_ref[0]=s
    y_ref[...]=jnp.concatenate(parts,axis=1)+ecum*mm(cc,s.astype(bf16))
    s_ref[...]=ecum[Q-1:Q,:]*s+mm(b,(x*etail).astype(bf16),0,0)

def bwd_kernel(c0,nc,nall,first_ref,raw_ref,pre_ref,y_ref,dy_ref,sp_ref,ck_ref,sb_ref,dl_ref,sk_ref,ee_ref,hh_ref,ds_in,sn_in,h_in,acc_in,acs_in,
               out_ref,ds_ref,sn_ref,h_ref,acc_ref,acs_ref,ext):
    i=pl.program_id(0)
    @pl.when(i==0)
    def _():
        ds_ref[...]=ds_in[...]; sn_ref[...]=sn_in[...]; h_ref[...]=h_in[...]; acc_ref[...]=acc_in[...]; acs_ref[...]=acs_in[...]
    c=c0+nc-1-i
    nxt=jnp.minimum(c+1,nall-1)
    start=(first_ref[nxt//(SPAN//Q)]==1)&(nxt%(SPAN//Q)==0)
    @pl.when(start)
    def _():
        ds_ref[...]=jnp.zeros_like(ds_ref); h_ref[...]=jnp.zeros_like(h_ref)
    pre=pre_ref[...]
    sg=sig(pre)
    act=pre*sg
    v=act[:,:VW]; b=act[:,VW:VW+NS].astype(bf16); cc=act[:,VW+NS:].astype(bf16)
    z=raw_ref[:,CW:]+sb_ref[...]
    dt=softplus(z)
    edl=jnp.exp(dl_ref[...])
    a=-dt*edl
    row,col=iotas()
    low=row>=col; up=row<=col
    cum=tri_sum(jnp.where(low,1.0,0.0).astype(bf16),a)
    cum_t=cum.T
    last=cum[Q-1:Q,:]
    ee=ee_ref[...]
    sprd=spread(jnp.concatenate([dt,jnp.exp(cum),jnp.exp(last-cum)],axis=0),ee)
    dte,ecum,etail=sprd[:Q],sprd[Q:2*Q],sprd[2*Q:]
    x=v*dte
    xb=x.astype(bf16)
    dy=dy_ref[...].astype(f32)
    dyb=dy.astype(bf16)
    gt=mm(b,cc,1,1)
    dgt=jnp.zeros((Q,Q),f32)
    parts=[]
    for p in range(VW//128):
        cols=slice(128*p,128*p+128)
        dw=mm(halves(x[:,cols]),dyb[:,cols],1,1)
        ws=[]
        for k in (0,1):
            h=2*p+k
            lt=jnp.exp(jnp.where(up,cum_t[h:h+1,:]-cum[:,h:h+1],NEG))
            ws.append((lt*gt).astype(bf16))
            dgt=dgt+lt*dw[k*Q:(k+1)*Q]
        parts.append(mm(jnp.concatenate(ws,axis=1),halves(dy[:,cols])))
    ds=ds_ref[...]
    dsb=ds.astype(bf16)
    s=sp_ref[0]
    dx=jnp.concatenate(parts,axis=1)+etail*mm(b,dsb)
    dgtb=dgt.astype(bf16)
    dye=(dy*ecum).astype(bf16)
    db=mm(dgtb,cc)+mm((x*etail).astype(bf16),dsb,1,1)
    dc=mm(dgtb,b,0,0)+mm(dye,s.astype(bf16),1,1)
    kk=jnp.sum(ds*sn_ref[...],axis=0,keepdims=True)
    kk=jnp.concatenate([kk,jnp.zeros((7,VW),f32)],axis=0)
    hs=head_sum(jnp.concatenate([dyb.astype(f32)*y_ref[...]-xb.astype(f32)*dx,v*dx,kk],axis=0),hh_ref[...])
    dcum,q,k0=hs[:Q],hs[Q:2*Q],hs[2*Q:2*Q+1]
    da=k0+tri_sum(jnp.where(up,1.0,0.0).astype(bf16),dcum)
    dst=(q-da*edl)*sig(z)
    ds_ref[...]=ecum[Q-1:Q,:]*ds+mm(cc,dye,0,0)
    sn_ref[...]=s
    acs_ref[0:1,:]+=jnp.sum(da*a,axis=0,keepdims=True)
    acs_ref[1:2,:]+=jnp.sum(dst,axis=0,keepdims=True)
    dv=dte*dx+sk_ref[...]*dy
    acc_ref[5:6,:VW]+=jnp.sum(dy*v,axis=0,keepdims=True)
    dpre=jnp.concatenate([dv,db,dc],axis=1)*(sg*(1.0+pre-act))
    ext[0:Q,:]=dpre
    ext[Q:Q+8,:]=h_ref[...]
    h_ref[...]=dpre[0:8,:]
    xr=raw_ref[:,:CW]
    draw=ck_ref[3:4,:]*dpre
    acc_ref[3:4,:]+=jnp.sum(dpre*xr,axis=0,keepdims=True)
    acc_ref[4:5,:]+=jnp.sum(dpre,axis=0,keepdims=True)
    for j in (1,2,3):
        sh=ext[j:j+Q,:]
        draw=draw+ck_ref[3-j:4-j,:]*sh
        acc_ref[3-j:4-j,:]+=jnp.sum(sh*xr,axis=0,keepdims=True)
    out_ref[:,:CW]=draw.astype(bf16)
    out_ref[:,CW:]=dst.astype(bf16)

def sd(shape,dt=f32): return jax.ShapeDtypeStruct(shape,dt)

def whole(shape): return pl.BlockSpec(shape,lambda i,*_: (0,)*len(shape))

def ssd_fwd(c0,nc,first,raw,ck,cb,sb,dl,ee,s_in,t_in):
    rb=lambda w: pl.BlockSpec((Q,w),lambda i,*_: (i,0))
    rin=pl.BlockSpec((Q,RW),lambda i,*_: (c0+i,0))
    return pl.pallas_call(partial(fwd_kernel,c0,nc),
        out_shape=(sd((nc*Q,VW)),sd((nc*Q,CW)),sd((nc,NS,VW)),sd((NS,VW)),sd((8,CW))),
        grid_spec=pltpu.PrefetchScalarGridSpec(num_scalar_prefetch=1,grid=(nc,),
            in_specs=[rin,whole((4,CW)),whole((1,CW)),whole((1,128)),whole((1,128)),whole((256,VW)),whole((NS,VW)),whole((8,CW))],
            out_specs=(rb(VW),rb(CW),pl.BlockSpec((1,NS,VW),lambda i,*_: (i,0,0)),whole((NS,VW)),whole((8,CW))),
            scratch_shapes=[pltpu.VMEM((Q+8,CW),f32)]),
        compiler_params=pltpu.CompilerParams(vmem_limit_bytes=40<<20),
        cost_estimate=pl.CostEstimate(flops=int(1.5e9*nc/8),bytes_accessed=16_000_000*nc//8,transcendentals=3_000_000*nc//8),
        name=f"ssd_forward_{c0}")(first,raw,ck,cb,sb,dl,ee,s_in,t_in)

def ssd_bwd(c0,nc,nall,first,raw,pre,y,dy,sp,ck,sb,dl,sk,ee,hh,ds,sn,hd,acc,acs,off=0):
    rv=lambda w,o=c0: pl.BlockSpec((Q,w),lambda i,*_: (o+nc-1-i,0))
    return pl.pallas_call(partial(bwd_kernel,c0,nc,nall),
        out_shape=(sd((nc*Q,RW),bf16),sd((NS,VW)),sd((NS,VW)),sd((8,CW)),sd((8,CW)),sd((8,128))),
        grid_spec=pltpu.PrefetchScalarGridSpec(num_scalar_prefetch=1,grid=(nc,),
            in_specs=[rv(RW),rv(CW,0),rv(VW,0),rv(VW),pl.BlockSpec((1,NS,VW),lambda i,*_: (nc-1-i,0,0)),
                      whole((4,CW)),whole((1,128)),whole((1,128)),whole((1,VW)),whole((256,VW)),whole((2*VW,128)),
                      whole((NS,VW)),whole((NS,VW)),whole((8,CW)),whole((8,CW)),whole((8,128))],
            out_specs=(rv(RW,0),whole((NS,VW)),whole((NS,VW)),whole((8,CW)),whole((8,CW)),whole((8,128))),
            scratch_shapes=[pltpu.VMEM((Q+8,CW),f32)]),
        compiler_params=pltpu.CompilerParams(vmem_limit_bytes=40<<20),
        cost_estimate=pl.CostEstimate(flops=int(3e9*nc/8),bytes_accessed=24_000_000*nc//8,transcendentals=4_000_000*nc//8),
        name=f"ssd_backward_{c0}")(first,raw,pre,y,dy,sp,ck,sb,dl,sk,ee,hh,ds,sn,hd,acc,acs)


D = 1536
H = 48
E = 3072
TOK_DEV = 1024
SEQ_DEV = 4
EPSILON = 1e-05
PARTS = 2


def contract(left, right, left_dim, right_dim, out=f32):
    return lax.dot_general(
        left, right, (((left_dim,), (right_dim,)), ((), ())), preferred_element_type=f32
    ).astype(out)


def span_layout(seq_lengths, seq_device, seq_offset, device):
    span_index = jnp.arange(SEQ_DEV, dtype=jnp.int32)
    needed = (seq_lengths + SPAN - 1) // SPAN
    owned_seq = (seq_device == device) & (seq_lengths > 0)
    relative = span_index[None, :] - seq_offset[:, None]
    inside = owned_seq[:, None] & (relative >= 0) & (relative < needed[:, None])
    live_rows = jnp.sum(
        jnp.where(inside, jnp.clip(seq_lengths[:, None] - relative * SPAN, 0, SPAN), 0), axis=0
    )
    seq_first = jnp.any(inside & (relative == 0), axis=0)
    return live_rows, seq_first.astype(jnp.int32)


def ring_order(count):
    if count == 8:
        return [0, 2, 4, 6, 7, 5, 3, 1]
    return list(range(count))


def place_kernel(cols, rows, off_ref, *refs):
    count = len(cols)
    out, sem = refs[count], refs[count + 1]
    copies = []
    for k, (c0, w) in enumerate(cols):
        at = pl.multiple_of(off_ref[k] * rows, 16)
        copies.append(
            pltpu.make_async_copy(refs[k], out.at[pl.ds(at, rows), pl.ds(c0, w)], sem.at[k])
        )
    for copy in copies:
        copy.start()
    for copy in copies:
        copy.wait()


def place(pieces, offsets, total):
    rows = pieces[0][0].shape[0]
    cols = [(c0, x.shape[1]) for x, c0 in pieces]
    width = max(c0 + w for c0, w in cols)
    any_spec = pl.BlockSpec(memory_space=pl.ANY)
    return pl.pallas_call(
        partial(place_kernel, cols, rows),
        out_shape=jax.ShapeDtypeStruct((total, width), pieces[0][0].dtype),
        grid_spec=pltpu.PrefetchScalarGridSpec(
            num_scalar_prefetch=1,
            grid=(1,),
            in_specs=[any_spec] * len(cols),
            out_specs=any_spec,
            scratch_shapes=[pltpu.SemaphoreType.DMA((len(cols),))],
        ),
        cost_estimate=pl.CostEstimate(flops=0, bytes_accessed=2 * total * width * 2, transcendentals=0),
        name="place_rows",
    )(offsets, *[x for x, _ in pieces])


class Ring:
    def __init__(self, count):
        self.count = count
        self.order = ring_order(count)
        at = {d: i for i, d in enumerate(self.order)}
        self.table = [[self.order[(at[d] + k) % count] for k in range(count)] for d in range(count)]
        self.ahead = [(self.order[i], self.order[(i + 1) % count]) for i in range(count)]
        self.back = [(b, a) for a, b in self.ahead]

    def places(self):
        return jnp.asarray(self.table, jnp.int32)[lax.axis_index("dp")]

    def gather(self, x):
        half = self.count // 2
        mid = x.shape[1] // 2 // 128 * 128
        pieces = [(x, 0, 0)]
        f = b = x
        for s in range(1, half + 1):
            if s == half:
                f, b = f[:, :mid], b[:, mid:]
            f = lax.ppermute(f, "dp", self.ahead)
            b = lax.ppermute(b, "dp", self.back)
            pieces += [(f, 0, self.count - s), (b, mid if s == half else 0, s)]
        return pieces

    def assemble(self, pieces, places):
        offsets = jnp.stack([places[k] for _, _, k in pieces])
        return place([(x, c0) for x, c0, _ in pieces], offsets, self.count * pieces[0][0].shape[0])

    def scatter_sum(self, x, places):
        half = self.count // 2
        mid = x.shape[2] // 2 // 128 * 128

        def block(k):
            return lax.dynamic_index_in_dim(x, places[k % self.count], 0, keepdims=False)

        far = block(half)
        f, b = far[:, :mid], far[:, mid:]
        for s in range(half - 1, -1, -1):
            f = lax.ppermute(f, "dp", self.ahead).astype(f32)
            b = lax.ppermute(b, "dp", self.back).astype(f32)
            own_f, own_b = block(s).astype(f32), block(self.count - s).astype(f32)
            if s == half - 1:
                f = jnp.pad(f, ((0, 0), (0, x.shape[2] - mid)))
                b = jnp.pad(b, ((0, 0), (mid, 0)))
            if s:
                f = (own_f + f).astype(bf16)
                b = (own_b + b).astype(bf16)
        return block(0).astype(f32) + f + b


def xor_swap(x, axis, count, bit):
    return lax.ppermute(x, axis, [(i, i ^ bit) for i in range(count)])


def bits_of(count):
    return [1 << k for k in range(count.bit_length() - 1)]


def sum_all(x, axis, count):
    for bit in bits_of(count):
        x = x + xor_swap(x, axis, count, bit)
    return x


def gather_tensor(x, count, me):
    pieces = {0: x}
    for bit in reversed(bits_of(count)):
        for k in list(pieces):
            pieces[k ^ bit] = xor_swap(pieces[k], "tensor", count, bit)
    keys = list(pieces)
    offsets = me ^ jnp.asarray(keys, jnp.int32)
    return place([(pieces[k], 0) for k in keys], offsets, count * x.shape[0])


def scatter_tensor(x, count, me, out=f32):
    left = count
    for bit in bits_of(count):
        mine = (me // bit) % 2
        x = x.reshape((left // 2, 2) + x.shape[-2:])
        send = lax.dynamic_index_in_dim(x, 1 - mine, 1, keepdims=False)
        keep = lax.dynamic_index_in_dim(x, mine, 1, keepdims=False)
        got = xor_swap(send, "tensor", count, bit)
        left //= 2
        x = keep.astype(f32) + got.astype(f32)
        if left > 1:
            x = x.astype(bf16)
    return x[0].astype(out)


def after(x, *others):
    return lax.optimization_barrier((x,) + others)[0]


def body(
    n_dp,
    n_tensor,
    hidden_in,
    norm_gain,
    gate_value_weight,
    state_proj_weight,
    step_weight,
    conv_value_kernel,
    conv_value_bias,
    conv_state_kernel,
    conv_state_bias,
    step_bias,
    decay_log,
    skip_scale,
    gate_norm_gain,
    out_weight,
    out_cotangent,
    seq_lengths,
    seq_device,
    seq_offset,
):
    quarter = hidden_in.shape[0]
    heads = step_weight.shape[1]
    rows = gate_value_weight.shape[0]
    pad_heads = lambda x: jnp.pad(x, (0, 128 - heads))[None]
    me = lax.axis_index("tensor")
    ring = Ring(n_dp)
    places = ring.places()

    live_rows, seq_first = span_layout(seq_lengths, seq_device, seq_offset, lax.axis_index("dp"))
    row = me * quarter + jnp.arange(quarter, dtype=jnp.int32)
    local_live = jnp.sum(
        jnp.where((row // SPAN)[:, None] == jnp.arange(SEQ_DEV)[None, :], live_rows[None, :], 0), axis=1
    )
    local_mask = (row % SPAN < local_live).astype(f32)

    first_own = jnp.concatenate(
        [gate_value_weight[:, 1, :], state_proj_weight, jnp.pad(step_weight, ((0, 0), (0, 128 - heads)))],
        axis=1,
    )
    first_pieces = ring.gather(first_own)
    inv_rms = lax.rsqrt(jnp.mean(hidden_in * hidden_in, axis=-1) + EPSILON)
    scaled = hidden_in * inv_rms[:, None]
    normed_local = (scaled * norm_gain[None, :]).astype(bf16)
    normed = gather_tensor(normed_local, n_tensor, me)
    gate_own = after(gate_value_weight[:, 0, :], first_pieces[-3][0], first_pieces[-4][0])
    gate_pieces = ring.gather(gate_own)
    out_own = after(out_weight, gate_pieces[-3][0], gate_pieces[-4][0])
    out_pieces = ring.gather(out_own)
    back_local = (local_mask[:, None] * out_cotangent).astype(bf16)
    back_mix = gather_tensor(after(back_local, normed), n_tensor, me)

    conv_kernel = jnp.concatenate([conv_value_kernel, conv_state_kernel], axis=0).T
    conv_bias = jnp.concatenate([conv_value_bias, conv_state_bias])[None]
    e1 = (jnp.arange(128)[:, None] == jnp.arange(VW)[None, :] // HW).astype(bf16)
    ee = jnp.concatenate([e1, e1], axis=0)
    hh = jnp.concatenate([e1.T, e1.T], axis=0)
    sb, dl = pad_heads(step_bias), pad_heads(decay_log)
    skip = jnp.repeat(skip_scale, HW)[None]
    zeros = lambda *s: jnp.zeros(s, f32)

    first_w = ring.assemble(first_pieces, places)
    raw = contract(normed, first_w, 1, 0)
    chunks = TOK_DEV // Q
    n = chunks // PARTS
    state, tail = zeros(NS, VW), zeros(8, CW)
    y_parts, pre_parts, state_parts = [], [], []
    for i in range(PARTS):
        y0, pre, sp, state, tail = ssd_fwd(
            i * n, n, seq_first, raw, conv_kernel, conv_bias, sb, dl, ee, state, tail
        )
        y_parts.append(y0)
        pre_parts.append(pre)
        state_parts.append(sp)
    y0 = jnp.concatenate(y_parts, axis=0)
    values = jax.nn.silu(jnp.concatenate([p[:, :VW] for p in pre_parts], axis=0))
    ssd = y0 + skip * values

    gate_w = ring.assemble(gate_pieces, places)
    gate_raw = contract(normed, gate_w, 1, 0)
    gate_sig = jax.nn.sigmoid(gate_raw)
    gate = gate_raw * gate_sig
    gated = ssd * gate
    square = jnp.sum(gated * gated, axis=-1)
    square = sum_all(square.reshape(8, 128), "tensor", n_tensor).reshape(TOK_DEV)
    gate_inv = lax.rsqrt(square / E + EPSILON)
    unit = gated * gate_inv[:, None]
    normed_y = (unit * gate_norm_gain[None, :]).astype(bf16)
    out_grad = contract(back_mix, normed_y, 0, 0, bf16)
    out_w = ring.assemble(out_pieces, places)
    out_out = ring.scatter_sum(out_grad.reshape(n_dp, rows, VW), places)

    back_y = contract(back_mix, out_w, 1, 0)
    gain_grad = jnp.sum(back_y * unit, axis=0)
    weighted = back_y * gate_norm_gain[None, :]
    cross = jnp.sum(weighted * unit, axis=-1)
    cross = sum_all(cross.reshape(8, 128), "tensor", n_tensor).reshape(TOK_DEV)
    back_gated = gate_inv[:, None] * (weighted - unit * (cross / E)[:, None])
    back_gate = (back_gated * ssd * (gate_sig * (1.0 + gate_raw - gate))).astype(bf16)
    back_ssd = back_gated * gate

    gate_grad = contract(normed, back_gate, 0, 0, bf16)
    gate_out = ring.scatter_sum(gate_grad.reshape(n_dp, rows, VW), places)
    mixer = contract(normed_y, out_w, 1, 1, bf16)
    mixer_rows = scatter_tensor(mixer.reshape(n_tensor, quarter, D), n_tensor, me)
    output = hidden_in + local_mask[:, None] * mixer_rows

    ds, sn, hd, acc, acs = zeros(NS, VW), zeros(NS, VW), zeros(8, CW), zeros(8, CW), zeros(8, 128)
    back_parts = []
    for i in reversed(range(PARTS)):
        out, ds, sn, hd, acc, acs = ssd_bwd(
            i * n, n, chunks, seq_first, raw, pre_parts[i], y_parts[i], back_ssd, state_parts[i],
            conv_kernel, sb, dl, skip, ee, hh, ds, sn, hd, acc, acs,
        )
        back_parts.insert(0, out)
    back_first = jnp.concatenate(back_parts, axis=0)

    value_grad = contract(normed, back_first[:, :VW], 0, 0, bf16)
    value_out = ring.scatter_sum(value_grad.reshape(n_dp, rows, VW), places)
    state_grad = contract(normed, back_first[:, VW:CW], 0, 0, bf16)
    step_grad = contract(back_first[:, CW:], normed, 0, 0, bf16)[:16]
    share = rows // n_tensor
    state_grad = state_grad.reshape(n_dp, n_tensor, share, 2 * NS).transpose(1, 0, 2, 3)
    state_grad = scatter_tensor(
        state_grad.reshape(n_tensor, n_dp * share, 2 * NS), n_tensor, me, bf16
    ).reshape(n_dp, share, 2 * NS)
    step_grad = step_grad.reshape(16, n_dp, rows).transpose(1, 0, 2)
    step_grad = jnp.pad(step_grad, ((0, 0), (0, 0), (0, 2 * NS - rows)))
    small_out = ring.scatter_sum(jnp.concatenate([state_grad, step_grad], axis=1), places)

    back_normed = contract(back_first, first_w, 1, 1) + contract(back_gate, gate_w, 1, 1)
    norm_grad = jnp.sum(back_normed * normed.astype(f32), axis=0) / norm_gain
    back_rows = scatter_tensor(
        back_normed.astype(bf16).reshape(n_tensor, quarter, D), n_tensor, me
    )
    back_scaled = back_rows * norm_gain[None, :]
    hidden_gradient = out_cotangent + inv_rms[:, None] * (
        back_scaled - scaled * jnp.mean(back_scaled * scaled, axis=-1)[:, None]
    )

    shared = jnp.concatenate([acc[:5, VW:], norm_grad.reshape(6, 256), zeros(5, 256)], axis=0)
    shared = sum_all(shared, "tensor", n_tensor)
    own = jnp.concatenate(
        [acc[:6], jnp.pad(jnp.concatenate([gain_grad, acs[0], acs[1]]), (0, 0))[None], zeros(1, CW)], axis=0
    )
    small = jnp.concatenate([own, shared.reshape(4, CW)], axis=0)
    small = sum_all(small, "dp", n_dp)
    shared = small[8:].reshape(16, 256)
    index = lax.axis_index("dp") * n_tensor + me
    all_count = n_dp * n_tensor
    kern_share = 2 * NS // all_count
    state_kernel_out = lax.dynamic_slice(shared, (0, index * kern_share), (5, kern_share))
    norm_out = lax.dynamic_slice(shared[5:11].reshape(D), (index * (D // all_count),), (D // all_count,))
    return (
        output,
        hidden_gradient,
        norm_out,
        jnp.stack([gate_out, value_out], axis=1),
        small_out[:share],
        small_out[share:, :rows].T[:, :heads],
        small[:4, :VW].T,
        small[4, :VW],
        state_kernel_out[:4].T,
        state_kernel_out[4],
        small[6, VW + 128 : VW + 128 + heads],
        small[6, VW : VW + heads],
        jnp.sum(small[5, :VW].reshape(heads, HW), axis=1),
        small[6, :VW],
        out_out,
    )


def solution(mesh):
    in_specs = (
        P(("dp", "tensor"), None),
        P(),
        P("dp", None, "tensor"),
        P("dp", None),
        P("dp", "tensor"),
        P("tensor", None),
        P("tensor"),
        P(),
        P(),
        P("tensor"),
        P("tensor"),
        P("tensor"),
        P("tensor"),
        P("dp", "tensor"),
        P(("dp", "tensor"), None),
        P(),
        P(),
        P(),
    )
    out_specs = (
        P(("dp", "tensor"), None),
        P(("dp", "tensor"), None),
        P(("dp", "tensor")),
        P("dp", None, "tensor"),
        P(("dp", "tensor"), None),
        P("dp", "tensor"),
        P("tensor", None),
        P("tensor"),
        P(("dp", "tensor"), None),
        P(("dp", "tensor")),
        P("tensor"),
        P("tensor"),
        P("tensor"),
        P("tensor"),
        P("dp", "tensor"),
    )
    return jax.shard_map(
        partial(body, mesh.shape["dp"], mesh.shape["tensor"]),
        mesh=mesh,
        in_specs=in_specs,
        out_specs=out_specs,
        check_vma=False,
    )
```

```python
from functools import partial

import jax, jax.numpy as jnp
from jax import lax
from jax.experimental import pallas as pl
from jax.experimental.pallas import tpu as pltpu
from jax.sharding import PartitionSpec as P
f32=jnp.float32; bf16=jnp.bfloat16
Q=128
NS=128
VW=768
HW=64
CW=1024
RW=1152
SPAN=256
LIMIT=14<<20
NEG=-1e30

def mm(a,b,ca=1,cb=0):
    return lax.dot_general(a,b,(((ca,),(cb,)),((),())),preferred_element_type=f32)

def split2(x):
    hi=x.astype(bf16); return hi,(x-hi.astype(f32)).astype(bf16)

def split3(x):
    hi=x.astype(bf16); r=x-hi.astype(f32); mid=r.astype(bf16); return hi,mid,(r-mid.astype(f32)).astype(bf16)

def mm3(a,b,ca=1,cb=0):
    ah,al=split2(a); bh,bl=split2(b)
    return mm(jnp.concatenate([ah,ah,al],axis=ca),jnp.concatenate([bh,bl,bh],axis=cb),ca,cb)

def tri_sum(tri,x):
    a,b,c=split3(x); w=x.shape[1]
    p=mm(tri,jnp.concatenate([a,b,c],axis=1))
    return p[:,:w]+p[:,w:2*w]+p[:,2*w:]

def spread(x,ee):
    a,b=split2(x)
    return mm(jnp.concatenate([a,b],axis=1),ee)

def head_sum(x,hh):
    a,b=split2(x)
    return mm(jnp.concatenate([a,b],axis=1),hh)

def iotas():
    return lax.broadcasted_iota(jnp.int32,(Q,Q),0),lax.broadcasted_iota(jnp.int32,(Q,Q),1)

def softplus(z):
    return jnp.maximum(z,0.0)+jnp.log(1.0+jnp.exp(-jnp.abs(z)))

def sig(z):
    return 1.0/(1.0+jnp.exp(-z))

def halves(x):
    lane=lax.broadcasted_iota(jnp.int32,x.shape,1)
    lo=jnp.where(lane<HW,x,0.0); hi=jnp.where(lane<HW,0.0,x)
    return jnp.concatenate([lo.astype(bf16),hi.astype(bf16)],axis=0)

def spread_matrix(shape):
    r=lax.broadcasted_iota(jnp.int32,shape,0)%128; c=lax.broadcasted_iota(jnp.int32,shape,1)//HW
    return jnp.where(r==c,1.0,0.0).astype(bf16)

def sum_matrix(shape):
    r=lax.broadcasted_iota(jnp.int32,shape,0)%VW//HW; c=lax.broadcasted_iota(jnp.int32,shape,1)
    return jnp.where(r==c,1.0,0.0).astype(bf16)

def halves2(x):
    lane=lax.broadcasted_iota(jnp.int32,x.shape,1)
    h,l=split2(jnp.concatenate([jnp.where(lane<HW,x,0.0),jnp.where(lane<HW,0.0,x)],axis=0))
    return h,l

def fwd_kernel(c0,nc,first_ref,raw_ref,par_ref,*rest):
    y_ref,pre_ref,sp_ref,s_ref,t_ref,ext,ee_ref=rest[-7:]
    ck_ref=par_ref
    i=pl.program_id(0)
    @pl.when(i==0)
    def _():
        ee_ref[...]=spread_matrix(ee_ref.shape)
        if c0:
            s_ref[...]=rest[0][...]; t_ref[...]=rest[1][...]
        else:
            s_ref[...]=jnp.zeros_like(s_ref); t_ref[...]=jnp.zeros_like(t_ref)
    c=c0+i
    start=(first_ref[c//(SPAN//Q)]==1)&(c%(SPAN//Q)==0)
    @pl.when(start)
    def _():
        s_ref[...]=jnp.zeros_like(s_ref); t_ref[...]=jnp.zeros_like(t_ref)
    ext[0:8,:]=t_ref[...]
    x=raw_ref[:,:CW]
    ext[8:8+Q,:]=x
    t_ref[...]=raw_ref[Q-8:Q,:CW]
    pre=par_ref[4:5,:]+ck_ref[3:4,:]*x
    for j in (1,2,3):
        pre=pre+ck_ref[3-j:4-j,:]*ext[8-j:8-j+Q,:]
    pre_ref[...]=pre
    act=pre*sig(pre)
    v=act[:,:VW]; b=act[:,VW:VW+NS].astype(bf16); cc=act[:,VW+NS:].astype(bf16)
    dt=softplus(raw_ref[:,CW:]+par_ref[5:6,:128])
    a=-dt*jnp.exp(par_ref[6:7,:128])
    row,col=iotas()
    low=row>=col
    tri=jnp.where(low,1.0,0.0).astype(bf16)
    cum=tri_sum(tri,a)
    cum_t=cum.T
    last=cum[Q-1:Q,:]
    ee=ee_ref[...]
    sprd=spread(jnp.concatenate([dt,jnp.exp(cum),jnp.exp(last-cum)],axis=0),ee)
    dte,ecum,etail=sprd[:Q],sprd[Q:2*Q],sprd[2*Q:]
    x=v*dte
    g=mm(cc,b,1,1)
    parts=[]
    for p in range(VW//128):
        ws=[]
        for h in (2*p,2*p+1):
            d=jnp.where(low,cum[:,h:h+1]-cum_t[h:h+1,:],NEG)
            ws.append((jnp.exp(d)*g).astype(bf16))
        parts.append(mm(jnp.concatenate(ws,axis=1),halves(x[:,128*p:128*p+128])))
    s=s_ref[...]
    sp_ref[0]=s
    y_ref[...]=jnp.concatenate(parts,axis=1)+ecum*mm(cc,s.astype(bf16))+par_ref[7:8,:VW]*v
    s_ref[...]=ecum[Q-1:Q,:]*s+mm(b,(x*etail).astype(bf16),0,0)

def bwd_kernel(c0,nc,nall,first_ref,raw_ref,pre_ref,y_ref,dy_ref,sp_ref,par_ref,*rest):
    out_ref,vs_ref,ds_ref,sn_ref,h_ref,acc_ref,acs_ref,ext,ee_ref,hh_ref=rest[-10:]
    ck_ref=par_ref
    i=pl.program_id(0)
    @pl.when(i==0)
    def _():
        ee_ref[...]=spread_matrix(ee_ref.shape)
        hh_ref[...]=sum_matrix(hh_ref.shape)
        for k,ref in enumerate((ds_ref,sn_ref,h_ref,acc_ref,acs_ref)):
            ref[...]=jnp.zeros_like(ref) if c0+nc==nall else rest[k][...]
    c=c0+nc-1-i
    nxt=jnp.minimum(c+1,nall-1)
    start=(first_ref[nxt//(SPAN//Q)]==1)&(nxt%(SPAN//Q)==0)
    @pl.when(start)
    def _():
        ds_ref[...]=jnp.zeros_like(ds_ref); h_ref[...]=jnp.zeros_like(h_ref)
    pre=pre_ref[...]
    sg=sig(pre)
    act=pre*sg
    v=act[:,:VW]; bf=act[:,VW:VW+NS]; cf=act[:,VW+NS:]
    b=bf.astype(bf16); cc=cf.astype(bf16)
    z=raw_ref[:,CW:]+par_ref[5:6,:128]
    dt=softplus(z)
    edl=jnp.exp(par_ref[6:7,:128])
    a=-dt*edl
    row,col=iotas()
    low=row>=col; up=row<=col
    cum=tri_sum(jnp.where(low,1.0,0.0).astype(bf16),a)
    cum_t=cum.T
    last=cum[Q-1:Q,:]
    ee=ee_ref[...]
    sprd=spread(jnp.concatenate([dt,jnp.exp(cum),jnp.exp(last-cum)],axis=0),ee)
    dte,ecum,etail=sprd[:Q],sprd[Q:2*Q],sprd[2*Q:]
    x=v*dte
    xb=x.astype(bf16)
    dy=dy_ref[...].astype(f32)
    dyb=dy.astype(bf16)
    gt=mm(b,cc,1,1)
    dgt=jnp.zeros((Q,Q),f32)
    parts=[]
    for p in range(VW//128):
        cols=slice(128*p,128*p+128)
        dyh,dyl=split2(dy[:,cols])
        xh,xl=halves2(x[:,cols])
        dw=mm(jnp.concatenate([xh,xl,xh],axis=1),jnp.concatenate([dyh,dyh,dyl],axis=1),1,1)
        ws=[]
        for k in (0,1):
            h=2*p+k
            lt=jnp.exp(jnp.where(up,cum_t[h:h+1,:]-cum[:,h:h+1],NEG))
            ws.append((lt*gt).astype(bf16))
            dgt=dgt+lt*dw[k*Q:(k+1)*Q]
        parts.append(mm(jnp.concatenate(ws,axis=1),halves(dy[:,cols])))
    ds=ds_ref[...]
    dsb=ds.astype(bf16)
    s=sp_ref[0]
    dxd=jnp.concatenate(parts,axis=1)
    bds=mm(b,dsb)
    dx=dxd+etail*bds
    xe=(x*etail).astype(bf16)
    dye=dy*ecum
    db=mm3(dgt,cf)+mm3(x*etail,ds,1,1)
    dc=mm3(dgt,bf,0,0)+mm3(dye,s,1,1)
    kk=jnp.sum(dsb.astype(f32)*sn_ref[...],axis=0,keepdims=True)
    kk=jnp.concatenate([kk,jnp.zeros((7,VW),f32)],axis=0)
    hs=head_sum(jnp.concatenate([dyb.astype(f32)*(y_ref[...]-par_ref[7:8,:VW]*v)-xb.astype(f32)*dxd-xe.astype(f32)*bds,v*dx,kk],axis=0),hh_ref[...])
    dcum,q,k0=hs[:Q],hs[Q:2*Q],hs[2*Q:2*Q+1]
    da=k0+tri_sum(jnp.where(up,1.0,0.0).astype(bf16),dcum)
    dst=(q-da*edl)*sig(z)
    ds_ref[...]=ecum[Q-1:Q,:]*ds+mm3(cf,dye,0,0)
    sn_ref[...]=s
    acs_ref[0:1,:]+=jnp.sum(da*a,axis=0,keepdims=True)
    acs_ref[1:2,:]+=jnp.sum(dst,axis=0,keepdims=True)
    dv=dte*dx+par_ref[7:8,:VW]*dy
    acc_ref[5:6,:VW]+=jnp.sum(dy*v,axis=0,keepdims=True)
    dpre=jnp.concatenate([dv,db,dc],axis=1)*(sg*(1.0+pre-act))
    ext[0:Q,:]=dpre
    ext[Q:Q+8,:]=h_ref[...]
    h_ref[...]=dpre[0:8,:]
    xr=raw_ref[:,:CW]
    draw=ck_ref[3:4,:]*dpre
    acc_ref[3:4,:]+=jnp.sum(dpre*xr,axis=0,keepdims=True)
    acc_ref[4:5,:]+=jnp.sum(dpre,axis=0,keepdims=True)
    for j in (1,2,3):
        sh=ext[j:j+Q,:]
        draw=draw+ck_ref[3-j:4-j,:]*sh
        acc_ref[3-j:4-j,:]+=jnp.sum(sh*xr,axis=0,keepdims=True)
    drawb,dstb=draw.astype(bf16),dst.astype(bf16)
    out_ref[:,:CW]=drawb
    out_ref[:,CW:]=dstb
    vs_ref[:,:VW]=drawb[:,:VW]
    vs_ref[:,VW:]=dstb

def sd(shape,dt=f32): return jax.ShapeDtypeStruct(shape,dt)

def whole(shape): return pl.BlockSpec(shape,lambda i,*_: (0,)*len(shape))

def once(shape): return pl.BlockSpec(shape,lambda i,*_: (0,)*len(shape),pipeline_mode=pl.Buffered(1))

def ssd_fwd(c0,nc,nall,first,raw,par,carry):
    rb=lambda w: pl.BlockSpec((Q,w),lambda i,*_: (c0+i,0))
    any_spec=pl.BlockSpec(memory_space=pl.ANY)
    held=[whole((NS,VW)),whole((8,CW))]
    return pl.pallas_call(partial(fwd_kernel,c0,nc),
        out_shape=(sd((nall*Q,VW)),sd((nall*Q,CW)),sd((nall,NS,VW)),sd((NS,VW)),sd((8,CW))),
        grid_spec=pltpu.PrefetchScalarGridSpec(num_scalar_prefetch=1,grid=(nc,),
            in_specs=[rb(RW),once((8,CW))]+(held+[any_spec]*3 if carry else []),
            out_specs=(rb(VW),rb(CW),pl.BlockSpec((1,NS,VW),lambda i,*_: (c0+i,0,0)),*held),
            scratch_shapes=[pltpu.VMEM((Q+8,CW),f32),pltpu.VMEM((256,VW),bf16)]),
        input_output_aliases={5+k:k for k in range(3)} if carry else {},
        compiler_params=pltpu.CompilerParams(vmem_limit_bytes=LIMIT),
        cost_estimate=pl.CostEstimate(flops=int(1.5e9*nc/8),bytes_accessed=30_000_000*nc//8,transcendentals=3_000_000*nc//8),
        name=f"ssd_forward_{c0}")(first,raw,par,*(carry[3:]+carry[:3] if carry else ()))

def ssd_bwd(c0,nc,nall,first,raw,pre,y,dy,sp,par,carry):
    rv=lambda w: pl.BlockSpec((Q,w),lambda i,*_: (c0+nc-1-i,0))
    any_spec=pl.BlockSpec(memory_space=pl.ANY)
    held=[whole((NS,VW)),whole((NS,VW)),whole((8,CW)),whole((8,CW)),whole((8,128))]
    return pl.pallas_call(partial(bwd_kernel,c0,nc,nall),
        out_shape=(sd((nall*Q,RW),bf16),sd((nall*Q,VW+128),bf16),sd((NS,VW)),sd((NS,VW)),sd((8,CW)),sd((8,CW)),sd((8,128))),
        grid_spec=pltpu.PrefetchScalarGridSpec(num_scalar_prefetch=1,grid=(nc,),
            in_specs=[rv(RW),rv(CW),rv(VW),rv(VW),pl.BlockSpec((1,NS,VW),lambda i,*_: (c0+nc-1-i,0,0)),once((8,CW))]
                     +(held+[any_spec]*2 if carry else []),
            out_specs=(rv(RW),rv(VW+128),*held),
            scratch_shapes=[pltpu.VMEM((Q+8,CW),f32),pltpu.VMEM((256,VW),bf16),pltpu.VMEM((2*VW,128),bf16)]),
        input_output_aliases={12+k:k for k in range(2)} if carry else {},
        compiler_params=pltpu.CompilerParams(vmem_limit_bytes=LIMIT),
        cost_estimate=pl.CostEstimate(flops=int(3e9*nc/8),bytes_accessed=60_000_000*nc//8,transcendentals=4_000_000*nc//8),
        name=f"ssd_backward_{c0}")(first,raw,pre,y,dy,sp,par,*(carry[2:]+carry[:2] if carry else ()))


D = 1536
H = 48
E = 3072
TOK_DEV = 1024
SEQ_DEV = 4
EPSILON = 1e-05
FWD_PARTS = 2
BACK_PARTS = 2


def contract(left, right, left_dim, right_dim, out=f32):
    return lax.dot_general(
        left, right, (((left_dim,), (right_dim,)), ((), ())), preferred_element_type=f32
    ).astype(out)


def span_layout(seq_lengths, seq_device, seq_offset, device):
    span_index = jnp.arange(SEQ_DEV, dtype=jnp.int32)
    needed = (seq_lengths + SPAN - 1) // SPAN
    owned_seq = (seq_device == device) & (seq_lengths > 0)
    relative = span_index[None, :] - seq_offset[:, None]
    inside = owned_seq[:, None] & (relative >= 0) & (relative < needed[:, None])
    live_rows = jnp.sum(
        jnp.where(inside, jnp.clip(seq_lengths[:, None] - relative * SPAN, 0, SPAN), 0), axis=0
    )
    seq_first = jnp.any(inside & (relative == 0), axis=0)
    return live_rows, seq_first.astype(jnp.int32)


def ring_order(count):
    if count == 8:
        return [0, 2, 4, 6, 7, 5, 3, 1]
    return list(range(count))


def lay(cols, rows, off_ref, refs, out):
    for k, (c0, w) in enumerate(cols):
        out[pl.ds(pl.multiple_of(off_ref[k] * rows, 16), rows), c0 : c0 + w] = refs[k][...]


def row_sums(x):
    a, b = split2(x)
    ones = jnp.ones((8, x.shape[1]), bf16)
    return mm(ones, a, 1, 1) + mm(ones, b, 1, 1)


def project_kernel(cols, rows, nx, off_ref, *refs):
    n = len(cols)
    xs = refs[n : n + nx]
    w_ref, x_ref, xt_ref, raw_ref, gate_ref = refs[n + nx :]
    i = pl.program_id(0)

    @pl.when(i == 0)
    def _():
        lay(cols, rows, off_ref, refs, w_ref)

    for k in range(nx):

        @pl.when(i == k)
        def _(k=k):
            x_ref[...] = xs[k][...]

    xt_ref[...] = x_ref[...].T
    r = mm(x_ref[...], w_ref[...])
    raw_ref[...] = r[:, :RW]
    gate_ref[...] = r[:, RW:]


def project(pieces, offsets, xs, total):
    rows, n = pieces[0][0].shape[0], len(pieces)
    cols = [(c0, x.shape[1]) for x, c0 in pieces]
    width = max(c0 + w for c0, w in cols)
    q, depth = xs[0].shape
    nx = len(xs)
    at = lambda w: pl.BlockSpec((q, w), lambda i, off: (off[n + i], 0))
    return pl.pallas_call(
        partial(project_kernel, cols, rows, nx),
        out_shape=(sd((total, width), bf16), sd((q * nx, depth), bf16), sd((depth, q * nx), bf16), sd((q * nx, RW)), sd((q * nx, width - RW))),
        grid_spec=pltpu.PrefetchScalarGridSpec(
            num_scalar_prefetch=1,
            grid=(nx,),
            in_specs=[once(x.shape) for x, _ in pieces] + [once(x.shape) for x in xs],
            out_specs=(whole((total, width)), at(depth), pl.BlockSpec((depth, q), lambda i, off: (0, off[n + i])), at(RW), at(width - RW)),
        ),
        compiler_params=pltpu.CompilerParams(vmem_limit_bytes=30 << 20),
        cost_estimate=pl.CostEstimate(flops=2 * q * nx * total * width, bytes_accessed=30_000_000, transcendentals=0),
        name="project",
    )(offsets, *[x for x, _ in pieces], *xs)


def cotangent_kernel(cols, rows, nx, off_ref, *refs):
    n = len(cols)
    xs = refs[n : n + nx]
    ssd_ref, gr_ref, gain_ref, w_ref, x_ref, by_ref, sum_ref, yr_ref = refs[n + nx :]
    i = pl.program_id(0)

    @pl.when(i == 0)
    def _():
        lay(cols, rows, off_ref, refs, w_ref)

    for k in range(nx):

        @pl.when(i == k)
        def _(k=k):
            x_ref[...] = xs[k][...]

    by = mm(x_ref[...], w_ref[...])
    by_ref[...] = by
    gr = gr_ref[...]
    gated = ssd_ref[...] * (gr * sig(gr))
    yr_ref[...] = (gated * gain_ref[...]).astype(bf16)
    square = row_sums(gated * gated)
    cross = row_sums(by * gain_ref[...] * gated)
    top = lax.broadcasted_iota(jnp.int32, square.shape, 0) == 0
    sum_ref[0] = jnp.where(top, square, cross)


def cotangent(pieces, offsets, xs, ssd, gate_raw, gain, total):
    rows, n = pieces[0][0].shape[0], len(pieces)
    cols = [(c0, x.shape[1]) for x, c0 in pieces]
    width = max(c0 + w for c0, w in cols)
    q, depth = xs[0].shape
    nx = len(xs)
    at = lambda w: pl.BlockSpec((q, w), lambda i, off: (off[n + i], 0))
    return pl.pallas_call(
        partial(cotangent_kernel, cols, rows, nx),
        out_shape=(sd((total, width), bf16), sd((q * nx, depth), bf16), sd((q * nx, width)), sd((nx, 8, q)), sd((q * nx, width), bf16)),
        grid_spec=pltpu.PrefetchScalarGridSpec(
            num_scalar_prefetch=1,
            grid=(nx,),
            in_specs=[once(x.shape) for x, _ in pieces]
            + [once(x.shape) for x in xs]
            + [at(width), at(width), once((1, width))],
            out_specs=(
                whole((total, width)),
                at(depth),
                at(width),
                pl.BlockSpec((1, 8, q), lambda i, off: (off[n + i], 0, 0)),
                at(width),
            ),
        ),
        compiler_params=pltpu.CompilerParams(vmem_limit_bytes=22 << 20),
        cost_estimate=pl.CostEstimate(flops=2 * q * nx * total * width, bytes_accessed=24_000_000, transcendentals=800_000),
        name="cotangent",
    )(offsets, *[x for x, _ in pieces], *xs, ssd, gate_raw, gain)


def gate_kernel(sum_ref, by_ref, gr_ref, ssd_ref, gain_ref, ny_ref, bg_ref, dy_ref, gg_ref):
    @pl.when(pl.program_id(0) == 0)
    def _():
        gg_ref[...] = jnp.zeros_like(gg_ref)

    sums = sum_ref[0].T
    inv = lax.rsqrt(sums[:, 0:1] / E + EPSILON)
    gr, ssd, by, gain = gr_ref[...], ssd_ref[...], by_ref[...], gain_ref[...]
    sg = sig(gr)
    gate = gr * sg
    unit = ssd * gate * inv
    ny_ref[...] = (unit * gain).astype(bf16)
    gg_ref[0:1, :] += jnp.sum(by * unit, axis=0, keepdims=True)
    back = inv * (by * gain - unit * (inv * sums[:, 1:2] / E))
    bg_ref[...] = (back * ssd * (sg * (1.0 + gr - gate))).astype(bf16)
    dy_ref[...] = back * gate


def gate_back(sums, by, gate_raw, ssd, gain):
    t, width = by.shape
    n, _, q = sums.shape
    rb = pl.BlockSpec((q, width), lambda i: (i, 0))
    return pl.pallas_call(
        gate_kernel,
        out_shape=(sd((t, width), bf16), sd((t, width), bf16), sd((t, width)), sd((8, width))),
        grid=(n,),
        in_specs=[pl.BlockSpec((1, 8, q), lambda i: (i, 0, 0)), rb, rb, rb, once((1, width))],
        out_specs=(rb, rb, rb, whole((8, width))),
        compiler_params=pltpu.CompilerParams(vmem_limit_bytes=12 << 20),
        cost_estimate=pl.CostEstimate(flops=20_000_000, bytes_accessed=15_000_000, transcendentals=800_000),
        name="gate_back",
    )(sums, by, gate_raw, ssd, gain)


def normed_kernel(at_ref, first_ref, gate_ref, w_ref, x_ref, ng_in, out_ref, ng_ref):
    @pl.when(pl.program_id(0) == 0)
    def _():
        ng_ref[...] = ng_in[...]

    back = mm(first_ref[...], w_ref[:, :RW], 1, 1) + mm(gate_ref[...], w_ref[:, RW:], 1, 1)
    out_ref[0] = back.astype(bf16)
    ng_ref[0:1, :] += jnp.sum(back * x_ref[...].astype(f32), axis=0, keepdims=True)


def back_normed_rows(at, q, first, gate, w, normed, ng):
    depth = normed.shape[1]
    n = at.shape[0]
    rb = lambda c: pl.BlockSpec((q, c), lambda i, at: (at[i], 0))
    return pl.pallas_call(
        normed_kernel,
        out_shape=(sd((n, q, depth), bf16), sd((8, depth))),
        grid_spec=pltpu.PrefetchScalarGridSpec(
            num_scalar_prefetch=1,
            grid=(n,),
            in_specs=[rb(RW), rb(VW), once(w.shape), rb(depth), once((8, depth))],
            out_specs=(pl.BlockSpec((1, q, depth), lambda i, at: (i, 0, 0)), whole((8, depth))),
        ),
        compiler_params=pltpu.CompilerParams(vmem_limit_bytes=16 << 20),
        cost_estimate=pl.CostEstimate(flops=2 * n * q * depth * (RW + VW), bytes_accessed=16_000_000, transcendentals=0),
        name="back_normed",
    )(at, first, gate, w, normed, ng)


def mixer_kernel(at_ref, x_ref, w_ref, out_ref):
    out_ref[0] = mm(x_ref[...], w_ref[...], 1, 1).astype(bf16)


def mixer_blocks(at, q, x, w):
    n, (depth, width) = at.shape[0], w.shape
    return pl.pallas_call(
        mixer_kernel,
        out_shape=sd((n, q, depth), bf16),
        grid_spec=pltpu.PrefetchScalarGridSpec(
            num_scalar_prefetch=1,
            grid=(n,),
            in_specs=[pl.BlockSpec((q, width), lambda i, at: (at[i], 0)), once(w.shape)],
            out_specs=pl.BlockSpec((1, q, depth), lambda i, at: (i, 0, 0)),
        ),
        compiler_params=pltpu.CompilerParams(vmem_limit_bytes=10 << 20),
        cost_estimate=pl.CostEstimate(flops=2 * n * q * depth * width, bytes_accessed=7_000_000, transcendentals=0),
        name="mixer_rows",
    )(at, x, w)


def grad_kernel(per, rows, at_ref, xt_ref, back_ref, out_ref):
    i = pl.program_id(0)
    r = mm(xt_ref[...], back_ref[...]).astype(bf16)
    for d in range(per):
        out_ref[pl.ds(at_ref[i * per + d], 1)] = r[d * rows : (d + 1) * rows][None]


def weight_grad(at, xt, back, n_dp):
    depth, t = xt.shape
    rows, width = depth // n_dp, back.shape[1]
    steps = 2
    return pl.pallas_call(
        partial(grad_kernel, n_dp // steps, rows),
        out_shape=sd((n_dp, rows, width), bf16),
        grid_spec=pltpu.PrefetchScalarGridSpec(
            num_scalar_prefetch=1,
            grid=(steps,),
            in_specs=[pl.BlockSpec((depth // steps, t), lambda i, at: (i, 0)), once(back.shape)],
            out_specs=whole((n_dp, rows, width)),
        ),
        compiler_params=pltpu.CompilerParams(vmem_limit_bytes=16 << 20),
        cost_estimate=pl.CostEstimate(flops=2 * depth * t * width, bytes_accessed=8_000_000, transcendentals=0),
        name="weight_grad",
    )(at, xt, back)


def state_grad_kernel(n_tensor, per, rows, at_ref, xt_ref, back_ref, out_ref):
    i = pl.program_id(0)
    share = rows // n_tensor
    r = mm(xt_ref[...], back_ref[...]).astype(bf16)
    for d in range(per):
        for t in range(n_tensor):
            k = d * n_tensor + t
            out_ref[pl.ds(at_ref[i * per * n_tensor + k], 1)] = r[k * share : (k + 1) * share][None]


def state_weight_grad(at, xt, back, n_dp, n_tensor):
    depth, t = xt.shape
    rows = depth // n_dp
    share, width, steps = rows // n_tensor, 2 * NS, 2
    return pl.pallas_call(
        partial(state_grad_kernel, n_tensor, n_dp // steps, rows),
        out_shape=sd((n_tensor * n_dp, share, width), bf16),
        grid_spec=pltpu.PrefetchScalarGridSpec(
            num_scalar_prefetch=1,
            grid=(steps,),
            in_specs=[pl.BlockSpec((depth // steps, t), lambda i, at: (i, 0)), pl.BlockSpec((t, width), lambda i, at: (0, VW // width))],
            out_specs=whole((n_tensor * n_dp, share, width)),
        ),
        compiler_params=pltpu.CompilerParams(vmem_limit_bytes=10 << 20),
        cost_estimate=pl.CostEstimate(flops=2 * depth * t * width, bytes_accessed=5_000_000, transcendentals=0),
        name="state_weight_grad",
    )(at, xt, back)


class Ring:
    def __init__(self, count):
        self.count = count
        self.half = count // 2
        self.order = ring_order(count)
        at = {d: i for i, d in enumerate(self.order)}
        self.table = [[self.order[(at[d] + k) % count] for k in range(count)] for d in range(count)]
        self.ahead = [(self.order[i], self.order[(i + 1) % count]) for i in range(count)]
        self.back = [(b, a) for a, b in self.ahead]

    def rows_of(self, table):
        return jnp.asarray(table, jnp.int32)[lax.axis_index("dp")]

    def hop(self, f, b):
        return lax.ppermute(f, "dp", self.ahead), lax.ppermute(b, "dp", self.back)


class Gather:
    def __init__(self, ring, x):
        self.ring, self.mid = ring, x.shape[1] // 2 // 128 * 128
        self.pieces, self.f, self.b, self.s = [(x, 0)], x, x, 0

    def ready(self):
        if self.s == self.ring.half - 1:
            return [self.f[:, : self.mid], self.b[:, self.mid :]]
        return [self.f, self.b]

    def step(self, f, b):
        self.s += 1
        self.f, self.b = self.ring.hop(f, b)
        self.pieces += [(self.f, 0), (self.b, self.mid if self.s == self.ring.half else 0)]

    @staticmethod
    def offsets(ring):
        ahead = [0]
        for s in range(1, ring.half + 1):
            ahead += [ring.count - s, s]
        return [[ring.table[d][k] for k in ahead] for d in range(ring.count)]


class Scatter:
    def __init__(self, ring, x):
        self.ring, self.x, self.mid, self.s = ring, x, x.shape[2] // 2 // 128 * 128, ring.half

    def ready(self):
        x, s, mid = self.x, self.s, self.mid
        if s == self.ring.half:
            return [x[s, :, :mid], x[s, :, mid:]]
        f, b = self.f, self.b
        if s == self.ring.half - 1:
            f = jnp.pad(f, ((0, 0), (0, x.shape[2] - mid)))
            b = jnp.pad(b, ((0, 0), (mid, 0)))
        f = x[s].astype(f32) + f.astype(f32)
        b = x[self.ring.count - s].astype(f32) + b.astype(f32)
        return [f.astype(bf16), b.astype(bf16)]

    def step(self, f, b):
        self.f, self.b = self.ring.hop(f, b)
        self.s -= 1

    def total(self):
        return self.x[0].astype(f32) + self.f.astype(f32) + self.b.astype(f32)


def swap(x, axis, count, bits):
    return lax.ppermute(x, axis, [(i, i ^ bits) for i in range(count)])


def tensor_order(count):
    keys = [0]
    bit = count // 2
    while bit:
        keys += [k ^ bit for k in keys]
        bit //= 2
    return keys


def pick(x, index, axis=0):
    return lax.dynamic_index_in_dim(x, index, axis, keepdims=False)


def groups_of(count):
    bits = [1 << k for k in range(count.bit_length() - 1)]
    first = len(bits) % 2
    return ([bits[:first]] if first else []) + [bits[k : k + 2] for k in range(first, len(bits), 2)]


def others(bits):
    return [bits[0]] if len(bits) == 1 else [bits[0], bits[1], bits[0] | bits[1]]


class Spread:
    def __init__(self, x, axis, count):
        self.x, self.axis, self.count, self.groups = x, axis, count, groups_of(count)

    def step(self, x):
        bits = self.groups.pop(0)
        self.x = sum((swap(x, self.axis, self.count, k) for k in others(bits)), x)


class Share:
    def __init__(self, x, axis, count):
        self.x, self.axis, self.count, self.groups = x, axis, count, groups_of(count)

    def ready(self):
        bits = self.groups[0]
        n = 2 ** len(bits)
        self.parts = self.x.reshape((self.x.shape[0] // n, n) + self.x.shape[1:])
        return [self.parts[:, k // bits[0]].astype(bf16) for k in others(bits)]

    def step(self, sends):
        bits = self.groups.pop(0)
        got = [swap(x, self.axis, self.count, k) for x, k in zip(sends, others(bits))]
        self.x = sum((g.astype(f32) for g in got), self.parts[:, 0].astype(f32))


def together(*lists):
    flat = lax.optimization_barrier(tuple(x for xs in lists for x in xs))
    out, at = [], 0
    for xs in lists:
        out.append(list(flat[at : at + len(xs)]))
        at += len(xs)
    return out


def body(
    n_dp,
    n_tensor,
    hidden_in,
    norm_gain,
    gate_value_weight,
    state_proj_weight,
    step_weight,
    conv_value_kernel,
    conv_value_bias,
    conv_state_kernel,
    conv_state_bias,
    step_bias,
    decay_log,
    skip_scale,
    gate_norm_gain,
    out_weight,
    out_cotangent,
    seq_lengths,
    seq_device,
    seq_offset,
):
    quarter = hidden_in.shape[0]
    heads = step_weight.shape[1]
    rows = gate_value_weight.shape[0]
    me, dp = lax.axis_index("tensor"), lax.axis_index("dp")
    ring = Ring(n_dp)
    ring_at = ring.rows_of([[ring.table[d].index(k) for k in range(n_dp)] for d in range(n_dp)])
    order = me ^ jnp.asarray([3, 1, 2, 0], jnp.int32)
    ids = jnp.arange(n_dp * n_tensor, dtype=jnp.int32)
    state_at = (ids % n_tensor ^ me) * n_dp + (ids // n_tensor ^ dp)
    offsets = jnp.concatenate([ring.rows_of(Gather.offsets(ring)), me ^ jnp.asarray(tensor_order(n_tensor), jnp.int32)])
    to_core = lambda x: swap(x, "tensor", n_tensor, 1)
    to_far = lambda x: swap(x, "tensor", n_tensor, 2)

    live_rows, seq_first = span_layout(seq_lengths, seq_device, seq_offset, dp)
    row = me * quarter + jnp.arange(quarter, dtype=jnp.int32)
    local_live = jnp.sum(
        jnp.where((row // SPAN)[:, None] == jnp.arange(SEQ_DEV)[None, :], live_rows[None, :], 0), axis=1
    )
    local_mask = (row % SPAN < local_live).astype(f32)

    pad_to = lambda x, w: jnp.pad(x, (0, w - x.shape[0]))[None]
    params = jnp.concatenate(
        [
            jnp.concatenate([conv_value_kernel, conv_state_kernel], axis=0).T,
            jnp.concatenate([conv_value_bias, conv_state_bias])[None],
            pad_to(step_bias, CW),
            pad_to(decay_log, CW),
            pad_to(jnp.repeat(skip_scale, HW), CW),
        ],
        axis=0,
    )
    gain = gate_norm_gain[None]
    zeros = lambda *s: jnp.zeros(s, f32)

    first_own = jnp.concatenate(
        [
            gate_value_weight[:, 1, :],
            state_proj_weight,
            jnp.pad(step_weight, ((0, 0), (0, 128 - heads))),
            gate_value_weight[:, 0, :],
        ],
        axis=1,
    )
    inv_rms = lax.rsqrt(jnp.mean(hidden_in * hidden_in, axis=-1) + EPSILON)
    scaled = hidden_in * inv_rms[:, None]
    normed_local = (scaled * norm_gain[None, :]).astype(bf16)
    back_local = (local_mask[:, None] * out_cotangent).astype(bf16)
    (first_own, offsets, ring_at, order, state_at, seq_first, params) = lax.optimization_barrier(
        (first_own, offsets, ring_at, order, state_at, seq_first, params)
    )
    first = Gather(ring, first_own)
    out = Gather(ring, out_weight)
    normed_local, = lax.optimization_barrier((normed_local,))
    first.step(*first.ready())
    normed_parts = [normed_local, to_far(normed_local)]
    for s in range(1, ring.half):
        sends = [first.ready()]
        if s == 1:
            sends.append(normed_parts)
        if s == min(2, ring.half - 1):
            sends.append([back_local] + normed_parts[2:])
        if s == ring.half - 1:
            sends += [out.ready(), back_parts]
        sends = together(*sends)
        first.step(*sends.pop(0))
        if s == 1:
            [a, b] = sends.pop(0)
            normed_parts = [a, b, to_core(a), to_core(b)]
        if s == min(2, ring.half - 1):
            [a, *normed_parts[2:]] = sends.pop(0)
            back_parts = [a, to_far(a)]
        if s == ring.half - 1:
            out.step(*sends.pop(0))
            [a, b] = sends.pop(0)
            back_parts = [a, b, to_core(a), to_core(b)]
    xs, os = together([x for x, _ in first.pieces] + normed_parts, out.ready())
    out.step(*os)
    n = len(first.pieces)
    first_w, normed, normed_t, raw, gate_raw = project(
        [(x, c0) for x, (_, c0) in zip(xs[:n], first.pieces)], offsets, xs[n:], D
    )
    chunks = TOK_DEV // Q
    n = chunks // FWD_PARTS
    carry = ()
    for i in range(FWD_PARTS):
        if out.s < ring.half:
            gated_by = [carry[3]] if carry else [raw]
            gated_by, os = together(gated_by, out.ready())
            out.step(*os)
            if carry:
                carry = carry[:3] + (gated_by[0],) + carry[4:]
            else:
                raw = gated_by[0]
        carry = tuple(ssd_fwd(i * n, n, chunks, seq_first, raw, params, carry))
    while out.s < ring.half:
        out.step(*out.ready())
    ssd, pre, states = carry[:3]

    out_w, back_mix, back_y, sums, gated = cotangent(out.pieces, offsets, back_parts, ssd, gate_raw, gain, D)
    total = Spread(sums, "tensor", n_tensor)
    while total.groups:
        total.step(total.x)
    sums = total.x
    mixer = mixer_blocks(order, quarter, gated, out_w)
    sums, mixer = lax.optimization_barrier((sums, mixer))
    normed_y, back_gate, back_ssd, gain_grad = gate_back(sums, back_y, gate_raw, ssd, gain)
    gate_sum = Scatter(ring, weight_grad(ring_at, normed_t, back_gate, n_dp))

    half_rows = quarter // 2
    gs, ms = together(gate_sum.ready(), [mixer[:2]])
    gate_sum.step(*gs)
    got = to_core(ms[0])
    out_grad = contract(back_mix, normed_y, 0, 0, bf16)
    out_out = lax.psum_scatter(out_grad, "dp", scatter_dimension=0, tiled=True).astype(f32)
    n = chunks // BACK_PARTS
    away = (mixer[2].astype(f32) + got[0].astype(f32)).astype(bf16)
    away = [away[:half_rows], away[half_rows:]]
    carry, mixer_parts = (), []
    for k, i in enumerate(reversed(range(BACK_PARTS))):
        held = [carry[2]] if carry else [back_ssd]
        held, gs, ms, mixer_parts = together(held, gate_sum.ready(), [away[k]], mixer_parts)
        if carry:
            carry = carry[:2] + (held[0],) + carry[3:]
        else:
            back_ssd = held[0]
        gate_sum.step(*gs)
        mixer_parts.append(to_far(ms[0]))
        carry = tuple(ssd_bwd(i * n, n, chunks, seq_first, raw, pre, ssd, back_ssd, states, params, carry))
    back_first, back_vs, _, _, _, acc, acs = carry
    square = pick(sums, me)[0]
    local_inv = lax.rsqrt(square / E + EPSILON)

    value_sum = Scatter(ring, weight_grad(ring_at, normed_t, back_vs, n_dp))
    gs, vs, mixer_parts, [back_first] = together(gate_sum.ready(), value_sum.ready(), mixer_parts, [back_first])
    value_sum.step(*vs)
    gate_sum.step(*gs)
    state_sum = Share(
        state_weight_grad(state_at, normed_t, back_first, n_dp, n_tensor).reshape(n_tensor, n_dp, rows // n_tensor, 2 * NS),
        "tensor",
        n_tensor,
    )
    away, ng = back_normed_rows(order[:2], quarter, back_first, back_gate, first_w, normed, zeros(8, D))
    vs, gs, cs, ss, [back_first] = together(
        value_sum.ready(), [gate_sum.f, gate_sum.b], [away], state_sum.ready(), [back_first]
    )
    value_sum.step(*vs)
    gate_sum.f, gate_sum.b = gs
    near = to_core(cs[0])
    state_sum.step(ss)
    keep, ng = back_normed_rows(order[2:], quarter, back_first, back_gate, first_w, normed, ng)
    while gate_sum.s:
        gate_sum.step(*gate_sum.ready())
    gate_out = gate_sum.total()
    output = hidden_in + (local_mask * local_inv)[:, None] * (
        mixer[3].astype(f32) + got[1].astype(f32) + jnp.concatenate(mixer_parts, axis=0).astype(f32)
    )
    away = (keep[0].astype(f32) + near[0].astype(f32)).astype(bf16)
    state_sum = Share(state_sum.x[0], "dp", n_dp)
    shared = jnp.concatenate([acc[:5, VW:], (ng[0] / norm_gain).reshape(6, 256), zeros(5, 256)], axis=0)
    shared = Spread(shared, "tensor", n_tensor)
    vs, cs, ss, ps = together(value_sum.ready(), [away[:half_rows], away[half_rows:]], state_sum.ready(), [shared.x])
    value_sum.step(*vs)
    got = [to_far(cs[0])]
    state_sum.step(ss)
    shared.step(ps[0])
    own = jnp.concatenate(
        [acc[:6], jnp.concatenate([gain_grad[0], acs[0], acs[1]])[None], zeros(1, CW)], axis=0
    )
    while shared.groups:
        shared.step(shared.x)
    small = Spread(jnp.concatenate([own, shared.x.reshape(4, CW)], axis=0), "dp", n_dp)
    vs, cs, ss, ps = together(value_sum.ready(), [got[0], cs[1]], state_sum.ready(), [small.x])
    value_sum.step(*vs)
    got = [cs[0], to_far(cs[1])]
    state_sum.step(ss)
    small.step(ps[0])
    if value_sum.s:
        while value_sum.s:
            value_sum.step(*value_sum.ready())
        while state_sum.groups:
            state_sum.step(state_sum.ready())
    vs, cs, ss, ps = together([value_sum.f, value_sum.b], got, [state_sum.x], [small.x])
    value_sum.f, value_sum.b = vs
    small.x = ps[0]
    while small.groups:
        small.step(small.x)
    small, state_out = small.x, ss[0][0]
    value_out = value_sum.total()
    back_rows = keep[1].astype(f32) + near[1].astype(f32) + jnp.concatenate(cs, axis=0).astype(f32)
    back_scaled = back_rows * norm_gain[None, :]
    hidden_gradient = out_cotangent + inv_rms[:, None] * (
        back_scaled - scaled * jnp.mean(back_scaled * scaled, axis=-1)[:, None]
    )
    shared = small[8:].reshape(16, 256)
    index = dp * n_tensor + me
    all_count = n_dp * n_tensor
    kern_share = 2 * NS // all_count
    state_kernel_out = lax.dynamic_slice(shared, (0, index * kern_share), (5, kern_share))
    norm_out = lax.dynamic_slice(shared[5:11].reshape(D), (index * (D // all_count),), (D // all_count,))
    return (
        output,
        hidden_gradient,
        norm_out,
        jnp.stack([gate_out, value_out[:, :VW]], axis=1),
        state_out,
        value_out[:, VW : VW + heads],
        small[:4, :VW].T,
        small[4, :VW],
        state_kernel_out[:4].T,
        state_kernel_out[4],
        small[6, VW + 128 : VW + 128 + heads],
        small[6, VW : VW + heads],
        jnp.sum(small[5, :VW].reshape(heads, HW), axis=1),
        small[6, :VW],
        out_out,
    )


def solution(mesh):
    in_specs = (
        P(("dp", "tensor"), None),
        P(),
        P("dp", None, "tensor"),
        P("dp", None),
        P("dp", "tensor"),
        P("tensor", None),
        P("tensor"),
        P(),
        P(),
        P("tensor"),
        P("tensor"),
        P("tensor"),
        P("tensor"),
        P("dp", "tensor"),
        P(("dp", "tensor"), None),
        P(),
        P(),
        P(),
    )
    out_specs = (
        P(("dp", "tensor"), None),
        P(("dp", "tensor"), None),
        P(("dp", "tensor")),
        P("dp", None, "tensor"),
        P(("dp", "tensor"), None),
        P("dp", "tensor"),
        P("tensor", None),
        P("tensor"),
        P(("dp", "tensor"), None),
        P(("dp", "tensor")),
        P("tensor"),
        P("tensor"),
        P("tensor"),
        P("tensor"),
        P("dp", "tensor"),
    )
    return jax.shard_map(
        partial(body, mesh.shape["dp"], mesh.shape["tensor"]),
        mesh=mesh,
        in_specs=in_specs,
        out_specs=out_specs,
        check_vma=False,
    )
```

```python
from functools import partial

import jax, jax.numpy as jnp
from jax import lax
from jax.experimental import pallas as pl
from jax.experimental.pallas import tpu as pltpu
from jax.sharding import PartitionSpec as P
f32=jnp.float32; bf16=jnp.bfloat16
Q=128
NS=128
VW=768
HW=64
CW=1024
RW=1152
SPAN=256
FWD_LIMIT=14<<20
BACK_LIMIT=18<<20
NEG=-1e30

def mm(a,b,ca=1,cb=0):
    return lax.dot_general(a,b,(((ca,),(cb,)),((),())),preferred_element_type=f32)

def split2(x):
    hi=x.astype(bf16); return hi,(x-hi.astype(f32)).astype(bf16)

def split3(x):
    hi=x.astype(bf16); r=x-hi.astype(f32); mid=r.astype(bf16); return hi,mid,(r-mid.astype(f32)).astype(bf16)

def mm3(a,b,ca=1,cb=0):
    ah,al=split2(a); bh,bl=split2(b)
    return mm(jnp.concatenate([ah,ah,al],axis=ca),jnp.concatenate([bh,bl,bh],axis=cb),ca,cb)

def tri_sum(tri,x):
    a,b,c=split3(x); w=x.shape[1]
    p=mm(tri,jnp.concatenate([a,b,c],axis=1))
    return p[:,:w]+p[:,w:2*w]+p[:,2*w:]

def spread(x,ee):
    a,b=split2(x)
    return mm(jnp.concatenate([a,b],axis=1),ee)

def head_sum(x,hh):
    a,b=split2(x)
    return mm(jnp.concatenate([a,b],axis=1),hh)

def iotas():
    return lax.broadcasted_iota(jnp.int32,(Q,Q),0),lax.broadcasted_iota(jnp.int32,(Q,Q),1)

def softplus(z):
    return jnp.maximum(z,0.0)+jnp.log(1.0+jnp.exp(-jnp.abs(z)))

def sig(z):
    return 1.0/(1.0+jnp.exp(-z))

def halves(x):
    lane=lax.broadcasted_iota(jnp.int32,x.shape,1)
    lo=jnp.where(lane<HW,x,0.0); hi=jnp.where(lane<HW,0.0,x)
    return jnp.concatenate([lo.astype(bf16),hi.astype(bf16)],axis=0)

def spread_matrix(shape):
    r=lax.broadcasted_iota(jnp.int32,shape,0)%128; c=lax.broadcasted_iota(jnp.int32,shape,1)//HW
    return jnp.where(r==c,1.0,0.0).astype(bf16)

def sum_matrix(shape):
    r=lax.broadcasted_iota(jnp.int32,shape,0)%VW//HW; c=lax.broadcasted_iota(jnp.int32,shape,1)
    return jnp.where(r==c,1.0,0.0).astype(bf16)

def halves2(x):
    lane=lax.broadcasted_iota(jnp.int32,x.shape,1)
    h,l=split2(jnp.concatenate([jnp.where(lane<HW,x,0.0),jnp.where(lane<HW,0.0,x)],axis=0))
    return h,l

def fwd_kernel(c0,nc,first_ref,raw_ref,par_ref,*rest):
    y_ref,act_ref,sl_ref,sp_ref,wt_ref,lt_ref,s_ref,t_ref,ext,ee_ref=rest[-10:]
    ck_ref=par_ref
    i=pl.program_id(0)
    @pl.when(i==0)
    def _():
        ee_ref[...]=spread_matrix(ee_ref.shape)
        if c0:
            s_ref[...]=rest[0][...]; t_ref[...]=rest[1][...]
        else:
            s_ref[...]=jnp.zeros_like(s_ref); t_ref[...]=jnp.zeros_like(t_ref)
    c=c0+i
    start=(first_ref[c//(SPAN//Q)]==1)&(c%(SPAN//Q)==0)
    @pl.when(start)
    def _():
        s_ref[...]=jnp.zeros_like(s_ref); t_ref[...]=jnp.zeros_like(t_ref)
    ext[0:8,:]=t_ref[...]
    x=raw_ref[:,:CW]
    ext[8:8+Q,:]=x
    t_ref[...]=raw_ref[Q-8:Q,:CW]
    pre=par_ref[4:5,:]+ck_ref[3:4,:]*x
    for j in (1,2,3):
        pre=pre+ck_ref[3-j:4-j,:]*ext[8-j:8-j+Q,:]
    sg=sig(pre)
    act=pre*sg
    act_ref[...]=act
    sl_ref[...]=sg*(1.0+pre-act)
    v=act[:,:VW]; b=act[:,VW:VW+NS].astype(bf16); cc=act[:,VW+NS:].astype(bf16)
    dt=softplus(raw_ref[:,CW:]+par_ref[5:6,:128])
    a=-dt*jnp.exp(par_ref[6:7,:128])
    row,col=iotas()
    low=row>=col; up=row<=col
    tri=jnp.where(low,1.0,0.0).astype(bf16)
    cum=tri_sum(tri,a)
    cum_t=cum.T
    last=cum[Q-1:Q,:]
    ee=ee_ref[...]
    sprd=spread(jnp.concatenate([dt,jnp.exp(cum),jnp.exp(last-cum)],axis=0),ee)
    dte,ecum,etail=sprd[:Q],sprd[Q:2*Q],sprd[2*Q:]
    x=v*dte
    g=mm(cc,b,1,1)
    gt=mm(b,cc,1,1)
    parts=[]
    for p in range(VW//128):
        ws=[]
        for h in (2*p,2*p+1):
            d=jnp.where(low,cum[:,h:h+1]-cum_t[h:h+1,:],NEG)
            ws.append((jnp.exp(d)*g).astype(bf16))
            lt=jnp.exp(jnp.where(up,cum_t[h:h+1,:]-cum[:,h:h+1],NEG))
            lt_ref[:,h*Q:(h+1)*Q]=lt
            wt_ref[:,h*Q:(h+1)*Q]=(lt*gt).astype(bf16)
        parts.append(mm(jnp.concatenate(ws,axis=1),halves(x[:,128*p:128*p+128])))
    s=s_ref[...]
    sp_ref[0]=s
    y_ref[...]=jnp.concatenate(parts,axis=1)+ecum*mm(cc,s.astype(bf16))+par_ref[7:8,:VW]*v
    s_ref[...]=ecum[Q-1:Q,:]*s+mm(b,(x*etail).astype(bf16),0,0)

def bwd_kernel(c0,nc,nall,first_ref,raw_ref,act_ref,sl_ref,y_ref,dy_ref,sp_ref,wt_ref,lt_ref,par_ref,*rest):
    out_ref,vs_ref,ds_ref,sn_ref,h_ref,acc_ref,acs_ref,ext,ee_ref,hh_ref=rest[-10:]
    ck_ref=par_ref
    i=pl.program_id(0)
    @pl.when(i==0)
    def _():
        ee_ref[...]=spread_matrix(ee_ref.shape)
        hh_ref[...]=sum_matrix(hh_ref.shape)
        for k,ref in enumerate((ds_ref,sn_ref,h_ref,acc_ref,acs_ref)):
            ref[...]=jnp.zeros_like(ref) if c0+nc==nall else rest[k][...]
    c=c0+nc-1-i
    nxt=jnp.minimum(c+1,nall-1)
    start=(first_ref[nxt//(SPAN//Q)]==1)&(nxt%(SPAN//Q)==0)
    @pl.when(start)
    def _():
        ds_ref[...]=jnp.zeros_like(ds_ref); h_ref[...]=jnp.zeros_like(h_ref)
    act=act_ref[...]
    v=act[:,:VW]; bf=act[:,VW:VW+NS]; cf=act[:,VW+NS:]
    b=bf.astype(bf16); cc=cf.astype(bf16)
    z=raw_ref[:,CW:]+par_ref[5:6,:128]
    dt=softplus(z)
    edl=jnp.exp(par_ref[6:7,:128])
    a=-dt*edl
    row,col=iotas()
    low=row>=col; up=row<=col
    cum=tri_sum(jnp.where(low,1.0,0.0).astype(bf16),a)
    last=cum[Q-1:Q,:]
    ee=ee_ref[...]
    sprd=spread(jnp.concatenate([dt,jnp.exp(cum),jnp.exp(last-cum)],axis=0),ee)
    dte,ecum,etail=sprd[:Q],sprd[Q:2*Q],sprd[2*Q:]
    x=v*dte
    xb=x.astype(bf16)
    dy=dy_ref[...].astype(f32)
    dyb=dy.astype(bf16)
    dgt=jnp.zeros((Q,Q),f32)
    parts=[]
    for p in range(VW//128):
        cols=slice(128*p,128*p+128)
        dyh,dyl=split2(dy[:,cols])
        xh,xl=halves2(x[:,cols])
        dw=mm(jnp.concatenate([xh,xl,xh],axis=1),jnp.concatenate([dyh,dyh,dyl],axis=1),1,1)
        for k in (0,1):
            h=2*p+k
            dgt=dgt+lt_ref[:,h*Q:(h+1)*Q]*dw[k*Q:(k+1)*Q]
        parts.append(mm(wt_ref[:,2*Q*p:2*Q*(p+1)],halves(dy[:,cols])))
    ds=ds_ref[...]
    dsb=ds.astype(bf16)
    s=sp_ref[0]
    dxd=jnp.concatenate(parts,axis=1)
    bds=mm(b,dsb)
    dx=dxd+etail*bds
    xe=(x*etail).astype(bf16)
    dye=dy*ecum
    db=mm3(dgt,cf)+mm3(x*etail,ds,1,1)
    dc=mm3(dgt,bf,0,0)+mm3(dye,s,1,1)
    kk=jnp.sum(dsb.astype(f32)*sn_ref[...],axis=0,keepdims=True)
    kk=jnp.concatenate([kk,jnp.zeros((7,VW),f32)],axis=0)
    hs=head_sum(jnp.concatenate([dyb.astype(f32)*(y_ref[...]-par_ref[7:8,:VW]*v)-xb.astype(f32)*dxd-xe.astype(f32)*bds,v*dx,kk],axis=0),hh_ref[...])
    dcum,q,k0=hs[:Q],hs[Q:2*Q],hs[2*Q:2*Q+1]
    da=k0+tri_sum(jnp.where(up,1.0,0.0).astype(bf16),dcum)
    dst=(q-da*edl)*sig(z)
    ds_ref[...]=ecum[Q-1:Q,:]*ds+mm3(cf,dye,0,0)
    sn_ref[...]=s
    acs_ref[0:1,:]+=jnp.sum(da*a,axis=0,keepdims=True)
    acs_ref[1:2,:]+=jnp.sum(dst,axis=0,keepdims=True)
    dv=dte*dx+par_ref[7:8,:VW]*dy
    acc_ref[5:6,:VW]+=jnp.sum(dy*v,axis=0,keepdims=True)
    dpre=jnp.concatenate([dv,db,dc],axis=1)*sl_ref[...]
    ext[0:Q,:]=dpre
    ext[Q:Q+8,:]=h_ref[...]
    h_ref[...]=dpre[0:8,:]
    xr=raw_ref[:,:CW]
    draw=ck_ref[3:4,:]*dpre
    acc_ref[3:4,:]+=jnp.sum(dpre*xr,axis=0,keepdims=True)
    acc_ref[4:5,:]+=jnp.sum(dpre,axis=0,keepdims=True)
    for j in (1,2,3):
        sh=ext[j:j+Q,:]
        draw=draw+ck_ref[3-j:4-j,:]*sh
        acc_ref[3-j:4-j,:]+=jnp.sum(sh*xr,axis=0,keepdims=True)
    drawb,dstb=draw.astype(bf16),dst.astype(bf16)
    out_ref[:,:CW]=drawb
    out_ref[:,CW:]=dstb
    vs_ref[:,:VW]=drawb[:,:VW]
    vs_ref[:,VW:]=dstb

def sd(shape,dt=f32): return jax.ShapeDtypeStruct(shape,dt)

def hbm(shape,dt=f32): return pltpu.HBM(shape,dt)

def stay(x): return pltpu.with_memory_space_constraint(x,pltpu.HBM)

def whole(shape): return pl.BlockSpec(shape,lambda i,*_: (0,)*len(shape))

def once(shape): return pl.BlockSpec(shape,lambda i,*_: (0,)*len(shape),pipeline_mode=pl.Buffered(1))

HL=VW//HW

def ssd_fwd(c0,nc,nall,first,raw,par,carry):
    rb=lambda w: pl.BlockSpec((Q,w),lambda i,*_: (c0+i,0))
    any_spec=pl.BlockSpec(memory_space=pl.ANY)
    held=[whole((NS,VW)),whole((8,CW))]
    return pl.pallas_call(partial(fwd_kernel,c0,nc),
        out_shape=(sd((nall*Q,VW)),hbm((nall*Q,CW)),hbm((nall*Q,CW)),hbm((nall,NS,VW)),hbm((nall*Q,HL*Q),bf16),hbm((nall*Q,HL*Q)),sd((NS,VW)),sd((8,CW))),
        grid_spec=pltpu.PrefetchScalarGridSpec(num_scalar_prefetch=1,grid=(nc,),
            in_specs=[rb(RW),once((8,CW))]+(held+[any_spec]*6 if carry else []),
            out_specs=(rb(VW),rb(CW),rb(CW),pl.BlockSpec((1,NS,VW),lambda i,*_: (c0+i,0,0)),rb(HL*Q),rb(HL*Q),*held),
            scratch_shapes=[pltpu.VMEM((Q+8,CW),f32),pltpu.VMEM((256,VW),bf16)]),
        input_output_aliases={5+k:k for k in range(6)} if carry else {},
        compiler_params=pltpu.CompilerParams(vmem_limit_bytes=FWD_LIMIT),
        cost_estimate=pl.CostEstimate(flops=int(1.5e9*nc/8),bytes_accessed=30_000_000*nc//8,transcendentals=3_000_000*nc//8),
        name=f"ssd_forward_{c0}")(first,stay(raw),par,*(carry[6:]+carry[:1]+tuple(stay(x) for x in carry[1:6]) if carry else ()))

def ssd_bwd(c0,nc,nall,first,raw,act,sl,y,dy,sp,wt,lt,par,carry):
    rv=lambda w: pl.BlockSpec((Q,w),lambda i,*_: (c0+nc-1-i,0))
    any_spec=pl.BlockSpec(memory_space=pl.ANY)
    held=[whole((NS,VW)),whole((NS,VW)),whole((8,CW)),whole((8,CW)),whole((8,128))]
    return pl.pallas_call(partial(bwd_kernel,c0,nc,nall),
        out_shape=(sd((nall*Q,RW),bf16),sd((nall*Q,VW+128),bf16),sd((NS,VW)),sd((NS,VW)),sd((8,CW)),sd((8,CW)),sd((8,128))),
        grid_spec=pltpu.PrefetchScalarGridSpec(num_scalar_prefetch=1,grid=(nc,),
            in_specs=[rv(RW),rv(CW),rv(CW),rv(VW),rv(VW),pl.BlockSpec((1,NS,VW),lambda i,*_: (c0+nc-1-i,0,0)),rv(HL*Q),rv(HL*Q),once((8,CW))]
                     +(held+[any_spec]*2 if carry else []),
            out_specs=(rv(RW),rv(VW+128),*held),
            scratch_shapes=[pltpu.VMEM((Q+8,CW),f32),pltpu.VMEM((256,VW),bf16),pltpu.VMEM((2*VW,128),bf16)]),
        input_output_aliases={15+k:k for k in range(2)} if carry else {},
        compiler_params=pltpu.CompilerParams(vmem_limit_bytes=BACK_LIMIT),
        cost_estimate=pl.CostEstimate(flops=int(3e9*nc/8),bytes_accessed=60_000_000*nc//8,transcendentals=4_000_000*nc//8),
        name=f"ssd_backward_{c0}")(first,stay(raw),stay(act),stay(sl),y,dy,stay(sp),stay(wt),stay(lt),par,*(carry[2:]+carry[:2] if carry else ()))


D = 1536
H = 48
E = 3072
TOK_DEV = 1024
SEQ_DEV = 4
EPSILON = 1e-05
FWD_PARTS = ((0, 4), (4, 4))
BACK_PARTS = ((6, 2), (3, 3), (0, 3))


def contract(left, right, left_dim, right_dim, out=f32):
    return lax.dot_general(
        left, right, (((left_dim,), (right_dim,)), ((), ())), preferred_element_type=f32
    ).astype(out)


def span_layout(seq_lengths, seq_device, seq_offset, device):
    span_index = jnp.arange(SEQ_DEV, dtype=jnp.int32)
    needed = (seq_lengths + SPAN - 1) // SPAN
    owned_seq = (seq_device == device) & (seq_lengths > 0)
    relative = span_index[None, :] - seq_offset[:, None]
    inside = owned_seq[:, None] & (relative >= 0) & (relative < needed[:, None])
    live_rows = jnp.sum(
        jnp.where(inside, jnp.clip(seq_lengths[:, None] - relative * SPAN, 0, SPAN), 0), axis=0
    )
    seq_first = jnp.any(inside & (relative == 0), axis=0)
    return live_rows, seq_first.astype(jnp.int32)


def ring_order(count):
    if count == 8:
        return [0, 2, 4, 6, 7, 5, 3, 1]
    return list(range(count))


def lay(cols, rows, off_ref, refs, out):
    for k, (c0, w) in enumerate(cols):
        out[pl.ds(pl.multiple_of(off_ref[k] * rows, 16), rows), c0 : c0 + w] = refs[k][...]


def row_sums(x):
    a, b = split2(x)
    ones = jnp.ones((8, x.shape[1]), bf16)
    return mm(ones, a, 1, 1) + mm(ones, b, 1, 1)


def project_kernel(cols, rows, nx, off_ref, *refs):
    n = len(cols)
    xs = refs[n : n + nx]
    w_ref, x_ref, xt_ref, raw_ref = refs[n + nx :]
    i = pl.program_id(0)

    @pl.when(i == 0)
    def _():
        lay(cols, rows, off_ref, refs, w_ref)

    for k in range(nx):

        @pl.when(i == k)
        def _(k=k):
            x_ref[...] = xs[k][...]

    xt_ref[...] = x_ref[...].T
    raw_ref[...] = mm(x_ref[...], w_ref[...])


def project(pieces, offsets, xs, total):
    rows, n = pieces[0][0].shape[0], len(pieces)
    cols = [(c0, x.shape[1]) for x, c0 in pieces]
    width = max(c0 + w for c0, w in cols)
    q, depth = xs[0].shape
    nx = len(xs)
    at = lambda w: pl.BlockSpec((q, w), lambda i, off: (off[n + i], 0))
    return pl.pallas_call(
        partial(project_kernel, cols, rows, nx),
        out_shape=(sd((total, width), bf16), sd((q * nx, depth), bf16), sd((depth, q * nx), bf16), hbm((q * nx, width))),
        grid_spec=pltpu.PrefetchScalarGridSpec(
            num_scalar_prefetch=1,
            grid=(nx,),
            in_specs=[once(x.shape) for x, _ in pieces] + [once(x.shape) for x in xs],
            out_specs=(whole((total, width)), at(depth), pl.BlockSpec((depth, q), lambda i, off: (0, off[n + i])), at(width)),
        ),
        compiler_params=pltpu.CompilerParams(vmem_limit_bytes=22 << 20),
        cost_estimate=pl.CostEstimate(flops=2 * q * nx * total * width, bytes_accessed=30_000_000, transcendentals=0),
        name="project",
    )(offsets, *[x for x, _ in pieces], *xs)


def cotangent_kernel(cols, rows, nx, off_ref, *refs):
    n = len(cols)
    xs = refs[n : n + nx]
    normed_ref, ssd_ref, gain_ref, w_ref, xt_ref, gr_ref, by_ref, sum_ref, yr_ref, x_ref = refs[n + nx :]
    i = pl.program_id(0)

    @pl.when(i == 0)
    def _():
        lay(cols, rows, off_ref, refs, w_ref)

    for k in range(nx):

        @pl.when(i == k)
        def _(k=k):
            x_ref[...] = xs[k][...]

    xt_ref[...] = x_ref[...].T
    by = mm(x_ref[...], w_ref[:, VW:])
    gr = mm(normed_ref[...], w_ref[:, :VW])
    by_ref[...] = by
    gr_ref[...] = gr
    gated = ssd_ref[...] * (gr * sig(gr))
    scaled = gated * gain_ref[...]
    yr_ref[...] = scaled.astype(bf16)
    square = row_sums(gated * gated)
    cross = row_sums(by * scaled)
    top = lax.broadcasted_iota(jnp.int32, square.shape, 0) == 0
    sum_ref[0] = jnp.where(top, square, cross)


def cotangent(pieces, offsets, xs, normed, ssd, gain, total):
    rows, n = pieces[0][0].shape[0], len(pieces)
    cols = [(c0, x.shape[1]) for x, c0 in pieces]
    width = max(c0 + w for c0, w in cols)
    q, depth = xs[0].shape
    nx = len(xs)
    at = lambda w: pl.BlockSpec((q, w), lambda i, off: (off[n + i], 0))
    return pl.pallas_call(
        partial(cotangent_kernel, cols, rows, nx),
        out_shape=(
            sd((total, width), bf16),
            sd((depth, q * nx), bf16),
            sd((q * nx, VW)),
            sd((q * nx, VW)),
            sd((nx, 8, q)),
            sd((q * nx, VW), bf16),
        ),
        grid_spec=pltpu.PrefetchScalarGridSpec(
            num_scalar_prefetch=1,
            grid=(nx,),
            in_specs=[once(x.shape) for x, _ in pieces]
            + [once(x.shape) for x in xs]
            + [at(depth), at(VW), once((1, VW))],
            out_specs=(
                whole((total, width)),
                pl.BlockSpec((depth, q), lambda i, off: (0, off[n + i])),
                at(VW),
                at(VW),
                pl.BlockSpec((1, 8, q), lambda i, off: (off[n + i], 0, 0)),
                at(VW),
            ),
            scratch_shapes=[pltpu.VMEM((q, depth), bf16)],
        ),
        compiler_params=pltpu.CompilerParams(vmem_limit_bytes=30 << 20),
        cost_estimate=pl.CostEstimate(flops=2 * q * nx * total * width, bytes_accessed=30_000_000, transcendentals=800_000),
        name="cotangent",
    )(offsets, *[x for x, _ in pieces], *xs, normed, ssd, gain)


def gate_kernel(sum_ref, by_ref, gr_ref, ssd_ref, gain_ref, ny_ref, bg_ref, dy_ref, gg_ref):
    @pl.when(pl.program_id(0) == 0)
    def _():
        gg_ref[...] = jnp.zeros_like(gg_ref)

    sums = sum_ref[0].T
    inv = lax.rsqrt(sums[:, 0:1] / E + EPSILON)
    gr, ssd, by, gain = gr_ref[...], ssd_ref[...], by_ref[...], gain_ref[...]
    sg = sig(gr)
    gate = gr * sg
    unit = ssd * gate * inv
    ny_ref[...] = (unit * gain).astype(bf16)
    gg_ref[0:1, :] += jnp.sum(by * unit, axis=0, keepdims=True)
    back = inv * (by * gain - unit * (inv * sums[:, 1:2] / E))
    bg_ref[...] = (back * ssd * (sg * (1.0 + gr - gate))).astype(bf16)
    dy_ref[...] = back * gate


def gate_back(sums, by, gate_raw, ssd, gain):
    t, width = by.shape
    n, _, q = sums.shape
    rb = pl.BlockSpec((q, width), lambda i: (i, 0))
    return pl.pallas_call(
        gate_kernel,
        out_shape=(sd((t, width), bf16), sd((t, width), bf16), sd((t, width)), sd((8, width))),
        grid=(n,),
        in_specs=[pl.BlockSpec((1, 8, q), lambda i: (i, 0, 0)), rb, rb, rb, once((1, width))],
        out_specs=(rb, rb, rb, whole((8, width))),
        compiler_params=pltpu.CompilerParams(vmem_limit_bytes=12 << 20),
        cost_estimate=pl.CostEstimate(flops=20_000_000, bytes_accessed=15_000_000, transcendentals=800_000),
        name="gate_back",
    )(sums, by, gate_raw, ssd, gain)


def normed_kernel(at_ref, first_ref, gate_ref, w_ref, g_ref, x_ref, ng_in, out_ref, ng_ref):
    @pl.when(pl.program_id(0) == 0)
    def _():
        ng_ref[...] = ng_in[...]

    back = mm(first_ref[...], w_ref[...], 1, 1) + mm(gate_ref[...], g_ref[...], 1, 1)
    out_ref[0] = back.astype(bf16)
    ng_ref[0:1, :] += jnp.sum(back * x_ref[...].astype(f32), axis=0, keepdims=True)


def back_normed_rows(at, q, first, gate, w, gate_w, normed, ng):
    depth = normed.shape[1]
    n = at.shape[0]
    rb = lambda c: pl.BlockSpec((q, c), lambda i, at: (at[i], 0))
    return pl.pallas_call(
        normed_kernel,
        out_shape=(sd((n, q, depth), bf16), sd((8, depth))),
        grid_spec=pltpu.PrefetchScalarGridSpec(
            num_scalar_prefetch=1,
            grid=(n,),
            in_specs=[rb(RW), rb(VW), once(w.shape), once((depth, VW)), rb(depth), once((8, depth))],
            out_specs=(pl.BlockSpec((1, q, depth), lambda i, at: (i, 0, 0)), whole((8, depth))),
        ),
        compiler_params=pltpu.CompilerParams(vmem_limit_bytes=16 << 20),
        cost_estimate=pl.CostEstimate(flops=2 * n * q * depth * (RW + VW), bytes_accessed=30_000_000, transcendentals=0),
        name="back_normed",
    )(at, first, gate, w, gate_w, normed, ng)


def mixer_kernel(half, at_ref, x_ref, w_ref, away_ref, keep_ref):
    r = mm(x_ref[...], w_ref[...], 1, 1).astype(bf16)
    i = pl.program_id(0)

    @pl.when(i < half)
    def _():
        away_ref[0] = r

    @pl.when(i >= half)
    def _():
        keep_ref[0] = r


def mixer_blocks(at, q, x, w):
    n, depth, width = at.shape[0], w.shape[0], x.shape[1]
    half = n // 2
    return pl.pallas_call(
        partial(mixer_kernel, half),
        out_shape=(sd((half, q, depth), bf16), sd((half, q, depth), bf16)),
        grid_spec=pltpu.PrefetchScalarGridSpec(
            num_scalar_prefetch=1,
            grid=(n,),
            in_specs=[
                pl.BlockSpec((q, width), lambda i, at: (at[i], 0)),
                pl.BlockSpec((depth, width), lambda i, at: (0, 1), pipeline_mode=pl.Buffered(1)),
            ],
            out_specs=(
                pl.BlockSpec((1, q, depth), lambda i, at: (jnp.minimum(i, half - 1), 0, 0)),
                pl.BlockSpec((1, q, depth), lambda i, at: (jnp.maximum(i - half, 0), 0, 0)),
            ),
        ),
        compiler_params=pltpu.CompilerParams(vmem_limit_bytes=12 << 20),
        cost_estimate=pl.CostEstimate(flops=2 * n * q * depth * width, bytes_accessed=20_000_000, transcendentals=0),
        name="mixer_rows",
    )(at, x, w)


def grad_kernel(per, rows, at_ref, xt_ref, back_ref, out_ref):
    i = pl.program_id(0)
    r = mm(xt_ref[...], back_ref[...]).astype(bf16)
    for d in range(per):
        out_ref[pl.ds(at_ref[i * per + d], 1)] = r[d * rows : (d + 1) * rows][None]


def weight_grad(at, xt, back, n_dp):
    depth, t = xt.shape
    rows, width = depth // n_dp, back.shape[1]
    steps = 2
    return pl.pallas_call(
        partial(grad_kernel, n_dp // steps, rows),
        out_shape=sd((n_dp, rows, width), bf16),
        grid_spec=pltpu.PrefetchScalarGridSpec(
            num_scalar_prefetch=1,
            grid=(steps,),
            in_specs=[pl.BlockSpec((depth // steps, t), lambda i, at: (i, 0)), once(back.shape)],
            out_specs=whole((n_dp, rows, width)),
        ),
        compiler_params=pltpu.CompilerParams(vmem_limit_bytes=16 << 20),
        cost_estimate=pl.CostEstimate(flops=2 * depth * t * width, bytes_accessed=8_000_000, transcendentals=0),
        name="weight_grad",
    )(at, xt, back)


def pair_grad_kernel(per, rows, at_ref, xt_ref, back_ref, zt_ref, y_ref, out_ref):
    i = pl.program_id(0)
    for k, r in enumerate((mm(xt_ref[...], back_ref[...]), mm(zt_ref[...], y_ref[...]))):
        r = r.astype(bf16)
        for d in range(per):
            out_ref[pl.ds(at_ref[i * per + d], 1), :, k * VW : (k + 1) * VW] = r[d * rows : (d + 1) * rows][None]


def pair_grad(at, xt, back, zt, y, n_dp):
    depth, t = xt.shape
    rows, steps = depth // n_dp, 4
    rb = pl.BlockSpec((depth // steps, t), lambda i, at: (i, 0))
    return pl.pallas_call(
        partial(pair_grad_kernel, n_dp // steps, rows),
        out_shape=sd((n_dp, rows, 2 * VW), bf16),
        grid_spec=pltpu.PrefetchScalarGridSpec(
            num_scalar_prefetch=1,
            grid=(steps,),
            in_specs=[rb, once(back.shape), rb, once(y.shape)],
            out_specs=whole((n_dp, rows, 2 * VW)),
        ),
        compiler_params=pltpu.CompilerParams(vmem_limit_bytes=22 << 20),
        cost_estimate=pl.CostEstimate(flops=4 * depth * t * VW, bytes_accessed=14_000_000, transcendentals=0),
        name="pair_grad",
    )(at, xt, back, zt, y)


def state_grad_kernel(n_tensor, per, rows, at_ref, xt_ref, back_ref, out_ref):
    i = pl.program_id(0)
    share = rows // n_tensor
    r = mm(xt_ref[...], back_ref[...]).astype(bf16)
    for d in range(per):
        for t in range(n_tensor):
            k = d * n_tensor + t
            out_ref[pl.ds(at_ref[i * per * n_tensor + k], 1)] = r[k * share : (k + 1) * share][None]


def state_weight_grad(at, xt, back, n_dp, n_tensor):
    depth, t = xt.shape
    rows = depth // n_dp
    share, width, steps = rows // n_tensor, 2 * NS, 2
    return pl.pallas_call(
        partial(state_grad_kernel, n_tensor, n_dp // steps, rows),
        out_shape=sd((n_tensor * n_dp, share, width), bf16),
        grid_spec=pltpu.PrefetchScalarGridSpec(
            num_scalar_prefetch=1,
            grid=(steps,),
            in_specs=[pl.BlockSpec((depth // steps, t), lambda i, at: (i, 0)), pl.BlockSpec((t, width), lambda i, at: (0, VW // width))],
            out_specs=whole((n_tensor * n_dp, share, width)),
        ),
        compiler_params=pltpu.CompilerParams(vmem_limit_bytes=10 << 20),
        cost_estimate=pl.CostEstimate(flops=2 * depth * t * width, bytes_accessed=5_000_000, transcendentals=0),
        name="state_weight_grad",
    )(at, xt, back)


class Ring:
    def __init__(self, count):
        self.count = count
        self.half = count // 2
        self.order = ring_order(count)
        at = {d: i for i, d in enumerate(self.order)}
        self.table = [[self.order[(at[d] + k) % count] for k in range(count)] for d in range(count)]
        self.ahead = [(self.order[i], self.order[(i + 1) % count]) for i in range(count)]
        self.back = [(b, a) for a, b in self.ahead]

    def rows_of(self, table):
        return jnp.asarray(table, jnp.int32)[lax.axis_index("dp")]

    def hop(self, f, b):
        return lax.ppermute(f, "dp", self.ahead), lax.ppermute(b, "dp", self.back)


class Gather:
    def __init__(self, ring, x):
        self.ring, self.mid = ring, x.shape[1] // 2 // 128 * 128
        self.pieces, self.f, self.b, self.s = [(x, 0)], x, x, 0

    def ready(self):
        if self.s == self.ring.half - 1:
            return [self.f[:, : self.mid], self.b[:, self.mid :]]
        return [self.f, self.b]

    def step(self, f, b):
        self.s += 1
        self.f, self.b = self.ring.hop(f, b)
        self.pieces += [(self.f, 0), (self.b, self.mid if self.s == self.ring.half else 0)]

    @staticmethod
    def offsets(ring):
        ahead = [0]
        for s in range(1, ring.half + 1):
            ahead += [ring.count - s, s]
        return [[ring.table[d][k] for k in ahead] for d in range(ring.count)]


class Scatter:
    def __init__(self, ring, x):
        self.ring, self.x, self.mid, self.s = ring, x, x.shape[2] // 2 // 128 * 128, ring.half

    def ready(self):
        x, s, mid = self.x, self.s, self.mid
        if s == self.ring.half:
            return [x[s, :, :mid], x[s, :, mid:]]
        f, b = self.f, self.b
        if s == self.ring.half - 1:
            f = jnp.pad(f, ((0, 0), (0, x.shape[2] - mid)))
            b = jnp.pad(b, ((0, 0), (mid, 0)))
        f = x[s].astype(f32) + f.astype(f32)
        b = x[self.ring.count - s].astype(f32) + b.astype(f32)
        return [f.astype(bf16), b.astype(bf16)]

    def step(self, f, b):
        self.f, self.b = self.ring.hop(f, b)
        self.s -= 1

    def total(self):
        return self.x[0].astype(f32) + self.f.astype(f32) + self.b.astype(f32)


def swap(x, axis, count, bits):
    return lax.ppermute(x, axis, [(i, i ^ bits) for i in range(count)])


def tensor_order(count):
    keys = [0]
    bit = count // 2
    while bit:
        keys += [k ^ bit for k in keys]
        bit //= 2
    return keys


def pick(x, index, axis=0):
    return lax.dynamic_index_in_dim(x, index, axis, keepdims=False)


def groups_of(count):
    bits = [1 << k for k in range(count.bit_length() - 1)]
    first = len(bits) % 2
    return ([bits[:first]] if first else []) + [bits[k : k + 2] for k in range(first, len(bits), 2)]


def others(bits):
    return [bits[0]] if len(bits) == 1 else [bits[0], bits[1], bits[0] | bits[1]]


class Spread:
    def __init__(self, x, axis, count):
        self.x, self.axis, self.count, self.groups = x, axis, count, groups_of(count)

    def step(self, x):
        bits = self.groups.pop(0)
        self.x = sum((swap(x, self.axis, self.count, k) for k in others(bits)), x)


class Share:
    def __init__(self, x, axis, count):
        self.x, self.axis, self.count, self.groups = x, axis, count, groups_of(count)

    def ready(self):
        bits = self.groups[0]
        n = 2 ** len(bits)
        self.parts = self.x.reshape((self.x.shape[0] // n, n) + self.x.shape[1:])
        return [self.parts[:, k // bits[0]].astype(bf16) for k in others(bits)]

    def step(self, sends):
        bits = self.groups.pop(0)
        got = [swap(x, self.axis, self.count, k) for x, k in zip(sends, others(bits))]
        self.x = sum((g.astype(f32) for g in got), self.parts[:, 0].astype(f32))


def together(*lists):
    flat = lax.optimization_barrier(tuple(x for xs in lists for x in xs))
    out, at = [], 0
    for xs in lists:
        out.append(list(flat[at : at + len(xs)]))
        at += len(xs)
    return out


def body(
    n_dp,
    n_tensor,
    hidden_in,
    norm_gain,
    gate_value_weight,
    state_proj_weight,
    step_weight,
    conv_value_kernel,
    conv_value_bias,
    conv_state_kernel,
    conv_state_bias,
    step_bias,
    decay_log,
    skip_scale,
    gate_norm_gain,
    out_weight,
    out_cotangent,
    seq_lengths,
    seq_device,
    seq_offset,
):
    quarter = hidden_in.shape[0]
    heads = step_weight.shape[1]
    rows = gate_value_weight.shape[0]
    me, dp = lax.axis_index("tensor"), lax.axis_index("dp")
    ring = Ring(n_dp)
    ring_at = ring.rows_of([[ring.table[d].index(k) for k in range(n_dp)] for d in range(n_dp)])
    order = me ^ jnp.asarray([3, 1, 2, 0], jnp.int32)
    ids = jnp.arange(n_dp * n_tensor, dtype=jnp.int32)
    state_at = (ids % n_tensor ^ me) * n_dp + (ids // n_tensor ^ dp)
    offsets = jnp.concatenate([ring.rows_of(Gather.offsets(ring)), me ^ jnp.asarray(tensor_order(n_tensor), jnp.int32)])
    to_core = lambda x: swap(x, "tensor", n_tensor, 1)
    to_far = lambda x: swap(x, "tensor", n_tensor, 2)

    live_rows, seq_first = span_layout(seq_lengths, seq_device, seq_offset, dp)
    row = me * quarter + jnp.arange(quarter, dtype=jnp.int32)
    local_live = jnp.sum(
        jnp.where((row // SPAN)[:, None] == jnp.arange(SEQ_DEV)[None, :], live_rows[None, :], 0), axis=1
    )
    local_mask = (row % SPAN < local_live).astype(f32)

    pad_to = lambda x, w: jnp.pad(x, (0, w - x.shape[0]))[None]
    params = jnp.concatenate(
        [
            jnp.concatenate([conv_value_kernel, conv_state_kernel], axis=0).T,
            jnp.concatenate([conv_value_bias, conv_state_bias])[None],
            pad_to(step_bias, CW),
            pad_to(decay_log, CW),
            pad_to(jnp.repeat(skip_scale, HW), CW),
        ],
        axis=0,
    )
    gain = gate_norm_gain[None]
    zeros = lambda *s: jnp.zeros(s, f32)

    first_own = jnp.concatenate(
        [gate_value_weight[:, 1, :], state_proj_weight, jnp.pad(step_weight, ((0, 0), (0, 128 - heads)))], axis=1
    )
    first_own, hidden = lax.optimization_barrier((first_own, hidden_in))
    inv_rms = lax.rsqrt(jnp.mean(hidden * hidden, axis=-1) + EPSILON)
    scaled = hidden * inv_rms[:, None]
    normed_local = (scaled * norm_gain[None, :]).astype(bf16)
    first = Gather(ring, first_own)
    first.step(*first.ready())
    normed_parts = [normed_local, to_far(normed_local)]
    out_own = jnp.concatenate([gate_value_weight[:, 0, :], out_weight], axis=1)
    back_local = (local_mask[:, None] * out_cotangent).astype(bf16)
    (out_own, offsets, ring_at, order, state_at, seq_first, params, back_local) = lax.optimization_barrier(
        (out_own, offsets, ring_at, order, state_at, seq_first, params, back_local)
    )
    out = Gather(ring, out_own)
    far = normed_parts[1]
    for s in range(1, ring.half):
        extra = []
        if s == min(2, ring.half - 1):
            extra = [[normed_local, far]]
        elif s == ring.half - 1:
            extra = [[back_local] + normed_parts[2:]]
        sends = together(first.ready(), *extra)
        first.step(*sends.pop(0))
        if s == min(2, ring.half - 1):
            [a, far] = sends.pop(0)
            normed_parts = [a, far, to_core(a), to_core(far)]
        elif s == ring.half - 1:
            [back_local, *normed_parts[2:]] = sends.pop(0)
            back_far = to_far(back_local)
    ps, os = together([x for x, _ in first.pieces] + normed_parts, out.ready())
    out.step(*os)
    n = len(first.pieces)
    first_w, normed, normed_t, raw = project(
        [(x, c0) for x, (_, c0) in zip(ps, first.pieces)], offsets, ps[n:], D
    )
    chunks = TOK_DEV // Q
    carry = ()
    for k, (c0, n) in enumerate(FWD_PARTS):
        held, os, bs = together([carry[6]] if carry else [raw], out.ready(), [back_local, back_far] if k == 0 else [])
        out.step(*os)
        if k:
            carry = carry[:6] + (held[0],) + carry[7:]
        else:
            raw = held[0]
            back_parts = bs + [to_core(x) for x in bs]
        carry = tuple(ssd_fwd(c0, n, chunks, seq_first, raw, params, carry))
    held, os, back_parts = together([carry[0]], out.ready(), back_parts)
    carry = (held[0],) + carry[1:]
    out.step(*os)
    while out.s < ring.half:
        out.step(*out.ready())
    ssd, act, slope, states, weights_t, decays_t = carry[:6]

    out_w, back_t, gate_raw, back_y, sums, gated = cotangent(
        out.pieces, offsets, back_parts, normed, ssd, gain, D
    )
    total = Spread(sums, "tensor", n_tensor)
    while total.groups:
        total.step(total.x)
    sums = total.x
    mixer = mixer_blocks(order, quarter, gated, out_w)
    sums, mixer_away, mixer_keep = lax.optimization_barrier((sums, *mixer))
    normed_y, back_gate, back_ssd, gain_grad = gate_back(sums, back_y, gate_raw, ssd, gain)
    pair_sum = Scatter(ring, pair_grad(ring_at, normed_t, back_gate, back_t, normed_y, n_dp))

    half_rows = quarter // 2
    carry, ms = (), [mixer_away]
    for k, (c0, n) in enumerate(BACK_PARTS):
        held, ps, ms = together([carry[2]] if carry else [back_ssd], pair_sum.ready() if pair_sum.s else [], ms)
        if carry:
            carry = carry[:2] + (held[0],) + carry[3:]
        else:
            back_ssd = held[0]
        if pair_sum.s:
            pair_sum.step(*ps)
        if k == 0:
            mixer_near = to_core(ms[0])
            ms = [(mixer_keep[0].astype(f32) + mixer_near[0].astype(f32)).astype(bf16)]
        elif k == 1:
            ms = [to_far(ms[0])]
        carry = tuple(
            ssd_bwd(
                c0, n, chunks, seq_first, raw, act, slope, ssd, back_ssd, states, weights_t, decays_t, params, carry
            )
        )
    mixer_far = ms[0]
    back_first, back_vs, _, _, _, acc, acs = carry
    square = pick(sums, me)[0]
    local_inv = lax.rsqrt(square / E + EPSILON)

    value_sum = Scatter(ring, weight_grad(ring_at, normed_t, back_vs, n_dp))
    gs, vs, [mixer_far], [back_first] = together(pair_sum.ready(), value_sum.ready(), [mixer_far], [back_first])
    value_sum.step(*vs)
    pair_sum.step(*gs)
    state_sum = Share(
        state_weight_grad(state_at, normed_t, back_first, n_dp, n_tensor).reshape(n_tensor, n_dp, rows // n_tensor, 2 * NS),
        "tensor",
        n_tensor,
    )
    away, ng = back_normed_rows(order[:2], quarter, back_first, back_gate, first_w, out_w, normed, zeros(8, D))
    keep, ng = back_normed_rows(order[2:], quarter, back_first, back_gate, first_w, out_w, normed, ng)
    vs, gs, cs, ss, [keep, ng, mixer_far] = together(
        value_sum.ready(), [pair_sum.f, pair_sum.b], [away], state_sum.ready(), [keep, ng, mixer_far]
    )
    value_sum.step(*vs)
    pair_sum.f, pair_sum.b = gs
    near = to_core(cs[0])
    state_sum.step(ss)
    while pair_sum.s:
        pair_sum.step(*pair_sum.ready())
    pair_out = pair_sum.total()
    output = hidden_in + (local_mask * local_inv)[:, None] * (
        mixer_keep[1].astype(f32) + mixer_near[1].astype(f32) + mixer_far.astype(f32)
    )
    away = (keep[0].astype(f32) + near[0].astype(f32)).astype(bf16)
    state_sum = Share(state_sum.x[0], "dp", n_dp)
    shared = jnp.concatenate([acc[:5, VW:], (ng[0] / norm_gain).reshape(6, 256), zeros(5, 256)], axis=0)
    shared = Spread(shared, "tensor", n_tensor)
    vs, cs, ss, ps = together(value_sum.ready(), [away[:half_rows], away[half_rows:]], state_sum.ready(), [shared.x])
    value_sum.step(*vs)
    got = [to_far(cs[0])]
    state_sum.step(ss)
    shared.step(ps[0])
    own = jnp.concatenate(
        [acc[:6], jnp.concatenate([gain_grad[0], acs[0], acs[1]])[None], zeros(1, CW)], axis=0
    )
    while shared.groups:
        shared.step(shared.x)
    small = Spread(jnp.concatenate([own, shared.x.reshape(4, CW)], axis=0), "dp", n_dp)
    vs, cs, ss, ps = together(value_sum.ready(), [got[0], cs[1]], state_sum.ready(), [small.x])
    value_sum.step(*vs)
    got = [cs[0], to_far(cs[1])]
    state_sum.step(ss)
    small.step(ps[0])
    if value_sum.s:
        while value_sum.s:
            value_sum.step(*value_sum.ready())
        while state_sum.groups:
            state_sum.step(state_sum.ready())
    vs, cs, ss, ps = together([value_sum.f, value_sum.b], got, [state_sum.x], [small.x])
    value_sum.f, value_sum.b = vs
    small.x = ps[0]
    while small.groups:
        small.step(small.x)
    small, state_out = small.x, ss[0][0]
    value_out = value_sum.total()
    back_rows = keep[1].astype(f32) + near[1].astype(f32) + jnp.concatenate(cs, axis=0).astype(f32)
    back_scaled = back_rows * norm_gain[None, :]
    hidden_gradient = out_cotangent + inv_rms[:, None] * (
        back_scaled - scaled * jnp.mean(back_scaled * scaled, axis=-1)[:, None]
    )
    shared = small[8:].reshape(16, 256)
    index = dp * n_tensor + me
    all_count = n_dp * n_tensor
    kern_share = 2 * NS // all_count
    state_kernel_out = lax.dynamic_slice(shared, (0, index * kern_share), (5, kern_share))
    norm_out = lax.dynamic_slice(shared[5:11].reshape(D), (index * (D // all_count),), (D // all_count,))
    return (
        output,
        hidden_gradient,
        norm_out,
        jnp.stack([pair_out[:, :VW], value_out[:, :VW]], axis=1),
        state_out,
        value_out[:, VW : VW + heads],
        small[:4, :VW].T,
        small[4, :VW],
        state_kernel_out[:4].T,
        state_kernel_out[4],
        small[6, VW + 128 : VW + 128 + heads],
        small[6, VW : VW + heads],
        jnp.sum(small[5, :VW].reshape(heads, HW), axis=1),
        small[6, :VW],
        pair_out[:, VW:],
    )


def solution(mesh):
    in_specs = (
        P(("dp", "tensor"), None),
        P(),
        P("dp", None, "tensor"),
        P("dp", None),
        P("dp", "tensor"),
        P("tensor", None),
        P("tensor"),
        P(),
        P(),
        P("tensor"),
        P("tensor"),
        P("tensor"),
        P("tensor"),
        P("dp", "tensor"),
        P(("dp", "tensor"), None),
        P(),
        P(),
        P(),
    )
    out_specs = (
        P(("dp", "tensor"), None),
        P(("dp", "tensor"), None),
        P(("dp", "tensor")),
        P("dp", None, "tensor"),
        P(("dp", "tensor"), None),
        P("dp", "tensor"),
        P("tensor", None),
        P("tensor"),
        P(("dp", "tensor"), None),
        P(("dp", "tensor")),
        P("tensor"),
        P("tensor"),
        P("tensor"),
        P("tensor"),
        P("dp", "tensor"),
    )
    return jax.shard_map(
        partial(body, mesh.shape["dp"], mesh.shape["tensor"]),
        mesh=mesh,
        in_specs=in_specs,
        out_specs=out_specs,
        check_vma=False,
    )
```

```python
from functools import partial

import jax, jax.numpy as jnp
from jax import lax
from jax.experimental import pallas as pl
from jax.experimental.pallas import tpu as pltpu
from jax.sharding import PartitionSpec as P
f32=jnp.float32; bf16=jnp.bfloat16
Q=128
NS=128
VW=768
HW=64
CW=1024
RW=1152
SPAN=256
FWD_LIMIT=14<<20
BACK_LIMIT=18<<20
NEG=-1e30

def mm(a,b,ca=1,cb=0):
    return lax.dot_general(a,b,(((ca,),(cb,)),((),())),preferred_element_type=f32)

def split2(x):
    hi=x.astype(bf16); return hi,(x-hi.astype(f32)).astype(bf16)

def split3(x):
    hi=x.astype(bf16); r=x-hi.astype(f32); mid=r.astype(bf16); return hi,mid,(r-mid.astype(f32)).astype(bf16)

def mm3(a,b,ca=1,cb=0):
    ah,al=split2(a); bh,bl=split2(b)
    return mm(jnp.concatenate([ah,ah,al],axis=ca),jnp.concatenate([bh,bl,bh],axis=cb),ca,cb)

def tri_sum(tri,x):
    a,b,c=split3(x); w=x.shape[1]
    p=mm(tri,jnp.concatenate([a,b,c],axis=1))
    return p[:,:w]+p[:,w:2*w]+p[:,2*w:]

def spread(x,ee):
    a,b=split2(x)
    return mm(jnp.concatenate([a,b],axis=1),ee)

def iotas():
    return lax.broadcasted_iota(jnp.int32,(Q,Q),0),lax.broadcasted_iota(jnp.int32,(Q,Q),1)

def softplus(z):
    return jnp.maximum(z,0.0)+jnp.log(1.0+jnp.exp(-jnp.abs(z)))

def sig(z):
    return 1.0/(1.0+jnp.exp(-z))

def halves(x):
    lane=lax.broadcasted_iota(jnp.int32,x.shape,1)
    lo=jnp.where(lane<HW,x,0.0); hi=jnp.where(lane<HW,0.0,x)
    return jnp.concatenate([lo.astype(bf16),hi.astype(bf16)],axis=0)

def spread_matrix(shape):
    r=lax.broadcasted_iota(jnp.int32,shape,0)%128; c=lax.broadcasted_iota(jnp.int32,shape,1)//HW
    return jnp.where(r==c,1.0,0.0).astype(bf16)

def sum_matrix(shape):
    r=lax.broadcasted_iota(jnp.int32,shape,0)%VW//HW; c=lax.broadcasted_iota(jnp.int32,shape,1)
    return jnp.where(r==c,1.0,0.0).astype(bf16)

def halves2(x):
    lane=lax.broadcasted_iota(jnp.int32,x.shape,1)
    h,l=split2(jnp.concatenate([jnp.where(lane<HW,x,0.0),jnp.where(lane<HW,0.0,x)],axis=0))
    return h,l

def fwd_kernel(c0,nc,first_ref,raw_ref,par_ref,*rest):
    y_ref,act_ref,sl_ref,sp_ref,wt_ref,lt_ref,s_ref,t_ref,ext,ee_ref=rest[-10:]
    ck_ref=par_ref
    i=pl.program_id(0)
    @pl.when(i==0)
    def _():
        ee_ref[...]=spread_matrix(ee_ref.shape)
        if c0:
            s_ref[...]=rest[0][...]; t_ref[...]=rest[1][...]
        else:
            s_ref[...]=jnp.zeros_like(s_ref); t_ref[...]=jnp.zeros_like(t_ref)
    c=c0+i
    start=(first_ref[c//(SPAN//Q)]==1)&(c%(SPAN//Q)==0)
    @pl.when(start)
    def _():
        s_ref[...]=jnp.zeros_like(s_ref); t_ref[...]=jnp.zeros_like(t_ref)
    ext[0:8,:]=t_ref[...]
    x=raw_ref[:,:CW]
    ext[8:8+Q,:]=x
    t_ref[...]=raw_ref[Q-8:Q,:CW]
    pre=par_ref[4:5,:]+ck_ref[3:4,:]*x
    for j in (1,2,3):
        pre=pre+ck_ref[3-j:4-j,:]*ext[8-j:8-j+Q,:]
    sg=sig(pre)
    act=pre*sg
    act_ref[...]=act
    sl_ref[...]=sg*(1.0+pre-act)
    v=act[:,:VW]; b=act[:,VW:VW+NS].astype(bf16); cc=act[:,VW+NS:].astype(bf16)
    dt=softplus(raw_ref[:,CW:]+par_ref[5:6,:128])
    a=-dt*jnp.exp(par_ref[6:7,:128])
    row,col=iotas()
    low=row>=col; up=row<=col
    tri=jnp.where(low,1.0,0.0).astype(bf16)
    cum=tri_sum(tri,a)
    cum_t=cum.T
    last=cum[Q-1:Q,:]
    ee=ee_ref[...]
    sprd=spread(jnp.concatenate([dt,jnp.exp(cum),jnp.exp(last-cum)],axis=0),ee)
    dte,ecum,etail=sprd[:Q],sprd[Q:2*Q],sprd[2*Q:]
    x=v*dte
    g=mm(cc,b,1,1)
    gt=mm(b,cc,1,1)
    parts=[]
    for p in range(VW//128):
        ws=[]
        for h in (2*p,2*p+1):
            d=jnp.where(low,cum[:,h:h+1]-cum_t[h:h+1,:],NEG)
            ws.append((jnp.exp(d)*g).astype(bf16))
            lt=jnp.exp(jnp.where(up,cum_t[h:h+1,:]-cum[:,h:h+1],NEG))
            lt_ref[:,h*Q:(h+1)*Q]=lt
            wt_ref[:,h*Q:(h+1)*Q]=(lt*gt).astype(bf16)
        parts.append(mm(jnp.concatenate(ws,axis=1),halves(x[:,128*p:128*p+128])))
    s=s_ref[...]
    sp_ref[0]=s
    y_ref[...]=jnp.concatenate(parts,axis=1)+ecum*mm(cc,s.astype(bf16))+par_ref[7:8,:VW]*v
    s_ref[...]=ecum[Q-1:Q,:]*s+mm(b,(x*etail).astype(bf16),0,0)

def bwd_kernel(c0,nc,nall,first_ref,raw_ref,act_ref,sl_ref,y_ref,dy_ref,sp_ref,wt_ref,lt_ref,par_ref,*rest):
    out_ref,ds_ref,sn_ref,h_ref,acc_ref,acs_ref,ext,ee_ref,hh_ref=rest[-9:]
    ck_ref=par_ref
    i=pl.program_id(0)
    @pl.when(i==0)
    def _():
        ee_ref[...]=spread_matrix(ee_ref.shape)
        hh_ref[...]=sum_matrix(hh_ref.shape)
        for k,ref in enumerate((ds_ref,sn_ref,h_ref,acc_ref,acs_ref)):
            ref[...]=jnp.zeros_like(ref) if c0+nc==nall else rest[k][...]
    c=c0+nc-1-i
    nxt=jnp.minimum(c+1,nall-1)
    start=(first_ref[nxt//(SPAN//Q)]==1)&(nxt%(SPAN//Q)==0)
    @pl.when(start)
    def _():
        ds_ref[...]=jnp.zeros_like(ds_ref); h_ref[...]=jnp.zeros_like(h_ref)
    act=act_ref[...]
    v=act[:,:VW]; bf=act[:,VW:VW+NS]; cf=act[:,VW+NS:]
    b=bf.astype(bf16); cc=cf.astype(bf16)
    z=raw_ref[:,CW:]+par_ref[5:6,:128]
    dt=softplus(z)
    edl=jnp.exp(par_ref[6:7,:128])
    a=-dt*edl
    row,col=iotas()
    low=row>=col; up=row<=col
    cum=tri_sum(jnp.where(low,1.0,0.0).astype(bf16),a)
    last=cum[Q-1:Q,:]
    ee=ee_ref[...]
    sprd=spread(jnp.concatenate([dt,jnp.exp(cum),jnp.exp(last-cum)],axis=0),ee)
    dte,ecum,etail=sprd[:Q],sprd[Q:2*Q],sprd[2*Q:]
    x=v*dte
    xb=x.astype(bf16)
    dy=dy_ref[...].astype(f32)
    dyb=dy.astype(bf16)
    dgt=jnp.zeros((Q,Q),f32)
    parts=[]
    for p in range(VW//128):
        cols=slice(128*p,128*p+128)
        dyh,dyl=split2(dy[:,cols])
        xh,xl=halves2(x[:,cols])
        dw=mm(jnp.concatenate([xh,xl,xh],axis=1),jnp.concatenate([dyh,dyh,dyl],axis=1),1,1)
        for k in (0,1):
            h=2*p+k
            dgt=dgt+lt_ref[:,h*Q:(h+1)*Q]*dw[k*Q:(k+1)*Q]
        parts.append(mm(wt_ref[:,2*Q*p:2*Q*(p+1)],halves(dy[:,cols])))
    ds=ds_ref[...]
    dsb=ds.astype(bf16)
    s=sp_ref[0]
    dxd=jnp.concatenate(parts,axis=1)
    bds=mm(b,dsb)
    dx=dxd+etail*bds
    xe=(x*etail).astype(bf16)
    dye=dy*ecum
    db=mm3(dgt,cf)+mm3(x*etail,ds,1,1)
    dc=mm3(dgt,bf,0,0)+mm3(dye,s,1,1)
    kk=jnp.sum(dsb.astype(f32)*sn_ref[...],axis=0,keepdims=True)
    rh,rl=split2(dyb.astype(f32)*(y_ref[...]-par_ref[7:8,:VW]*v)-xb.astype(f32)*dxd-xe.astype(f32)*bds)
    kh,kl=split2(jnp.concatenate([kk,jnp.zeros((7,VW),f32)],axis=0))
    hs=mm(jnp.concatenate([rh,rl,(v*dx).astype(bf16),jnp.concatenate([kh,kl],axis=0)],axis=0),hh_ref[...])
    dcum,q,k0=hs[:Q]+hs[Q:2*Q],hs[2*Q:3*Q],hs[3*Q:3*Q+1]+hs[3*Q+8:3*Q+9]
    da=k0+tri_sum(jnp.where(up,1.0,0.0).astype(bf16),dcum)
    dst=(q-da*edl)*sig(z)
    ds_ref[...]=ecum[Q-1:Q,:]*ds+mm3(cf,dye,0,0)
    sn_ref[...]=s
    acs_ref[0:1,:]+=jnp.sum(da*a,axis=0,keepdims=True)
    acs_ref[1:2,:]+=jnp.sum(dst,axis=0,keepdims=True)
    dv=dte*dx+par_ref[7:8,:VW]*dy
    acc_ref[5:6,:VW]+=jnp.sum(dy*v,axis=0,keepdims=True)
    dpre=jnp.concatenate([dv,db,dc],axis=1)*sl_ref[...]
    ext[0:Q,:]=dpre
    ext[Q:Q+8,:]=h_ref[...]
    h_ref[...]=dpre[0:8,:]
    xr=raw_ref[:,:CW]
    draw=ck_ref[3:4,:]*dpre
    acc_ref[3:4,:]+=jnp.sum(dpre*xr,axis=0,keepdims=True)
    acc_ref[4:5,:]+=jnp.sum(dpre,axis=0,keepdims=True)
    for j in (1,2,3):
        sh=ext[j:j+Q,:]
        draw=draw+ck_ref[3-j:4-j,:]*sh
        acc_ref[3-j:4-j,:]+=jnp.sum(sh*xr,axis=0,keepdims=True)
    out_ref[:,:CW]=draw.astype(bf16)
    out_ref[:,CW:]=dst.astype(bf16)

def sd(shape,dt=f32): return jax.ShapeDtypeStruct(shape,dt)

def hbm(shape,dt=f32): return pltpu.HBM(shape,dt)

def vmem(shape,dt=f32): return pltpu.VMEM(shape,dt)

def near_by(x): return pltpu.with_memory_space_constraint(x,pltpu.VMEM)

def stay(x): return pltpu.with_memory_space_constraint(x,pltpu.HBM)

def whole(shape): return pl.BlockSpec(shape,lambda i,*_: (0,)*len(shape))

def once(shape): return pl.BlockSpec(shape,lambda i,*_: (0,)*len(shape),pipeline_mode=pl.Buffered(1))

HL=VW//HW

def ssd_fwd(c0,nc,nall,first,raw,par,carry):
    rb=lambda w: pl.BlockSpec((Q,w),lambda i,*_: (c0+i,0))
    any_spec=pl.BlockSpec(memory_space=pl.ANY)
    held=[whole((NS,VW)),whole((8,CW))]
    return pl.pallas_call(partial(fwd_kernel,c0,nc),
        out_shape=(vmem((nall*Q,VW)),hbm((nall*Q,CW)),hbm((nall*Q,CW)),hbm((nall,NS,VW)),hbm((nall*Q,HL*Q),bf16),hbm((nall*Q,HL*Q)),sd((NS,VW)),sd((8,CW))),
        grid_spec=pltpu.PrefetchScalarGridSpec(num_scalar_prefetch=1,grid=(nc,),
            in_specs=[rb(RW),once((8,CW))]+(held+[any_spec]*6 if carry else []),
            out_specs=(rb(VW),rb(CW),rb(CW),pl.BlockSpec((1,NS,VW),lambda i,*_: (c0+i,0,0)),rb(HL*Q),rb(HL*Q),*held),
            scratch_shapes=[pltpu.VMEM((Q+8,CW),f32),pltpu.VMEM((256,VW),bf16)]),
        input_output_aliases={5+k:k for k in range(6)} if carry else {},
        compiler_params=pltpu.CompilerParams(vmem_limit_bytes=FWD_LIMIT),
        cost_estimate=pl.CostEstimate(flops=int(1.5e9*nc/8),bytes_accessed=30_000_000*nc//8,transcendentals=3_000_000*nc//8),
        name=f"ssd_forward_{c0}")(first,stay(raw),par,*(carry[6:]+(near_by(carry[0]),)+tuple(stay(x) for x in carry[1:6]) if carry else ()))

def ssd_bwd(c0,nc,nall,first,raw,act,sl,y,dy,sp,wt,lt,par,carry):
    rv=lambda w: pl.BlockSpec((Q,w),lambda i,*_: (c0+nc-1-i,0))
    any_spec=pl.BlockSpec(memory_space=pl.ANY)
    held=[whole((NS,VW)),whole((NS,VW)),whole((8,CW)),whole((8,CW)),whole((8,128))]
    return pl.pallas_call(partial(bwd_kernel,c0,nc,nall),
        out_shape=(vmem((nall*Q,RW),bf16),hbm((NS,VW)),hbm((NS,VW)),sd((8,CW)),sd((8,CW)),sd((8,128))),
        grid_spec=pltpu.PrefetchScalarGridSpec(num_scalar_prefetch=1,grid=(nc,),
            in_specs=[rv(RW),rv(CW),rv(CW),rv(VW),rv(VW),pl.BlockSpec((1,NS,VW),lambda i,*_: (c0+nc-1-i,0,0)),rv(HL*Q),rv(HL*Q),once((8,CW))]
                     +(held+[any_spec] if carry else []),
            out_specs=(rv(RW),*held),
            scratch_shapes=[pltpu.VMEM((Q+8,CW),f32),pltpu.VMEM((256,VW),bf16),pltpu.VMEM((VW,128),bf16)]),
        input_output_aliases={15:0} if carry else {},
        compiler_params=pltpu.CompilerParams(vmem_limit_bytes=BACK_LIMIT),
        cost_estimate=pl.CostEstimate(flops=int(3e9*nc/8),bytes_accessed=60_000_000*nc//8,transcendentals=4_000_000*nc//8),
        name=f"ssd_backward_{c0}")(first,stay(raw),stay(act),stay(sl),near_by(y),near_by(dy),stay(sp),stay(wt),stay(lt),par,*((stay(carry[1]),stay(carry[2]))+carry[3:]+(near_by(carry[0]),) if carry else ()))


D = 1536
H = 48
E = 3072
TOK_DEV = 1024
SEQ_DEV = 4
EPSILON = 1e-05
FWD_PARTS = ((0, 4), (4, 4))
BACK_PARTS = ((5, 3), (2, 3), (0, 2))


def contract(left, right, left_dim, right_dim, out=f32):
    return lax.dot_general(
        left, right, (((left_dim,), (right_dim,)), ((), ())), preferred_element_type=f32
    ).astype(out)


def span_layout(seq_lengths, seq_device, seq_offset, device):
    span_index = jnp.arange(SEQ_DEV, dtype=jnp.int32)
    needed = (seq_lengths + SPAN - 1) // SPAN
    owned_seq = (seq_device == device) & (seq_lengths > 0)
    relative = span_index[None, :] - seq_offset[:, None]
    inside = owned_seq[:, None] & (relative >= 0) & (relative < needed[:, None])
    live_rows = jnp.sum(
        jnp.where(inside, jnp.clip(seq_lengths[:, None] - relative * SPAN, 0, SPAN), 0), axis=0
    )
    seq_first = jnp.any(inside & (relative == 0), axis=0)
    return live_rows, seq_first.astype(jnp.int32)


def ring_order(count):
    if count == 8:
        return [0, 2, 4, 6, 7, 5, 3, 1]
    return list(range(count))


def lay(cols, rows, off_ref, refs, out):
    for k, (c0, w) in enumerate(cols):
        out[pl.ds(pl.multiple_of(off_ref[k] * rows, 16), rows), c0 : c0 + w] = refs[k][...]


def row_sums(x):
    a, b = split2(x)
    ones = jnp.ones((8, x.shape[1]), bf16)
    return mm(ones, a, 1, 1) + mm(ones, b, 1, 1)


def project_kernel(cols, rows, nx, off_ref, *refs):
    n = len(cols)
    xs = refs[n : n + nx]
    w_ref, x_ref, xt_ref, raw_ref = refs[n + nx :]
    i = pl.program_id(0)

    @pl.when(i == 0)
    def _():
        lay(cols, rows, off_ref, refs, w_ref)

    for k in range(nx):

        @pl.when(i == k)
        def _(k=k):
            x_ref[...] = xs[k][...]

    xt_ref[...] = x_ref[...].T
    raw_ref[...] = mm(x_ref[...], w_ref[...])


def project(pieces, offsets, xs, total):
    rows, n = pieces[0][0].shape[0], len(pieces)
    cols = [(c0, x.shape[1]) for x, c0 in pieces]
    width = max(c0 + w for c0, w in cols)
    q, depth = xs[0].shape
    nx = len(xs)
    at = lambda w: pl.BlockSpec((q, w), lambda i, off: (off[n + i], 0))
    return pl.pallas_call(
        partial(project_kernel, cols, rows, nx),
        out_shape=(hbm((total, width), bf16), sd((q * nx, depth), bf16), sd((depth, q * nx), bf16), hbm((q * nx, width))),
        grid_spec=pltpu.PrefetchScalarGridSpec(
            num_scalar_prefetch=1,
            grid=(nx,),
            in_specs=[once(x.shape) for x, _ in pieces] + [once(x.shape) for x in xs],
            out_specs=(whole((total, width)), at(depth), pl.BlockSpec((depth, q), lambda i, off: (0, off[n + i])), at(width)),
        ),
        compiler_params=pltpu.CompilerParams(vmem_limit_bytes=22 << 20),
        cost_estimate=pl.CostEstimate(flops=2 * q * nx * total * width, bytes_accessed=30_000_000, transcendentals=0),
        name="project",
    )(offsets, *[x for x, _ in pieces], *xs)


def cotangent_kernel(cols, rows, nx, off_ref, *refs):
    n = len(cols)
    xs = refs[n : n + nx]
    normed_ref, ssd_ref, gain_ref, w_ref, gr_ref, by_ref, sum_ref, yr_ref, x_ref = refs[n + nx :]
    i = pl.program_id(0)

    @pl.when(i == 0)
    def _():
        lay(cols, rows, off_ref, refs, w_ref)

    for k in range(nx):

        @pl.when(i == k)
        def _(k=k):
            x_ref[...] = xs[k][...]

    by = mm(x_ref[...], w_ref[:, VW:])
    gr = mm(normed_ref[...], w_ref[:, :VW])
    by_ref[...] = by
    gr_ref[...] = gr
    gated = ssd_ref[...] * (gr * sig(gr))
    scaled = gated * gain_ref[...]
    yr_ref[...] = scaled.astype(bf16)
    square = row_sums(gated * gated)
    cross = row_sums(by * scaled)
    top = lax.broadcasted_iota(jnp.int32, square.shape, 0) == 0
    sum_ref[0] = jnp.where(top, square, cross)


def cotangent(pieces, offsets, xs, normed, ssd, gain, total):
    rows, n = pieces[0][0].shape[0], len(pieces)
    cols = [(c0, x.shape[1]) for x, c0 in pieces]
    width = max(c0 + w for c0, w in cols)
    q, depth = xs[0].shape
    nx = len(xs)
    at = lambda w: pl.BlockSpec((q, w), lambda i, off: (off[n + i], 0))
    return pl.pallas_call(
        partial(cotangent_kernel, cols, rows, nx),
        out_shape=(
            vmem((total, width), bf16),
            sd((q * nx, VW)),
            sd((q * nx, VW)),
            sd((nx, 8, q)),
            sd((q * nx, VW), bf16),
        ),
        grid_spec=pltpu.PrefetchScalarGridSpec(
            num_scalar_prefetch=1,
            grid=(nx,),
            in_specs=[once(x.shape) for x, _ in pieces]
            + [once(x.shape) for x in xs]
            + [at(depth), at(VW), once((1, VW))],
            out_specs=(
                whole((total, width)),
                at(VW),
                at(VW),
                pl.BlockSpec((1, 8, q), lambda i, off: (off[n + i], 0, 0)),
                at(VW),
            ),
            scratch_shapes=[pltpu.VMEM((q, depth), bf16)],
        ),
        compiler_params=pltpu.CompilerParams(vmem_limit_bytes=30 << 20),
        cost_estimate=pl.CostEstimate(flops=2 * q * nx * total * width, bytes_accessed=30_000_000, transcendentals=800_000),
        name="cotangent",
    )(offsets, *[x for x, _ in pieces], *xs, normed, near_by(ssd), gain)


def turn_kernel(nx, off_ref, *refs):
    i = pl.program_id(0)
    for k in range(nx):

        @pl.when(i == k)
        def _(k=k):
            refs[nx][...] = refs[k][...].T


def turn(offsets, xs):
    q, depth = xs[0].shape
    nx = len(xs)
    n = offsets.shape[0] - nx
    return pl.pallas_call(
        partial(turn_kernel, nx),
        out_shape=sd((depth, q * nx), bf16),
        grid_spec=pltpu.PrefetchScalarGridSpec(
            num_scalar_prefetch=1,
            grid=(nx,),
            in_specs=[once(x.shape) for x in xs],
            out_specs=pl.BlockSpec((depth, q), lambda i, off: (0, off[n + i])),
        ),
        compiler_params=pltpu.CompilerParams(vmem_limit_bytes=8 << 20),
        cost_estimate=pl.CostEstimate(flops=0, bytes_accessed=10_000_000, transcendentals=0),
        name="turn",
    )(offsets, *xs)


def gate_kernel(sum_ref, by_ref, gr_ref, ssd_ref, gain_ref, ny_ref, bg_ref, dy_ref, gg_ref):
    @pl.when(pl.program_id(0) == 0)
    def _():
        gg_ref[...] = jnp.zeros_like(gg_ref)

    sums = sum_ref[0].T
    inv = lax.rsqrt(sums[:, 0:1] / E + EPSILON)
    gr, ssd, by, gain = gr_ref[...], ssd_ref[...], by_ref[...], gain_ref[...]
    sg = sig(gr)
    gate = gr * sg
    unit = ssd * gate * inv
    ny_ref[...] = (unit * gain).astype(bf16)
    gg_ref[0:1, :] += jnp.sum(by * unit, axis=0, keepdims=True)
    back = inv * (by * gain - unit * (inv * sums[:, 1:2] / E))
    bg_ref[...] = (back * ssd * (sg * (1.0 + gr - gate))).astype(bf16)
    dy_ref[...] = back * gate


def gate_back(sums, by, gate_raw, ssd, gain):
    t, width = by.shape
    n, _, q = sums.shape
    rb = pl.BlockSpec((q, width), lambda i: (i, 0))
    return pl.pallas_call(
        gate_kernel,
        out_shape=(sd((t, width), bf16), sd((t, width), bf16), vmem((t, width)), sd((8, width))),
        grid=(n,),
        in_specs=[pl.BlockSpec((1, 8, q), lambda i: (i, 0, 0)), rb, rb, rb, once((1, width))],
        out_specs=(rb, rb, rb, whole((8, width))),
        compiler_params=pltpu.CompilerParams(vmem_limit_bytes=12 << 20),
        cost_estimate=pl.CostEstimate(flops=20_000_000, bytes_accessed=15_000_000, transcendentals=800_000),
        name="gate_back",
    )(sums, by, gate_raw, near_by(ssd), gain)


def normed_kernel(
    half, at_ref, first_ref, gate_ref, w_ref, g_ref, x_ref, h_ref, m_ref, s_ref, mk_ref, mn_ref, ma_ref, mb_ref, away_ref, keep_ref, ng_ref, o_ref, scale_ref
):
    i = pl.program_id(0)

    @pl.when(i == 0)
    def _():
        ng_ref[...] = jnp.zeros_like(ng_ref)
        inv = lax.rsqrt(s_ref[0, 0:1, :] / E + EPSILON) * m_ref[...]
        scale_ref[...] = jnp.broadcast_to(inv, (8, inv.shape[1])).T

    n = o_ref.shape[0]
    scale = scale_ref[pl.ds(pl.multiple_of(i * n, 8), n), 0:1]
    far = jnp.where(i < half, ma_ref[...].astype(f32), mb_ref[...].astype(f32))
    mixed = mk_ref[0].astype(f32) + mn_ref[0].astype(f32) + far
    o_ref[...] = h_ref[...] + scale * mixed
    back = mm(first_ref[...], w_ref[...], 1, 1) + mm(gate_ref[...], g_ref[...], 1, 1)
    ng_ref[0:1, :] += jnp.sum(back * x_ref[...].astype(f32), axis=0, keepdims=True)

    @pl.when(i < half)
    def _():
        away_ref[0] = back.astype(bf16)

    @pl.when(i >= half)
    def _():
        keep_ref[0] = back.astype(bf16)


def back_normed_rows(at, q, first, gate, w, gate_w, normed, hidden, mask, sums, keep, near, far):
    depth = normed.shape[1]
    n = at.shape[0]
    half = n // 2
    rb = lambda c: pl.BlockSpec((q, c), lambda i, at: (at[i], 0))
    part = lambda c: pl.BlockSpec((q // n, c), lambda i, at: (i, 0))
    second = pl.BlockSpec((1, q // n, depth), lambda i, at: (1, i, 0))
    return pl.pallas_call(
        partial(normed_kernel, half),
        out_shape=(sd((half, q, depth), bf16), sd((half, q, depth), bf16), sd((8, depth)), sd((q, depth))),
        grid_spec=pltpu.PrefetchScalarGridSpec(
            num_scalar_prefetch=1,
            grid=(n,),
            in_specs=[rb(RW), rb(VW), once(w.shape), once((depth, VW)), rb(depth)]
            + [part(depth), whole((1, q)), pl.BlockSpec((1, 8, q), lambda i, at: (at[n - 1], 0, 0)), second, second]
            + [
                pl.BlockSpec((q // n, depth), lambda i, at: (jnp.minimum(i, half - 1), 0)),
                pl.BlockSpec((q // n, depth), lambda i, at: (jnp.maximum(i - half, 0), 0)),
            ],
            out_specs=(
                pl.BlockSpec((1, q, depth), lambda i, at: (jnp.minimum(i, half - 1), 0, 0)),
                pl.BlockSpec((1, q, depth), lambda i, at: (jnp.maximum(i - half, 0), 0, 0)),
                whole((8, depth)),
                part(depth),
            ),
            scratch_shapes=[pltpu.VMEM((q, 8), f32)],
        ),
        compiler_params=pltpu.CompilerParams(vmem_limit_bytes=22 << 20),
        cost_estimate=pl.CostEstimate(flops=2 * n * q * depth * (RW + VW), bytes_accessed=60_000_000, transcendentals=0),
        name="back_normed",
    )(at, near_by(first), gate, w, near_by(gate_w), normed, hidden, mask, sums, keep, near, *far)


def mixer_kernel(half, at_ref, x_ref, w_ref, away_ref, keep_ref):
    r = mm(x_ref[...], w_ref[...], 1, 1).astype(bf16)
    i = pl.program_id(0)

    @pl.when(i < half)
    def _():
        away_ref[0] = r

    @pl.when(i >= half)
    def _():
        keep_ref[0] = r


def mixer_blocks(at, q, x, w):
    n, depth, width = at.shape[0], w.shape[0], x.shape[1]
    half = n // 2
    return pl.pallas_call(
        partial(mixer_kernel, half),
        out_shape=(sd((half, q, depth), bf16), sd((half, q, depth), bf16)),
        grid_spec=pltpu.PrefetchScalarGridSpec(
            num_scalar_prefetch=1,
            grid=(n,),
            in_specs=[
                pl.BlockSpec((q, width), lambda i, at: (at[i], 0)),
                pl.BlockSpec((depth, width), lambda i, at: (0, 1), pipeline_mode=pl.Buffered(1)),
            ],
            out_specs=(
                pl.BlockSpec((1, q, depth), lambda i, at: (jnp.minimum(i, half - 1), 0, 0)),
                pl.BlockSpec((1, q, depth), lambda i, at: (jnp.maximum(i - half, 0), 0, 0)),
            ),
        ),
        compiler_params=pltpu.CompilerParams(vmem_limit_bytes=12 << 20),
        cost_estimate=pl.CostEstimate(flops=2 * n * q * depth * width, bytes_accessed=20_000_000, transcendentals=0),
        name="mixer_rows",
    )(at, x, near_by(w))


def grad_kernel(per, rows, at_ref, xt_ref, back_ref, out_ref):
    i = pl.program_id(0)
    r = mm(xt_ref[...], back_ref[...]).astype(bf16)
    for d in range(per):
        out_ref[pl.ds(at_ref[i * per + d], 1)] = r[d * rows : (d + 1) * rows][None]


def weight_grad(at, xt, back, n_dp):
    depth, t = xt.shape
    rows, width = depth // n_dp, back.shape[1]
    steps = 2
    return pl.pallas_call(
        partial(grad_kernel, n_dp // steps, rows),
        out_shape=sd((n_dp, rows, width), bf16),
        grid_spec=pltpu.PrefetchScalarGridSpec(
            num_scalar_prefetch=1,
            grid=(steps,),
            in_specs=[pl.BlockSpec((depth // steps, t), lambda i, at: (i, 0)), once(back.shape)],
            out_specs=whole((n_dp, rows, width)),
        ),
        compiler_params=pltpu.CompilerParams(vmem_limit_bytes=20 << 20),
        cost_estimate=pl.CostEstimate(flops=2 * depth * t * width, bytes_accessed=8_000_000, transcendentals=0),
        name="weight_grad",
    )(at, xt, near_by(back))


def far_pair_kernel(at_ref, xt_ref, back_ref, zt_ref, y_ref, f_ref, b_ref):
    f_ref[...] = mm(xt_ref[...], back_ref[...]).astype(bf16)
    b_ref[...] = mm(zt_ref[...], y_ref[...]).astype(bf16)


def far_value_kernel(mid, at_ref, xt_ref, back_ref, f_ref, b_ref):
    r = mm(xt_ref[...], back_ref[...]).astype(bf16)
    f_ref[...] = r[:, :mid]
    b_ref[...] = r[:, mid:]


def far_grad(at, rows, pairs, mid=0):
    depth, t = pairs[0][0].shape
    block = pl.BlockSpec((rows, t), lambda i, at: (at[0], 0))
    specs, args = [], []
    for xt, back in pairs:
        specs += [block, once(back.shape)]
        args += [xt, back]
    widths = (mid, pairs[0][1].shape[1] - mid) if mid else tuple(b.shape[1] for _, b in pairs)
    return pl.pallas_call(
        partial(far_value_kernel, mid) if mid else far_pair_kernel,
        out_shape=tuple(sd((rows, w), bf16) for w in widths),
        grid_spec=pltpu.PrefetchScalarGridSpec(
            num_scalar_prefetch=1,
            grid=(1,),
            in_specs=specs,
            out_specs=tuple(whole((rows, w)) for w in widths),
        ),
        compiler_params=pltpu.CompilerParams(vmem_limit_bytes=12 << 20),
        cost_estimate=pl.CostEstimate(flops=2 * rows * t * sum(widths), bytes_accessed=4_000_000, transcendentals=0),
        name="far_grad",
    )(at, *args)


def pair_grad_kernel(per, rows, at_ref, xt_ref, back_ref, zt_ref, y_ref, out_ref):
    i = pl.program_id(0)
    for k, r in enumerate((mm(xt_ref[...], back_ref[...]), mm(zt_ref[...], y_ref[...]))):
        r = r.astype(bf16)
        for d in range(per):
            out_ref[pl.ds(at_ref[i * per + d], 1), :, k * VW : (k + 1) * VW] = r[d * rows : (d + 1) * rows][None]


def pair_grad(at, xt, back, zt, y, n_dp):
    depth, t = xt.shape
    rows, steps = depth // n_dp, 4
    rb = pl.BlockSpec((depth // steps, t), lambda i, at: (i, 0))
    return pl.pallas_call(
        partial(pair_grad_kernel, n_dp // steps, rows),
        out_shape=sd((n_dp, rows, 2 * VW), bf16),
        grid_spec=pltpu.PrefetchScalarGridSpec(
            num_scalar_prefetch=1,
            grid=(steps,),
            in_specs=[rb, once(back.shape), rb, once(y.shape)],
            out_specs=whole((n_dp, rows, 2 * VW)),
        ),
        compiler_params=pltpu.CompilerParams(vmem_limit_bytes=22 << 20),
        cost_estimate=pl.CostEstimate(flops=4 * depth * t * VW, bytes_accessed=14_000_000, transcendentals=0),
        name="pair_grad",
    )(at, xt, back, zt, y)


def finish_kernel(x_ref, f_ref, b_ref, g_ref, small_ref, gv_ref, rest_ref, taps_ref, bias_ref, gain_ref, step_ref, decay_ref):
    value = x_ref[...].astype(f32) + f_ref[...].astype(f32) + b_ref[...].astype(f32)
    gv_ref[:, 0, :] = g_ref[...]
    gv_ref[:, 1, :] = value[:, :VW]
    rest_ref[...] = value[:, VW:]
    taps_ref[...] = small_ref[0:8, :VW].T[:, :4]
    bias_ref[...] = small_ref[4:5, :VW]
    gain_ref[...] = small_ref[6:7, :VW]
    heads = step_ref.shape[1]
    decay_ref[...] = small_ref[6:7, VW : VW + heads]
    step_ref[...] = small_ref[6:7, VW + 128 : VW + 128 + heads]


def finish(x, f, b, pair_out, small, heads):
    rows, width = x.shape
    full = whole((rows, width))
    outs = ((rows, 2, VW), (rows, width - VW), (VW, 4), (1, VW), (1, VW), (1, heads), (1, heads))
    return pl.pallas_call(
        finish_kernel,
        out_shape=tuple(sd(o) for o in outs),
        grid=(1,),
        in_specs=[full, full, full, pl.BlockSpec((rows, VW), lambda i: (0, 0)), whole(small.shape)],
        out_specs=tuple(whole(o) for o in outs),
        compiler_params=pltpu.CompilerParams(vmem_limit_bytes=16 << 20),
        cost_estimate=pl.CostEstimate(flops=1_000_000, bytes_accessed=5_000_000, transcendentals=0),
        name="finish",
    )(x, f, b, pair_out, small)


class Ring:
    def __init__(self, count):
        self.count = count
        self.half = count // 2
        self.order = ring_order(count)
        at = {d: i for i, d in enumerate(self.order)}
        self.table = [[self.order[(at[d] + k) % count] for k in range(count)] for d in range(count)]
        self.ahead = [(self.order[i], self.order[(i + 1) % count]) for i in range(count)]
        self.back = [(b, a) for a, b in self.ahead]

    def rows_of(self, table):
        return jnp.asarray(table, jnp.int32)[lax.axis_index("dp")]

    def hop(self, f, b):
        return lax.ppermute(f, "dp", self.ahead), lax.ppermute(b, "dp", self.back)


class Gather:
    def __init__(self, ring, x, c0=0):
        self.ring, self.mid, self.c0 = ring, x.shape[1] // 2 // 128 * 128, c0
        self.pieces, self.f, self.b, self.s = [(x, c0)], x, x, 0

    def ready(self):
        if self.s == self.ring.half - 1:
            return [self.f[:, : self.mid], self.b[:, self.mid :]]
        return [self.f, self.b]

    def step(self, f, b):
        self.s += 1
        self.f, self.b = self.ring.hop(f, b)
        self.pieces += [(self.f, self.c0), (self.b, self.c0 + (self.mid if self.s == self.ring.half else 0))]

    @staticmethod
    def offsets(ring):
        ahead = [0]
        for s in range(1, ring.half + 1):
            ahead += [ring.count - s, s]
        return [[ring.table[d][k] for k in ahead] for d in range(ring.count)]


class Scatter:
    def __init__(self, ring, first):
        self.ring, self.first, self.x, self.s = ring, list(first), None, ring.half

    def ready(self):
        x, s = self.x, self.s
        if s == self.ring.half:
            return self.first
        f, b = self.f, self.b
        if s == self.ring.half - 1:
            f = jnp.pad(f, ((0, 0), (0, x.shape[2] - f.shape[1])))
            b = jnp.pad(b, ((0, 0), (x.shape[2] - b.shape[1], 0)))
        f = x[s].astype(f32) + f.astype(f32)
        b = x[self.ring.count - s].astype(f32) + b.astype(f32)
        return [f.astype(bf16), b.astype(bf16)]

    def step(self, f, b):
        self.f, self.b = self.ring.hop(f, b)
        self.s -= 1

    def total(self, columns=slice(None)):
        return self.x[0, :, columns].astype(f32) + self.f[:, columns].astype(f32) + self.b[:, columns].astype(f32)


def swap(x, axis, count, bits):
    return lax.ppermute(x, axis, [(i, i ^ bits) for i in range(count)])


def tensor_order(count):
    keys = [0]
    bit = count // 2
    while bit:
        keys += [k ^ bit for k in keys]
        bit //= 2
    return keys


def pick(x, index, axis=0):
    return lax.dynamic_index_in_dim(x, index, axis, keepdims=False)


def groups_of(count):
    bits = [1 << k for k in range(count.bit_length() - 1)]
    first = len(bits) % 2
    return ([bits[:first]] if first else []) + [bits[k : k + 2] for k in range(first, len(bits), 2)]


def others(bits):
    return [bits[0]] if len(bits) == 1 else [bits[0], bits[1], bits[0] | bits[1]]


class Spread:
    def __init__(self, x, axis, count):
        self.x, self.axis, self.count, self.groups = x, axis, count, groups_of(count)

    def step(self, x):
        bits = self.groups.pop(0)
        self.x = sum((swap(x, self.axis, self.count, k) for k in others(bits)), x)


def together(*lists):
    flat = lax.optimization_barrier(tuple(x for xs in lists for x in xs))
    out, at = [], 0
    for xs in lists:
        out.append(list(flat[at : at + len(xs)]))
        at += len(xs)
    return out


def body(
    n_dp,
    n_tensor,
    hidden_in,
    norm_gain,
    gate_value_weight,
    state_proj_weight,
    step_weight,
    conv_value_kernel,
    conv_value_bias,
    conv_state_kernel,
    conv_state_bias,
    step_bias,
    decay_log,
    skip_scale,
    gate_norm_gain,
    out_weight,
    out_cotangent,
    seq_lengths,
    seq_device,
    seq_offset,
):
    quarter = hidden_in.shape[0]
    heads = step_weight.shape[1]
    rows = gate_value_weight.shape[0]
    me, dp = lax.axis_index("tensor"), lax.axis_index("dp")
    ring = Ring(n_dp)
    ring_at = ring.rows_of([[ring.table[d].index(k) for k in range(n_dp)] for d in range(n_dp)])
    far_at = ring.rows_of([[ring.table[d][ring.half]] for d in range(n_dp)])
    order = me ^ jnp.asarray([3, 1, 2, 0], jnp.int32)
    offsets = jnp.concatenate([ring.rows_of(Gather.offsets(ring)), me ^ jnp.asarray(tensor_order(n_tensor), jnp.int32)])
    to_core = lambda x: swap(x, "tensor", n_tensor, 1)
    to_far = lambda x: swap(x, "tensor", n_tensor, 2)

    live_rows, seq_first = span_layout(seq_lengths, seq_device, seq_offset, dp)
    row = me * quarter + jnp.arange(quarter, dtype=jnp.int32)
    local_live = jnp.sum(
        jnp.where((row // SPAN)[:, None] == jnp.arange(SEQ_DEV)[None, :], live_rows[None, :], 0), axis=1
    )
    local_mask = (row % SPAN < local_live).astype(f32)

    pad_to = lambda x, w: jnp.pad(x, (0, w - x.shape[0]))[None]
    params = jnp.concatenate(
        [
            jnp.concatenate([conv_value_kernel, conv_state_kernel], axis=0).T,
            jnp.concatenate([conv_value_bias, conv_state_bias])[None],
            pad_to(step_bias, CW),
            pad_to(decay_log, CW),
            pad_to(jnp.repeat(skip_scale, HW), CW),
        ],
        axis=0,
    )
    gain = gate_norm_gain[None]
    zeros = lambda *s: jnp.zeros(s, f32)

    first_own = jnp.concatenate(
        [gate_value_weight[:, 1, :], state_proj_weight, jnp.pad(step_weight, ((0, 0), (0, 128 - heads)))], axis=1
    )
    first_own, hidden = lax.optimization_barrier((first_own, hidden_in))
    inv_rms = lax.rsqrt(jnp.mean(hidden * hidden, axis=-1) + EPSILON)
    scaled = hidden * inv_rms[:, None]
    normed_local = (scaled * norm_gain[None, :]).astype(bf16)
    first = Gather(ring, first_own)
    first.step(*first.ready())
    far = to_far(normed_local)
    out_own = jnp.concatenate([gate_value_weight[:, 0, :], out_weight], axis=1)
    back_local = (local_mask[:, None] * out_cotangent).astype(bf16)
    (out_own, offsets, ring_at, far_at, order, seq_first, params, back_local) = lax.optimization_barrier(
        (out_own, offsets, ring_at, far_at, order, seq_first, params, back_local)
    )
    out = Gather(ring, out_own)
    for s in range(1, ring.half):
        extra = []
        if s == min(2, ring.half - 1):
            extra = [[normed_local, far]]
        elif s == ring.half - 1:
            extra = [[back_local] + normed_parts[2:]]
        sends = together(first.ready(), *extra)
        first.step(*sends.pop(0))
        if s == min(2, ring.half - 1):
            [a, far] = sends.pop(0)
            normed_parts = [a, far, to_core(a), to_core(far)]
        elif s == ring.half - 1:
            [back_local, *normed_parts[2:]] = sends.pop(0)
            back_far = to_far(back_local)
    ps, os = together([x for x, _ in first.pieces] + normed_parts, out.ready())
    out.step(*os)
    n = len(first.pieces)
    first_w, normed, normed_t, raw = project(
        [(x, c0) for x, (_, c0) in zip(ps, first.pieces)], offsets, ps[n:], D
    )
    chunks = TOK_DEV // Q
    carry = ()
    for k, (c0, n) in enumerate(FWD_PARTS):
        held, os, bs = together([carry[6]] if carry else [raw], out.ready(), [back_local, back_far] if k == 0 else [])
        out.step(*os)
        if k:
            carry = carry[:6] + (held[0],) + carry[7:]
        else:
            raw = held[0]
            back_parts = bs + [to_core(x) for x in bs]
        carry = tuple(ssd_fwd(c0, n, chunks, seq_first, raw, params, carry))
    held, os, back_parts = together([carry[0]], out.ready(), back_parts)
    carry = (held[0],) + carry[1:]
    out.step(*os)
    back_t = turn(offsets, back_parts)
    while out.s < ring.half:
        out.step(*out.ready())
    ssd, act, slope, states, weights_t, decays_t = carry[:6]

    out_w, gate_raw, back_y, sums, gated = cotangent(
        out.pieces, offsets, back_parts, normed, ssd, gain, D
    )
    total = Spread(sums, "tensor", n_tensor)
    while total.groups:
        total.step(total.x)
    sums = total.x
    mixer = mixer_blocks(order, quarter, gated, out_w)
    sums, mixer_away, mixer_keep = lax.optimization_barrier((sums, *mixer))
    normed_y, back_gate, back_ssd, gain_grad = gate_back(sums, back_y, gate_raw, ssd, gain)
    pair_sum = Scatter(ring, far_grad(far_at, rows, [(normed_t, back_gate), (back_t, normed_y)]))
    ps, [away, mixer_keep, back_gate, normed_y] = together(
        pair_sum.ready(), [mixer_away, mixer_keep, back_gate, normed_y]
    )
    pair_sum.step(*ps)
    mixer_near = to_core(away)
    pair_sum.x = pair_grad(ring_at, normed_t, back_gate, back_t, normed_y, n_dp)
    [pair_sum.f, pair_sum.b, pair_sum.x, mixer_near], = together([pair_sum.f, pair_sum.b, pair_sum.x, mixer_near])

    half_rows = quarter // 2
    away = (mixer_keep[0].astype(f32) + mixer_near[0].astype(f32)).astype(bf16)
    away = [away[:half_rows], away[half_rows:]]
    carry, held, mixer_far = (), [back_ssd], []
    for k, (c0, n) in enumerate(BACK_PARTS):
        ps = pair_sum.ready() if pair_sum.s else []
        held, ps, ms = together(held, ps, away[k : k + 1])
        if carry:
            carry = carry[:1] + (held[0],) + carry[2:]
        else:
            back_ssd = held[0]
        if pair_sum.s:
            pair_sum.step(*ps)
        ms = [to_far(x) for x in ms]
        carry = tuple(
            ssd_bwd(
                c0, n, chunks, seq_first, raw, act, slope, ssd, back_ssd, states, weights_t, decays_t, params, carry
            )
        )
        last = k == len(BACK_PARTS) - 1
        held, [pair_sum.f, pair_sum.b], ms = together([carry[0 if last else 1]], [pair_sum.f, pair_sum.b], ms)
        mixer_far += ms
    carry = (held[0],) + carry[1:]
    while pair_sum.s:
        pair_sum.step(*pair_sum.ready())
    back_first, _, _, _, acc, acs = carry
    value_sum = Scatter(ring, far_grad(far_at, rows, [(normed_t, back_first)], RW // 2 // 128 * 128))
    vs, [back_first] = together(value_sum.ready(), [back_first])
    value_sum.step(*vs)
    value_sum.x = weight_grad(ring_at, normed_t, back_first, n_dp)
    [value_sum.f, value_sum.b, value_sum.x, back_first], = together(
        [value_sum.f, value_sum.b, value_sum.x, back_first]
    )
    vs, [back_first] = together(value_sum.ready(), [back_first])
    value_sum.step(*vs)
    away, keep, ng, output = back_normed_rows(
        order, quarter, back_first, back_gate, first_w, out_w, normed, hidden_in, local_mask[None], sums, mixer_keep, mixer_near, mixer_far
    )
    [value_sum.f, value_sum.b, away, keep, ng], = together([value_sum.f, value_sum.b, away, keep, ng])
    shared = jnp.concatenate([acc[:5, VW:], (ng[0] / norm_gain).reshape(6, 256), zeros(5, 256)], axis=0)
    shared = Spread(shared, "tensor", n_tensor)
    vs, cs, ps = together(value_sum.ready(), [away], [shared.x])
    value_sum.step(*vs)
    near = to_core(cs[0])
    away = (keep[0].astype(f32) + near[0].astype(f32)).astype(bf16)
    got = to_far(away[:half_rows])
    shared.step(ps[0])
    [value_sum.f, value_sum.b, near, away, got, shared.x], = together(
        [value_sum.f, value_sum.b, near, away, got, shared.x]
    )
    own = jnp.concatenate(
        [acc[:6], jnp.concatenate([gain_grad[0], acs[0], acs[1]])[None], zeros(1, CW)], axis=0
    )
    while shared.groups:
        shared.step(shared.x)
    small = Spread(jnp.concatenate([own, shared.x.reshape(4, CW)], axis=0), "dp", n_dp)
    vs, cs, ps = together(value_sum.ready(), [away[half_rows:]], [small.x])
    value_sum.step(*vs)
    cs = [got, to_far(cs[0])]
    small.step(ps[0])
    while value_sum.s:
        value_sum.step(*value_sum.ready())
    [value_sum.f, value_sum.b, small.x], cs = together([value_sum.f, value_sum.b, small.x], cs)
    state_grad = value_sum.total(slice(VW, CW)).reshape(n_tensor, rows // n_tensor, 2 * NS)
    ps, ss = together([small.x], [pick(state_grad, me ^ k) for k in range(n_tensor)])
    state_out = sum((swap(ss[k], "tensor", n_tensor, k) for k in range(1, n_tensor)), ss[0])
    small.x = ps[0]
    while small.groups:
        small.step(small.x)
    small = small.x
    pair_out = pair_sum.total()
    gv_out, rest, taps, bias, gains, steps, decays = finish(
        value_sum.x[0], value_sum.f, value_sum.b, pair_out, small, heads
    )
    back_rows = keep[1].astype(f32) + near[1].astype(f32) + jnp.concatenate(cs, axis=0).astype(f32)
    back_scaled = back_rows * norm_gain[None, :]
    hidden_gradient = out_cotangent + inv_rms[:, None] * (
        back_scaled - scaled * jnp.mean(back_scaled * scaled, axis=-1)[:, None]
    )
    shared = small[8:].reshape(16, 256)
    index = dp * n_tensor + me
    all_count = n_dp * n_tensor
    kern_share = 2 * NS // all_count
    state_kernel_out = lax.dynamic_slice(shared, (0, index * kern_share), (5, kern_share))
    norm_out = lax.dynamic_slice(shared[5:11].reshape(D), (index * (D // all_count),), (D // all_count,))
    return (
        output,
        hidden_gradient,
        norm_out,
        gv_out,
        state_out,
        rest[:, 2 * NS : 2 * NS + heads],
        taps,
        bias.reshape(VW),
        state_kernel_out[:4].T,
        state_kernel_out[4],
        steps.reshape(heads),
        decays.reshape(heads),
        jnp.sum(small[5, :VW].reshape(heads, HW), axis=1),
        gains.reshape(VW),
        pair_out[:, VW:],
    )


def solution(mesh):
    in_specs = (
        P(("dp", "tensor"), None),
        P(),
        P("dp", None, "tensor"),
        P("dp", None),
        P("dp", "tensor"),
        P("tensor", None),
        P("tensor"),
        P(),
        P(),
        P("tensor"),
        P("tensor"),
        P("tensor"),
        P("tensor"),
        P("dp", "tensor"),
        P(("dp", "tensor"), None),
        P(),
        P(),
        P(),
    )
    out_specs = (
        P(("dp", "tensor"), None),
        P(("dp", "tensor"), None),
        P(("dp", "tensor")),
        P("dp", None, "tensor"),
        P(("dp", "tensor"), None),
        P("dp", "tensor"),
        P("tensor", None),
        P("tensor"),
        P(("dp", "tensor"), None),
        P(("dp", "tensor")),
        P("tensor"),
        P("tensor"),
        P("tensor"),
        P("tensor"),
        P("dp", "tensor"),
    )
    return jax.shard_map(
        partial(body, mesh.shape["dp"], mesh.shape["tensor"]),
        mesh=mesh,
        in_specs=in_specs,
        out_specs=out_specs,
        check_vma=False,
    )
```

```python
from functools import partial

import jax, jax.numpy as jnp
from jax import lax
from jax.experimental import pallas as pl
from jax.experimental.pallas import tpu as pltpu
from jax.sharding import PartitionSpec as P
f32=jnp.float32; bf16=jnp.bfloat16
Q=128
NS=128
VW=768
HW=64
CW=1024
RW=1152
SPAN=256
FWD_LIMIT=14<<20
BACK_LIMIT=18<<20
NEG=-1e30

def mm(a,b,ca=1,cb=0):
    return lax.dot_general(a,b,(((ca,),(cb,)),((),())),preferred_element_type=f32)

def split2(x):
    hi=x.astype(bf16); return hi,(x-hi.astype(f32)).astype(bf16)

def split3(x):
    hi=x.astype(bf16); r=x-hi.astype(f32); mid=r.astype(bf16); return hi,mid,(r-mid.astype(f32)).astype(bf16)

def mm3(a,b,ca=1,cb=0):
    ah,al=split2(a); bh,bl=split2(b)
    return mm(jnp.concatenate([ah,ah,al],axis=ca),jnp.concatenate([bh,bl,bh],axis=cb),ca,cb)

def tri_sum(tri,x):
    a,b,c=split3(x); w=x.shape[1]
    p=mm(tri,jnp.concatenate([a,b,c],axis=1))
    return p[:,:w]+p[:,w:2*w]+p[:,2*w:]

def spread(x,ee):
    a,b=split2(x)
    return mm(jnp.concatenate([a,b],axis=1),ee)

def iotas():
    return lax.broadcasted_iota(jnp.int32,(Q,Q),0),lax.broadcasted_iota(jnp.int32,(Q,Q),1)

def softplus(z):
    return jnp.maximum(z,0.0)+jnp.log(1.0+jnp.exp(-jnp.abs(z)))

def sig(z):
    return 1.0/(1.0+jnp.exp(-z))

def halves(x):
    lane=lax.broadcasted_iota(jnp.int32,x.shape,1)
    lo=jnp.where(lane<HW,x,0.0); hi=jnp.where(lane<HW,0.0,x)
    return jnp.concatenate([lo.astype(bf16),hi.astype(bf16)],axis=0)

def spread_matrix(shape):
    r=lax.broadcasted_iota(jnp.int32,shape,0)%128; c=lax.broadcasted_iota(jnp.int32,shape,1)//HW
    return jnp.where(r==c,1.0,0.0).astype(bf16)

def sum_matrix(shape):
    r=lax.broadcasted_iota(jnp.int32,shape,0)%VW//HW; c=lax.broadcasted_iota(jnp.int32,shape,1)
    return jnp.where(r==c,1.0,0.0).astype(bf16)

def halves2(x):
    lane=lax.broadcasted_iota(jnp.int32,x.shape,1)
    h,l=split2(jnp.concatenate([jnp.where(lane<HW,x,0.0),jnp.where(lane<HW,0.0,x)],axis=0))
    return h,l

def fwd_kernel(c0,nc,first_ref,raw_ref,par_ref,*rest):
    y_ref,act_ref,sl_ref,sp_ref,wt_ref,lt_ref,s_ref,t_ref,ext,ee_ref=rest[-10:]
    ck_ref=par_ref
    i=pl.program_id(0)
    @pl.when(i==0)
    def _():
        ee_ref[...]=spread_matrix(ee_ref.shape)
        if c0:
            s_ref[...]=rest[0][...]; t_ref[...]=rest[1][...]
        else:
            s_ref[...]=jnp.zeros_like(s_ref); t_ref[...]=jnp.zeros_like(t_ref)
    c=c0+i
    start=(first_ref[c//(SPAN//Q)]==1)&(c%(SPAN//Q)==0)
    @pl.when(start)
    def _():
        s_ref[...]=jnp.zeros_like(s_ref); t_ref[...]=jnp.zeros_like(t_ref)
    ext[0:8,:]=t_ref[...]
    x=raw_ref[:,:CW]
    ext[8:8+Q,:]=x
    t_ref[...]=raw_ref[Q-8:Q,:CW]
    pre=par_ref[4:5,:]+ck_ref[3:4,:]*x
    for j in (1,2,3):
        pre=pre+ck_ref[3-j:4-j,:]*ext[8-j:8-j+Q,:]
    sg=sig(pre)
    act=pre*sg
    act_ref[...]=act
    sl_ref[...]=sg*(1.0+pre-act)
    v=act[:,:VW]; b=act[:,VW:VW+NS].astype(bf16); cc=act[:,VW+NS:].astype(bf16)
    dt=softplus(raw_ref[:,CW:]+par_ref[5:6,:128])
    a=-dt*jnp.exp(par_ref[6:7,:128])
    row,col=iotas()
    low=row>=col; up=row<=col
    tri=jnp.where(low,1.0,0.0).astype(bf16)
    cum=tri_sum(tri,a)
    cum_t=cum.T
    last=cum[Q-1:Q,:]
    ee=ee_ref[...]
    sprd=spread(jnp.concatenate([dt,jnp.exp(cum),jnp.exp(last-cum)],axis=0),ee)
    dte,ecum,etail=sprd[:Q],sprd[Q:2*Q],sprd[2*Q:]
    x=v*dte
    g=mm(cc,b,1,1)
    gt=mm(b,cc,1,1)
    parts=[]
    for p in range(VW//128):
        ws=[]
        for h in (2*p,2*p+1):
            d=jnp.where(low,cum[:,h:h+1]-cum_t[h:h+1,:],NEG)
            ws.append((jnp.exp(d)*g).astype(bf16))
            lt=jnp.exp(jnp.where(up,cum_t[h:h+1,:]-cum[:,h:h+1],NEG))
            lt_ref[:,h*Q:(h+1)*Q]=lt
            wt_ref[:,h*Q:(h+1)*Q]=(lt*gt).astype(bf16)
        parts.append(mm(jnp.concatenate(ws,axis=1),halves(x[:,128*p:128*p+128])))
    s=s_ref[...]
    sp_ref[0]=s
    y_ref[...]=jnp.concatenate(parts,axis=1)+ecum*mm(cc,s.astype(bf16))+par_ref[7:8,:VW]*v
    s_ref[...]=ecum[Q-1:Q,:]*s+mm(b,(x*etail).astype(bf16),0,0)

def bwd_kernel(c0,nc,nall,first_ref,raw_ref,act_ref,sl_ref,y_ref,dy_ref,sp_ref,wt_ref,lt_ref,par_ref,*rest):
    out_ref,ds_ref,sn_ref,h_ref,acc_ref,acs_ref,ext,ee_ref,hh_ref=rest[-9:]
    ck_ref=par_ref
    i=pl.program_id(0)
    @pl.when(i==0)
    def _():
        ee_ref[...]=spread_matrix(ee_ref.shape)
        hh_ref[...]=sum_matrix(hh_ref.shape)
        for k,ref in enumerate((ds_ref,sn_ref,h_ref,acc_ref,acs_ref)):
            ref[...]=jnp.zeros_like(ref) if c0+nc==nall else rest[k][...]
    c=c0+nc-1-i
    nxt=jnp.minimum(c+1,nall-1)
    start=(first_ref[nxt//(SPAN//Q)]==1)&(nxt%(SPAN//Q)==0)
    @pl.when(start)
    def _():
        ds_ref[...]=jnp.zeros_like(ds_ref); h_ref[...]=jnp.zeros_like(h_ref)
    act=act_ref[...]
    v=act[:,:VW]; bf=act[:,VW:VW+NS]; cf=act[:,VW+NS:]
    b=bf.astype(bf16); cc=cf.astype(bf16)
    z=raw_ref[:,CW:]+par_ref[5:6,:128]
    dt=softplus(z)
    edl=jnp.exp(par_ref[6:7,:128])
    a=-dt*edl
    row,col=iotas()
    low=row>=col; up=row<=col
    cum=tri_sum(jnp.where(low,1.0,0.0).astype(bf16),a)
    last=cum[Q-1:Q,:]
    ee=ee_ref[...]
    sprd=spread(jnp.concatenate([dt,jnp.exp(cum),jnp.exp(last-cum)],axis=0),ee)
    dte,ecum,etail=sprd[:Q],sprd[Q:2*Q],sprd[2*Q:]
    x=v*dte
    xb=x.astype(bf16)
    dy=dy_ref[...].astype(f32)
    dyb=dy.astype(bf16)
    dgt=jnp.zeros((Q,Q),f32)
    parts=[]
    for p in range(VW//128):
        cols=slice(128*p,128*p+128)
        dyh,dyl=split2(dy[:,cols])
        xh,xl=halves2(x[:,cols])
        dw=mm(jnp.concatenate([xh,xl,xh],axis=1),jnp.concatenate([dyh,dyh,dyl],axis=1),1,1)
        for k in (0,1):
            h=2*p+k
            dgt=dgt+lt_ref[:,h*Q:(h+1)*Q]*dw[k*Q:(k+1)*Q]
        parts.append(mm(wt_ref[:,2*Q*p:2*Q*(p+1)],halves(dy[:,cols])))
    ds=ds_ref[...]
    dsb=ds.astype(bf16)
    s=sp_ref[0]
    dxd=jnp.concatenate(parts,axis=1)
    bds=mm(b,dsb)
    dx=dxd+etail*bds
    xe=(x*etail).astype(bf16)
    dye=dy*ecum
    db=mm3(dgt,cf)+mm3(x*etail,ds,1,1)
    dc=mm3(dgt,bf,0,0)+mm3(dye,s,1,1)
    kk=jnp.sum(dsb.astype(f32)*sn_ref[...],axis=0,keepdims=True)
    rh,rl=split2(dyb.astype(f32)*(y_ref[...]-par_ref[7:8,:VW]*v)-xb.astype(f32)*dxd-xe.astype(f32)*bds)
    kh,kl=split2(jnp.concatenate([kk,jnp.zeros((7,VW),f32)],axis=0))
    hs=mm(jnp.concatenate([rh,rl,(v*dx).astype(bf16),jnp.concatenate([kh,kl],axis=0)],axis=0),hh_ref[...])
    dcum,q,k0=hs[:Q]+hs[Q:2*Q],hs[2*Q:3*Q],hs[3*Q:3*Q+1]+hs[3*Q+8:3*Q+9]
    da=k0+tri_sum(jnp.where(up,1.0,0.0).astype(bf16),dcum)
    dst=(q-da*edl)*sig(z)
    ds_ref[...]=ecum[Q-1:Q,:]*ds+mm3(cf,dye,0,0)
    sn_ref[...]=s
    acs_ref[0:1,:]+=jnp.sum(da*a,axis=0,keepdims=True)
    acs_ref[1:2,:]+=jnp.sum(dst,axis=0,keepdims=True)
    dv=dte*dx+par_ref[7:8,:VW]*dy
    acc_ref[5:6,:VW]+=jnp.sum(dy*v,axis=0,keepdims=True)
    dpre=jnp.concatenate([dv,db,dc],axis=1)*sl_ref[...]
    ext[0:Q,:]=dpre
    ext[Q:Q+8,:]=h_ref[...]
    h_ref[...]=dpre[0:8,:]
    xr=raw_ref[:,:CW]
    draw=ck_ref[3:4,:]*dpre
    acc_ref[3:4,:]+=jnp.sum(dpre*xr,axis=0,keepdims=True)
    acc_ref[4:5,:]+=jnp.sum(dpre,axis=0,keepdims=True)
    for j in (1,2,3):
        sh=ext[j:j+Q,:]
        draw=draw+ck_ref[3-j:4-j,:]*sh
        acc_ref[3-j:4-j,:]+=jnp.sum(sh*xr,axis=0,keepdims=True)
    out_ref[:,:CW]=draw.astype(bf16)
    out_ref[:,CW:]=dst.astype(bf16)

def sd(shape,dt=f32): return jax.ShapeDtypeStruct(shape,dt)

def hbm(shape,dt=f32): return pltpu.HBM(shape,dt)

def vmem(shape,dt=f32): return pltpu.VMEM(shape,dt)

def near_by(x): return pltpu.with_memory_space_constraint(x,pltpu.VMEM)

def stay(x): return pltpu.with_memory_space_constraint(x,pltpu.HBM)

def whole(shape): return pl.BlockSpec(shape,lambda i,*_: (0,)*len(shape))

def once(shape): return pl.BlockSpec(shape,lambda i,*_: (0,)*len(shape),pipeline_mode=pl.Buffered(1))

HL=VW//HW

def ssd_fwd(c0,nc,nall,first,raw,par,carry):
    rb=lambda w: pl.BlockSpec((Q,w),lambda i,*_: (c0+i,0))
    any_spec=pl.BlockSpec(memory_space=pl.ANY)
    held=[whole((NS,VW)),whole((8,CW))]
    return pl.pallas_call(partial(fwd_kernel,c0,nc),
        out_shape=(vmem((nall*Q,VW)),hbm((nall*Q,CW)),hbm((nall*Q,CW)),hbm((nall,NS,VW)),hbm((nall*Q,HL*Q),bf16),hbm((nall*Q,HL*Q)),sd((NS,VW)),sd((8,CW))),
        grid_spec=pltpu.PrefetchScalarGridSpec(num_scalar_prefetch=1,grid=(nc,),
            in_specs=[rb(RW),once((8,CW))]+(held+[any_spec]*6 if carry else []),
            out_specs=(rb(VW),rb(CW),rb(CW),pl.BlockSpec((1,NS,VW),lambda i,*_: (c0+i,0,0)),rb(HL*Q),rb(HL*Q),*held),
            scratch_shapes=[pltpu.VMEM((Q+8,CW),f32),pltpu.VMEM((256,VW),bf16)]),
        input_output_aliases={5+k:k for k in range(6)} if carry else {},
        compiler_params=pltpu.CompilerParams(vmem_limit_bytes=FWD_LIMIT),
        cost_estimate=pl.CostEstimate(flops=int(1.5e9*nc/8),bytes_accessed=30_000_000*nc//8,transcendentals=3_000_000*nc//8),
        name=f"ssd_forward_{c0}")(first,stay(raw),par,*(carry[6:]+(near_by(carry[0]),)+tuple(stay(x) for x in carry[1:6]) if carry else ()))

def ssd_bwd(c0,nc,nall,first,raw,act,sl,y,dy,sp,wt,lt,par,carry):
    rv=lambda w: pl.BlockSpec((Q,w),lambda i,*_: (c0+nc-1-i,0))
    any_spec=pl.BlockSpec(memory_space=pl.ANY)
    held=[whole((NS,VW)),whole((NS,VW)),whole((8,CW)),whole((8,CW)),whole((8,128))]
    return pl.pallas_call(partial(bwd_kernel,c0,nc,nall),
        out_shape=(vmem((nall*Q,RW),bf16),hbm((NS,VW)),hbm((NS,VW)),sd((8,CW)),sd((8,CW)),sd((8,128))),
        grid_spec=pltpu.PrefetchScalarGridSpec(num_scalar_prefetch=1,grid=(nc,),
            in_specs=[rv(RW),rv(CW),rv(CW),rv(VW),rv(VW),pl.BlockSpec((1,NS,VW),lambda i,*_: (c0+nc-1-i,0,0)),rv(HL*Q),rv(HL*Q),once((8,CW))]
                     +(held+[any_spec] if carry else []),
            out_specs=(rv(RW),*held),
            scratch_shapes=[pltpu.VMEM((Q+8,CW),f32),pltpu.VMEM((256,VW),bf16),pltpu.VMEM((VW,128),bf16)]),
        input_output_aliases={15:0} if carry else {},
        compiler_params=pltpu.CompilerParams(vmem_limit_bytes=BACK_LIMIT),
        cost_estimate=pl.CostEstimate(flops=int(3e9*nc/8),bytes_accessed=60_000_000*nc//8,transcendentals=4_000_000*nc//8),
        name=f"ssd_backward_{c0}")(first,stay(raw),stay(act),stay(sl),near_by(y),near_by(dy),stay(sp),stay(wt),stay(lt),par,*((stay(carry[1]),stay(carry[2]))+carry[3:]+(near_by(carry[0]),) if carry else ()))


D = 1536
H = 48
E = 3072
TOK_DEV = 1024
SEQ_DEV = 4
EPSILON = 1e-05
FWD_PARTS = ((0, 4), (4, 4))
BACK_PARTS = ((5, 3), (2, 3), (0, 2))


def contract(left, right, left_dim, right_dim, out=f32):
    return lax.dot_general(
        left, right, (((left_dim,), (right_dim,)), ((), ())), preferred_element_type=f32
    ).astype(out)


def span_layout(seq_lengths, seq_device, seq_offset, device):
    span_index = jnp.arange(SEQ_DEV, dtype=jnp.int32)
    needed = (seq_lengths + SPAN - 1) // SPAN
    owned_seq = (seq_device == device) & (seq_lengths > 0)
    relative = span_index[None, :] - seq_offset[:, None]
    inside = owned_seq[:, None] & (relative >= 0) & (relative < needed[:, None])
    live_rows = jnp.sum(
        jnp.where(inside, jnp.clip(seq_lengths[:, None] - relative * SPAN, 0, SPAN), 0), axis=0
    )
    seq_first = jnp.any(inside & (relative == 0), axis=0)
    return live_rows, seq_first.astype(jnp.int32)


def ring_order(count):
    if count == 8:
        return [0, 2, 4, 6, 7, 5, 3, 1]
    return list(range(count))


def lay(cols, rows, off_ref, refs, out):
    for k, (c0, w) in enumerate(cols):
        out[pl.ds(pl.multiple_of(off_ref[k] * rows, 16), rows), c0 : c0 + w] = refs[k][...]


def row_sums(x):
    a, b = split2(x)
    ones = jnp.ones((8, x.shape[1]), bf16)
    return mm(ones, a, 1, 1) + mm(ones, b, 1, 1)


def project_kernel(cols, rows, nx, off_ref, *refs):
    n = len(cols)
    xs = refs[n : n + nx]
    w_ref, x_ref, xt_ref, raw_ref = refs[n + nx :]
    i = pl.program_id(0)

    @pl.when(i == 0)
    def _():
        lay(cols, rows, off_ref, refs, w_ref)

    for k in range(nx):

        @pl.when(i == k)
        def _(k=k):
            x_ref[...] = xs[k][...]

    xt_ref[...] = x_ref[...].T
    raw_ref[...] = mm(x_ref[...], w_ref[...])


def project(pieces, offsets, xs, total):
    rows, n = pieces[0][0].shape[0], len(pieces)
    cols = [(c0, x.shape[1]) for x, c0 in pieces]
    width = max(c0 + w for c0, w in cols)
    q, depth = xs[0].shape
    nx = len(xs)
    at = lambda w: pl.BlockSpec((q, w), lambda i, off: (off[n + i], 0))
    return pl.pallas_call(
        partial(project_kernel, cols, rows, nx),
        out_shape=(hbm((total, width), bf16), sd((q * nx, depth), bf16), sd((depth, q * nx), bf16), hbm((q * nx, width))),
        grid_spec=pltpu.PrefetchScalarGridSpec(
            num_scalar_prefetch=1,
            grid=(nx,),
            in_specs=[once(x.shape) for x, _ in pieces] + [once(x.shape) for x in xs],
            out_specs=(whole((total, width)), at(depth), pl.BlockSpec((depth, q), lambda i, off: (0, off[n + i])), at(width)),
        ),
        compiler_params=pltpu.CompilerParams(vmem_limit_bytes=22 << 20),
        cost_estimate=pl.CostEstimate(flops=2 * q * nx * total * width, bytes_accessed=30_000_000, transcendentals=0),
        name="project",
    )(offsets, *[x for x, _ in pieces], *xs)


def cotangent_kernel(cols, rows, nx, off_ref, *refs):
    n = len(cols)
    xs = refs[n : n + nx]
    normed_ref, ssd_ref, gain_ref, w_ref, gr_ref, by_ref, sum_ref, yr_ref, x_ref = refs[n + nx :]
    i = pl.program_id(0)

    @pl.when(i == 0)
    def _():
        lay(cols, rows, off_ref, refs, w_ref)

    for k in range(nx):

        @pl.when(i == k)
        def _(k=k):
            x_ref[...] = xs[k][...]

    by = mm(x_ref[...], w_ref[:, VW:])
    gr = mm(normed_ref[...], w_ref[:, :VW])
    by_ref[...] = by
    gr_ref[...] = gr
    gated = ssd_ref[...] * (gr * sig(gr))
    scaled = gated * gain_ref[...]
    yr_ref[...] = scaled.astype(bf16)
    square = row_sums(gated * gated)
    cross = row_sums(by * scaled)
    top = lax.broadcasted_iota(jnp.int32, square.shape, 0) == 0
    sum_ref[0] = jnp.where(top, square, cross)


def cotangent(pieces, offsets, xs, normed, ssd, gain, total):
    rows, n = pieces[0][0].shape[0], len(pieces)
    cols = [(c0, x.shape[1]) for x, c0 in pieces]
    width = max(c0 + w for c0, w in cols)
    q, depth = xs[0].shape
    nx = len(xs)
    at = lambda w: pl.BlockSpec((q, w), lambda i, off: (off[n + i], 0))
    return pl.pallas_call(
        partial(cotangent_kernel, cols, rows, nx),
        out_shape=(
            vmem((total, width), bf16),
            sd((q * nx, VW)),
            sd((q * nx, VW)),
            sd((nx, 8, q)),
            sd((q * nx, VW), bf16),
        ),
        grid_spec=pltpu.PrefetchScalarGridSpec(
            num_scalar_prefetch=1,
            grid=(nx,),
            in_specs=[once(x.shape) for x, _ in pieces]
            + [once(x.shape) for x in xs]
            + [at(depth), at(VW), once((1, VW))],
            out_specs=(
                whole((total, width)),
                at(VW),
                at(VW),
                pl.BlockSpec((1, 8, q), lambda i, off: (off[n + i], 0, 0)),
                at(VW),
            ),
            scratch_shapes=[pltpu.VMEM((q, depth), bf16)],
        ),
        compiler_params=pltpu.CompilerParams(vmem_limit_bytes=30 << 20),
        cost_estimate=pl.CostEstimate(flops=2 * q * nx * total * width, bytes_accessed=30_000_000, transcendentals=800_000),
        name="cotangent",
    )(offsets, *[x for x, _ in pieces], *xs, normed, near_by(ssd), gain)


def turn_kernel(nx, off_ref, *refs):
    i = pl.program_id(0)
    for k in range(nx):

        @pl.when(i == k)
        def _(k=k):
            refs[nx][...] = refs[k][...].T


def turn(offsets, xs):
    q, depth = xs[0].shape
    nx = len(xs)
    n = offsets.shape[0] - nx
    return pl.pallas_call(
        partial(turn_kernel, nx),
        out_shape=sd((depth, q * nx), bf16),
        grid_spec=pltpu.PrefetchScalarGridSpec(
            num_scalar_prefetch=1,
            grid=(nx,),
            in_specs=[once(x.shape) for x in xs],
            out_specs=pl.BlockSpec((depth, q), lambda i, off: (0, off[n + i])),
        ),
        compiler_params=pltpu.CompilerParams(vmem_limit_bytes=8 << 20),
        cost_estimate=pl.CostEstimate(flops=0, bytes_accessed=10_000_000, transcendentals=0),
        name="turn",
    )(offsets, *xs)


def gate_kernel(sum_ref, by_ref, gr_ref, ssd_ref, gain_ref, ny_ref, bg_ref, dy_ref, gg_ref):
    @pl.when(pl.program_id(0) == 0)
    def _():
        gg_ref[...] = jnp.zeros_like(gg_ref)

    sums = sum_ref[0].T
    inv = lax.rsqrt(sums[:, 0:1] / E + EPSILON)
    gr, ssd, by, gain = gr_ref[...], ssd_ref[...], by_ref[...], gain_ref[...]
    sg = sig(gr)
    gate = gr * sg
    unit = ssd * gate * inv
    ny_ref[...] = (unit * gain).astype(bf16)
    gg_ref[0:1, :] += jnp.sum(by * unit, axis=0, keepdims=True)
    back = inv * (by * gain - unit * (inv * sums[:, 1:2] / E))
    bg_ref[...] = (back * ssd * (sg * (1.0 + gr - gate))).astype(bf16)
    dy_ref[...] = back * gate


def gate_back(sums, by, gate_raw, ssd, gain):
    t, width = by.shape
    n, _, q = sums.shape
    rb = pl.BlockSpec((q, width), lambda i: (i, 0))
    return pl.pallas_call(
        gate_kernel,
        out_shape=(sd((t, width), bf16), sd((t, width), bf16), vmem((t, width)), sd((8, width))),
        grid=(n,),
        in_specs=[pl.BlockSpec((1, 8, q), lambda i: (i, 0, 0)), rb, rb, rb, once((1, width))],
        out_specs=(rb, rb, rb, whole((8, width))),
        compiler_params=pltpu.CompilerParams(vmem_limit_bytes=12 << 20),
        cost_estimate=pl.CostEstimate(flops=20_000_000, bytes_accessed=15_000_000, transcendentals=800_000),
        name="gate_back",
    )(sums, by, gate_raw, near_by(ssd), gain)


def normed_kernel(
    half, at_ref, first_ref, gate_ref, w_ref, g_ref, x_ref, h_ref, m_ref, s_ref, mk_ref, mn_ref, ma_ref, mb_ref, away_ref, keep_ref, ng_ref, o_ref, scale_ref
):
    i = pl.program_id(0)

    @pl.when(i == 0)
    def _():
        ng_ref[...] = jnp.zeros_like(ng_ref)
        inv = lax.rsqrt(s_ref[0, 0:1, :] / E + EPSILON) * m_ref[...]
        scale_ref[...] = jnp.broadcast_to(inv, (8, inv.shape[1])).T

    n = o_ref.shape[0]
    scale = scale_ref[pl.ds(pl.multiple_of(i * n, 8), n), 0:1]
    far = jnp.where(i < half, ma_ref[...].astype(f32), mb_ref[...].astype(f32))
    mixed = mk_ref[0].astype(f32) + mn_ref[0].astype(f32) + far
    o_ref[...] = h_ref[...] + scale * mixed
    back = mm(first_ref[...], w_ref[...], 1, 1) + mm(gate_ref[...], g_ref[...], 1, 1)
    ng_ref[0:1, :] += jnp.sum(back * x_ref[...].astype(f32), axis=0, keepdims=True)

    @pl.when(i < half)
    def _():
        away_ref[0] = back.astype(bf16)

    @pl.when(i >= half)
    def _():
        keep_ref[0] = back.astype(bf16)


def back_normed_rows(at, q, first, gate, w, gate_w, normed, hidden, mask, sums, keep, near, far):
    depth = normed.shape[1]
    n = at.shape[0]
    half = n // 2
    rb = lambda c: pl.BlockSpec((q, c), lambda i, at: (at[i], 0))
    part = lambda c: pl.BlockSpec((q // n, c), lambda i, at: (i, 0))
    second = pl.BlockSpec((1, q // n, depth), lambda i, at: (1, i, 0))
    return pl.pallas_call(
        partial(normed_kernel, half),
        out_shape=(sd((half, q, depth), bf16), sd((half, q, depth), bf16), sd((8, depth)), sd((q, depth))),
        grid_spec=pltpu.PrefetchScalarGridSpec(
            num_scalar_prefetch=1,
            grid=(n,),
            in_specs=[rb(RW), rb(VW), once(w.shape), once((depth, VW)), rb(depth)]
            + [part(depth), whole((1, q)), pl.BlockSpec((1, 8, q), lambda i, at: (at[n - 1], 0, 0)), second, second]
            + [
                pl.BlockSpec((q // n, depth), lambda i, at: (jnp.minimum(i, half - 1), 0)),
                pl.BlockSpec((q // n, depth), lambda i, at: (jnp.maximum(i - half, 0), 0)),
            ],
            out_specs=(
                pl.BlockSpec((1, q, depth), lambda i, at: (jnp.minimum(i, half - 1), 0, 0)),
                pl.BlockSpec((1, q, depth), lambda i, at: (jnp.maximum(i - half, 0), 0, 0)),
                whole((8, depth)),
                part(depth),
            ),
            scratch_shapes=[pltpu.VMEM((q, 8), f32)],
        ),
        compiler_params=pltpu.CompilerParams(vmem_limit_bytes=22 << 20),
        cost_estimate=pl.CostEstimate(flops=2 * n * q * depth * (RW + VW), bytes_accessed=60_000_000, transcendentals=0),
        name="back_normed",
    )(at, near_by(first), gate, w, near_by(gate_w), normed, hidden, mask, sums, keep, near, *far)


def mixer_kernel(half, at_ref, x_ref, w_ref, away_ref, keep_ref):
    r = mm(x_ref[...], w_ref[...], 1, 1).astype(bf16)
    i = pl.program_id(0)

    @pl.when(i < half)
    def _():
        away_ref[0] = r

    @pl.when(i >= half)
    def _():
        keep_ref[0] = r


def mixer_blocks(at, q, x, w):
    n, depth, width = at.shape[0], w.shape[0], x.shape[1]
    half = n // 2
    return pl.pallas_call(
        partial(mixer_kernel, half),
        out_shape=(sd((half, q, depth), bf16), sd((half, q, depth), bf16)),
        grid_spec=pltpu.PrefetchScalarGridSpec(
            num_scalar_prefetch=1,
            grid=(n,),
            in_specs=[
                pl.BlockSpec((q, width), lambda i, at: (at[i], 0)),
                pl.BlockSpec((depth, width), lambda i, at: (0, 1), pipeline_mode=pl.Buffered(1)),
            ],
            out_specs=(
                pl.BlockSpec((1, q, depth), lambda i, at: (jnp.minimum(i, half - 1), 0, 0)),
                pl.BlockSpec((1, q, depth), lambda i, at: (jnp.maximum(i - half, 0), 0, 0)),
            ),
        ),
        compiler_params=pltpu.CompilerParams(vmem_limit_bytes=12 << 20),
        cost_estimate=pl.CostEstimate(flops=2 * n * q * depth * width, bytes_accessed=20_000_000, transcendentals=0),
        name="mixer_rows",
    )(at, x, near_by(w))


def grad_kernel(per, rows, at_ref, xt_ref, back_ref, out_ref):
    i = pl.program_id(0)
    r = mm(xt_ref[...], back_ref[...]).astype(bf16)
    for d in range(per):
        out_ref[pl.ds(at_ref[i * per + d], 1)] = r[d * rows : (d + 1) * rows][None]


def weight_grad(at, xt, back, n_dp):
    depth, t = xt.shape
    rows, width = depth // n_dp, back.shape[1]
    steps = 2
    return pl.pallas_call(
        partial(grad_kernel, n_dp // steps, rows),
        out_shape=sd((n_dp, rows, width), bf16),
        grid_spec=pltpu.PrefetchScalarGridSpec(
            num_scalar_prefetch=1,
            grid=(steps,),
            in_specs=[pl.BlockSpec((depth // steps, t), lambda i, at: (i, 0)), once(back.shape)],
            out_specs=whole((n_dp, rows, width)),
        ),
        compiler_params=pltpu.CompilerParams(vmem_limit_bytes=20 << 20),
        cost_estimate=pl.CostEstimate(flops=2 * depth * t * width, bytes_accessed=8_000_000, transcendentals=0),
        name="weight_grad",
    )(at, xt, near_by(back))


def far_pair_kernel(at_ref, xt_ref, back_ref, zt_ref, y_ref, f_ref, b_ref):
    f_ref[...] = mm(xt_ref[...], back_ref[...]).astype(bf16)
    b_ref[...] = mm(zt_ref[...], y_ref[...]).astype(bf16)


def far_value_kernel(mid, at_ref, xt_ref, back_ref, f_ref, b_ref):
    r = mm(xt_ref[...], back_ref[...]).astype(bf16)
    f_ref[...] = r[:, :mid]
    b_ref[...] = r[:, mid:]


def far_grad(at, rows, pairs, mid=0):
    depth, t = pairs[0][0].shape
    block = pl.BlockSpec((rows, t), lambda i, at: (at[0], 0))
    specs, args = [], []
    for xt, back in pairs:
        specs += [block, once(back.shape)]
        args += [xt, back]
    widths = (mid, pairs[0][1].shape[1] - mid) if mid else tuple(b.shape[1] for _, b in pairs)
    return pl.pallas_call(
        partial(far_value_kernel, mid) if mid else far_pair_kernel,
        out_shape=tuple(sd((rows, w), bf16) for w in widths),
        grid_spec=pltpu.PrefetchScalarGridSpec(
            num_scalar_prefetch=1,
            grid=(1,),
            in_specs=specs,
            out_specs=tuple(whole((rows, w)) for w in widths),
        ),
        compiler_params=pltpu.CompilerParams(vmem_limit_bytes=12 << 20),
        cost_estimate=pl.CostEstimate(flops=2 * rows * t * sum(widths), bytes_accessed=4_000_000, transcendentals=0),
        name="far_grad",
    )(at, *args)


def pair_grad_kernel(per, rows, at_ref, xt_ref, back_ref, zt_ref, y_ref, out_ref):
    i = pl.program_id(0)
    for k, r in enumerate((mm(xt_ref[...], back_ref[...]), mm(zt_ref[...], y_ref[...]))):
        r = r.astype(bf16)
        for d in range(per):
            out_ref[pl.ds(at_ref[i * per + d], 1), :, k * VW : (k + 1) * VW] = r[d * rows : (d + 1) * rows][None]


def pair_grad(at, xt, back, zt, y, n_dp):
    depth, t = xt.shape
    rows, steps = depth // n_dp, 4
    rb = pl.BlockSpec((depth // steps, t), lambda i, at: (i, 0))
    return pl.pallas_call(
        partial(pair_grad_kernel, n_dp // steps, rows),
        out_shape=sd((n_dp, rows, 2 * VW), bf16),
        grid_spec=pltpu.PrefetchScalarGridSpec(
            num_scalar_prefetch=1,
            grid=(steps,),
            in_specs=[rb, once(back.shape), rb, once(y.shape)],
            out_specs=whole((n_dp, rows, 2 * VW)),
        ),
        compiler_params=pltpu.CompilerParams(vmem_limit_bytes=22 << 20),
        cost_estimate=pl.CostEstimate(flops=4 * depth * t * VW, bytes_accessed=14_000_000, transcendentals=0),
        name="pair_grad",
    )(at, xt, back, zt, y)


def finish_kernel(
    x_ref, f_ref, b_ref, g_ref, small_ref, gv_ref, steps_ref, taps_ref, bias_ref, gain_ref, sb_ref, dl_ref, skip_ref
):
    value = x_ref[...].astype(f32) + f_ref[...].astype(f32) + b_ref[...].astype(f32)
    gv_ref[:, 0, :] = g_ref[...]
    gv_ref[:, 1, :] = value[:, :VW]
    heads = sb_ref.shape[0]
    steps_ref[...] = value[:, CW:].T[:heads, :]
    taps_ref[...] = small_ref[0:4, :VW]
    bias_ref[...] = small_ref[4, :VW]
    gain_ref[...] = small_ref[6, :VW]
    dl_ref[...] = small_ref[6, VW : VW + heads]
    sb_ref[...] = small_ref[6, VW + 128 : VW + 128 + heads]
    parts = jnp.concatenate(split3(small_ref[0:8, :VW]), axis=0)
    sums = mm(parts, sum_matrix((VW, 128)))
    skip_ref[...] = (sums[5:6] + sums[13:14] + sums[21:22])[0, :heads]


def finish(x, f, b, pair_out, small, heads):
    rows, width = x.shape
    full = whole((rows, width))
    outs = ((rows, 2, VW), (heads, rows), (4, VW), (VW,), (VW,), (heads,), (heads,), (heads,))
    return pl.pallas_call(
        finish_kernel,
        out_shape=tuple(sd(o) for o in outs),
        grid=(1,),
        in_specs=[full, full, full, pl.BlockSpec((rows, VW), lambda i: (0, 0)), whole(small.shape)],
        out_specs=tuple(whole(o) for o in outs),
        compiler_params=pltpu.CompilerParams(vmem_limit_bytes=16 << 20),
        cost_estimate=pl.CostEstimate(flops=1_000_000, bytes_accessed=5_000_000, transcendentals=0),
        name="finish",
    )(x, stay(f), stay(b), pair_out, small)


class Ring:
    def __init__(self, count):
        self.count = count
        self.half = count // 2
        self.order = ring_order(count)
        at = {d: i for i, d in enumerate(self.order)}
        self.table = [[self.order[(at[d] + k) % count] for k in range(count)] for d in range(count)]
        self.ahead = [(self.order[i], self.order[(i + 1) % count]) for i in range(count)]
        self.back = [(b, a) for a, b in self.ahead]

    def rows_of(self, table):
        return jnp.asarray(table, jnp.int32)[lax.axis_index("dp")]

    def hop(self, f, b):
        return lax.ppermute(f, "dp", self.ahead), lax.ppermute(b, "dp", self.back)


class Gather:
    def __init__(self, ring, x, c0=0):
        self.ring, self.mid, self.c0 = ring, x.shape[1] // 2 // 128 * 128, c0
        self.pieces, self.f, self.b, self.s = [(x, c0)], x, x, 0

    def ready(self):
        if self.s == self.ring.half - 1:
            return [self.f[:, : self.mid], self.b[:, self.mid :]]
        return [self.f, self.b]

    def step(self, f, b):
        self.s += 1
        self.f, self.b = self.ring.hop(f, b)
        self.pieces += [(self.f, self.c0), (self.b, self.c0 + (self.mid if self.s == self.ring.half else 0))]

    @staticmethod
    def offsets(ring):
        ahead = [0]
        for s in range(1, ring.half + 1):
            ahead += [ring.count - s, s]
        return [[ring.table[d][k] for k in ahead] for d in range(ring.count)]


class Scatter:
    def __init__(self, ring, first):
        self.ring, self.first, self.x, self.s = ring, list(first), None, ring.half

    def ready(self):
        x, s = self.x, self.s
        if s == self.ring.half:
            return self.first
        f, b = self.f, self.b
        if s == self.ring.half - 1:
            f = jnp.pad(f, ((0, 0), (0, x.shape[2] - f.shape[1])))
            b = jnp.pad(b, ((0, 0), (x.shape[2] - b.shape[1], 0)))
        f = x[s].astype(f32) + f.astype(f32)
        b = x[self.ring.count - s].astype(f32) + b.astype(f32)
        return [f.astype(bf16), b.astype(bf16)]

    def step(self, f, b):
        self.f, self.b = self.ring.hop(f, b)
        self.s -= 1

    def total(self, columns=slice(None)):
        return self.x[0, :, columns].astype(f32) + self.f[:, columns].astype(f32) + self.b[:, columns].astype(f32)


def swap(x, axis, count, bits):
    return lax.ppermute(x, axis, [(i, i ^ bits) for i in range(count)])


def tensor_order(count):
    keys = [0]
    bit = count // 2
    while bit:
        keys += [k ^ bit for k in keys]
        bit //= 2
    return keys


def pick(x, index, axis=0):
    return lax.dynamic_index_in_dim(x, index, axis, keepdims=False)


def groups_of(count):
    bits = [1 << k for k in range(count.bit_length() - 1)]
    first = len(bits) % 2
    return ([bits[:first]] if first else []) + [bits[k : k + 2] for k in range(first, len(bits), 2)]


def others(bits):
    return [bits[0]] if len(bits) == 1 else [bits[0], bits[1], bits[0] | bits[1]]


class Spread:
    def __init__(self, x, axis, count):
        self.x, self.axis, self.count, self.groups = x, axis, count, groups_of(count)

    def step(self, x):
        bits = self.groups.pop(0)
        self.x = sum((swap(x, self.axis, self.count, k) for k in others(bits)), x)


def together(*lists):
    flat = lax.optimization_barrier(tuple(x for xs in lists for x in xs))
    out, at = [], 0
    for xs in lists:
        out.append(list(flat[at : at + len(xs)]))
        at += len(xs)
    return out


def body(
    n_dp,
    n_tensor,
    hidden_in,
    norm_gain,
    gate_value_weight,
    state_proj_weight,
    step_weight,
    conv_value_kernel,
    conv_value_bias,
    conv_state_kernel,
    conv_state_bias,
    step_bias,
    decay_log,
    skip_scale,
    gate_norm_gain,
    out_weight,
    out_cotangent,
    seq_lengths,
    seq_device,
    seq_offset,
):
    quarter = hidden_in.shape[0]
    heads = step_weight.shape[1]
    rows = gate_value_weight.shape[0]
    me, dp = lax.axis_index("tensor"), lax.axis_index("dp")
    ring = Ring(n_dp)
    ring_at = ring.rows_of([[ring.table[d].index(k) for k in range(n_dp)] for d in range(n_dp)])
    far_at = ring.rows_of([[ring.table[d][ring.half]] for d in range(n_dp)])
    order = me ^ jnp.asarray([3, 1, 2, 0], jnp.int32)
    offsets = jnp.concatenate([ring.rows_of(Gather.offsets(ring)), me ^ jnp.asarray(tensor_order(n_tensor), jnp.int32)])
    to_core = lambda x: swap(x, "tensor", n_tensor, 1)
    to_far = lambda x: swap(x, "tensor", n_tensor, 2)

    live_rows, seq_first = span_layout(seq_lengths, seq_device, seq_offset, dp)
    row = me * quarter + jnp.arange(quarter, dtype=jnp.int32)
    local_live = jnp.sum(
        jnp.where((row // SPAN)[:, None] == jnp.arange(SEQ_DEV)[None, :], live_rows[None, :], 0), axis=1
    )
    local_mask = (row % SPAN < local_live).astype(f32)

    pad_to = lambda x, w: jnp.pad(x, (0, w - x.shape[0]))[None]
    params = jnp.concatenate(
        [
            jnp.concatenate([conv_value_kernel, conv_state_kernel], axis=0).T,
            jnp.concatenate([conv_value_bias, conv_state_bias])[None],
            pad_to(step_bias, CW),
            pad_to(decay_log, CW),
            pad_to(jnp.repeat(skip_scale, HW), CW),
        ],
        axis=0,
    )
    gain = gate_norm_gain[None]
    zeros = lambda *s: jnp.zeros(s, f32)

    first_own = jnp.concatenate(
        [gate_value_weight[:, 1, :], state_proj_weight, jnp.pad(step_weight, ((0, 0), (0, 128 - heads)))], axis=1
    )
    first_own, hidden, later = lax.optimization_barrier((first_own, hidden_in, gate_value_weight))
    inv_rms = lax.rsqrt(jnp.mean(hidden * hidden, axis=-1) + EPSILON)
    scaled = hidden * inv_rms[:, None]
    normed_local = (scaled * norm_gain[None, :]).astype(bf16)
    first = Gather(ring, first_own)
    first.step(*first.ready())
    far = to_far(normed_local)
    out_own = jnp.concatenate([later[:, 0, :], out_weight], axis=1)
    back_local = (local_mask[:, None] * out_cotangent).astype(bf16)
    (out_own, offsets, ring_at, far_at, order, seq_first, params, back_local) = lax.optimization_barrier(
        (out_own, offsets, ring_at, far_at, order, seq_first, params, back_local)
    )
    out = Gather(ring, out_own)
    for s in range(1, ring.half):
        extra = []
        if s == min(2, ring.half - 1):
            extra = [[normed_local, far]]
        elif s == ring.half - 1:
            extra = [[back_local] + normed_parts[2:]]
        sends = together(first.ready(), *extra)
        first.step(*sends.pop(0))
        if s == min(2, ring.half - 1):
            [a, far] = sends.pop(0)
            normed_parts = [a, far, to_core(a), to_core(far)]
        elif s == ring.half - 1:
            [back_local, *normed_parts[2:]] = sends.pop(0)
            back_far = to_far(back_local)
    ps, os = together([x for x, _ in first.pieces] + normed_parts, out.ready())
    out.step(*os)
    n = len(first.pieces)
    first_w, normed, normed_t, raw = project(
        [(x, c0) for x, (_, c0) in zip(ps, first.pieces)], offsets, ps[n:], D
    )
    chunks = TOK_DEV // Q
    carry = ()
    for k, (c0, n) in enumerate(FWD_PARTS):
        held, os, bs = together([carry[6]] if carry else [raw], out.ready(), [back_local, back_far] if k == 0 else [])
        out.step(*os)
        if k:
            carry = carry[:6] + (held[0],) + carry[7:]
        else:
            raw = held[0]
            back_parts = bs + [to_core(x) for x in bs]
        carry = tuple(ssd_fwd(c0, n, chunks, seq_first, raw, params, carry))
    held, os, back_parts = together([carry[0]], out.ready(), back_parts)
    carry = (held[0],) + carry[1:]
    out.step(*os)
    back_t = turn(offsets, back_parts)
    while out.s < ring.half:
        out.step(*out.ready())
    ssd, act, slope, states, weights_t, decays_t = carry[:6]

    out_w, gate_raw, back_y, sums, gated = cotangent(
        out.pieces, offsets, back_parts, normed, ssd, gain, D
    )
    total = Spread(sums, "tensor", n_tensor)
    while total.groups:
        total.step(total.x)
    sums = total.x
    mixer = mixer_blocks(order, quarter, gated, out_w)
    sums, mixer_away, mixer_keep = lax.optimization_barrier((sums, *mixer))
    normed_y, back_gate, back_ssd, gain_grad = gate_back(sums, back_y, gate_raw, ssd, gain)
    pair_sum = Scatter(ring, far_grad(far_at, rows, [(normed_t, back_gate), (back_t, normed_y)]))
    ps, [away, mixer_keep, back_gate, normed_y] = together(
        pair_sum.ready(), [mixer_away, mixer_keep, back_gate, normed_y]
    )
    pair_sum.step(*ps)
    mixer_near = to_core(away)
    pair_sum.x = pair_grad(ring_at, normed_t, back_gate, back_t, normed_y, n_dp)
    [pair_sum.f, pair_sum.b, pair_sum.x, mixer_near], = together([pair_sum.f, pair_sum.b, pair_sum.x, mixer_near])

    half_rows = quarter // 2
    away = (mixer_keep[0].astype(f32) + mixer_near[0].astype(f32)).astype(bf16)
    away = [away[:half_rows], away[half_rows:]]
    carry, held, mixer_far = (), [back_ssd], []
    for k, (c0, n) in enumerate(BACK_PARTS):
        ps = pair_sum.ready() if pair_sum.s else []
        held, ps, ms = together(held, ps, away[k : k + 1])
        if carry:
            carry = carry[:1] + (held[0],) + carry[2:]
        else:
            back_ssd = held[0]
        if pair_sum.s:
            pair_sum.step(*ps)
        ms = [to_far(x) for x in ms]
        carry = tuple(
            ssd_bwd(
                c0, n, chunks, seq_first, raw, act, slope, ssd, back_ssd, states, weights_t, decays_t, params, carry
            )
        )
        last = k == len(BACK_PARTS) - 1
        held, [pair_sum.f, pair_sum.b], ms = together([carry[0 if last else 1]], [pair_sum.f, pair_sum.b], ms)
        mixer_far += ms
    carry = (held[0],) + carry[1:]
    while pair_sum.s:
        pair_sum.step(*pair_sum.ready())
    back_first, _, _, _, acc, acs = carry
    value_sum = Scatter(ring, far_grad(far_at, rows, [(normed_t, back_first)], RW // 2 // 128 * 128))
    vs, [back_first] = together(value_sum.ready(), [back_first])
    value_sum.step(*vs)
    value_sum.x = weight_grad(ring_at, normed_t, back_first, n_dp)
    [value_sum.f, value_sum.b, value_sum.x, back_first], = together(
        [value_sum.f, value_sum.b, value_sum.x, back_first]
    )
    vs, [back_first] = together(value_sum.ready(), [back_first])
    value_sum.step(*vs)
    away, keep, ng, output = back_normed_rows(
        order, quarter, back_first, back_gate, first_w, out_w, normed, hidden_in, local_mask[None], sums, mixer_keep, mixer_near, mixer_far
    )
    [value_sum.f, value_sum.b, away, keep, ng], = together([value_sum.f, value_sum.b, away, keep, ng])
    shared = jnp.concatenate([acc[:5, VW:], (ng[0] / norm_gain).reshape(6, 256), zeros(5, 256)], axis=0)
    shared = Spread(shared, "tensor", n_tensor)
    vs, cs, ps = together(value_sum.ready(), [away], [shared.x])
    value_sum.step(*vs)
    near = to_core(cs[0])
    away = (keep[0].astype(f32) + near[0].astype(f32)).astype(bf16)
    got = to_far(away[:half_rows])
    shared.step(ps[0])
    [value_sum.f, value_sum.b, near, away, got, shared.x], = together(
        [value_sum.f, value_sum.b, near, away, got, shared.x]
    )
    own = jnp.concatenate(
        [acc[:6], jnp.concatenate([gain_grad[0], acs[0], acs[1]])[None], zeros(1, CW)], axis=0
    )
    while shared.groups:
        shared.step(shared.x)
    small = Spread(jnp.concatenate([own, shared.x.reshape(4, CW)], axis=0), "dp", n_dp)
    vs, cs, ps = together(value_sum.ready(), [away[half_rows:]], [small.x])
    value_sum.step(*vs)
    cs = [got, to_far(cs[0])]
    small.step(ps[0])
    while value_sum.s:
        value_sum.step(*value_sum.ready())
    [value_sum.f, value_sum.b, small.x], cs = together([value_sum.f, value_sum.b, small.x], cs)
    state_grad = value_sum.total(slice(VW, CW)).reshape(n_tensor, rows // n_tensor, 2 * NS)
    ps, ss = together([small.x], [pick(state_grad, me ^ k) for k in range(n_tensor)])
    state_out = sum((swap(ss[k], "tensor", n_tensor, k) for k in range(1, n_tensor)), ss[0])
    small.x = ps[0]
    while small.groups:
        small.step(small.x)
    small = small.x
    pair_out = pair_sum.total()
    gv_out, step_out, taps, bias, gains, steps, decays, skips = finish(
        value_sum.x[0], value_sum.f, value_sum.b, pair_out, small, heads
    )
    back_rows = keep[1].astype(f32) + near[1].astype(f32) + jnp.concatenate(cs, axis=0).astype(f32)
    back_scaled = back_rows * norm_gain[None, :]
    hidden_gradient = out_cotangent + inv_rms[:, None] * (
        back_scaled - scaled * jnp.mean(back_scaled * scaled, axis=-1)[:, None]
    )
    shared = small[8:].reshape(16, 256)
    index = dp * n_tensor + me
    all_count = n_dp * n_tensor
    kern_share = 2 * NS // all_count
    state_kernel_out = lax.dynamic_slice(shared, (0, index * kern_share), (5, kern_share))
    norm_out = lax.dynamic_slice(shared[5:11].reshape(D), (index * (D // all_count),), (D // all_count,))
    return (
        output,
        hidden_gradient,
        norm_out,
        gv_out,
        state_out,
        step_out.T,
        taps.T,
        bias,
        state_kernel_out[:4].T,
        state_kernel_out[4],
        steps,
        decays,
        skips,
        gains,
        pair_out[:, VW:],
    )


def solution(mesh):
    in_specs = (
        P(("dp", "tensor"), None),
        P(),
        P("dp", None, "tensor"),
        P("dp", None),
        P("dp", "tensor"),
        P("tensor", None),
        P("tensor"),
        P(),
        P(),
        P("tensor"),
        P("tensor"),
        P("tensor"),
        P("tensor"),
        P("dp", "tensor"),
        P(("dp", "tensor"), None),
        P(),
        P(),
        P(),
    )
    out_specs = (
        P(("dp", "tensor"), None),
        P(("dp", "tensor"), None),
        P(("dp", "tensor")),
        P("dp", None, "tensor"),
        P(("dp", "tensor"), None),
        P("dp", "tensor"),
        P("tensor", None),
        P("tensor"),
        P(("dp", "tensor"), None),
        P(("dp", "tensor")),
        P("tensor"),
        P("tensor"),
        P("tensor"),
        P("tensor"),
        P("dp", "tensor"),
    )
    return jax.shard_map(
        partial(body, mesh.shape["dp"], mesh.shape["tensor"]),
        mesh=mesh,
        in_specs=in_specs,
        out_specs=out_specs,
        check_vma=False,
    )
```

```python
from functools import partial

import jax, jax.numpy as jnp
from jax import lax
from jax.experimental import pallas as pl
from jax.experimental.pallas import tpu as pltpu
from jax.sharding import PartitionSpec as P
f32=jnp.float32; bf16=jnp.bfloat16
Q=128
NS=128
VW=768
HW=64
CW=1024
RW=1152
SPAN=256
FWD_LIMIT=12<<20
BACK_LIMIT=16<<20
NEG=-1e30

def mm(a,b,ca=1,cb=0):
    return lax.dot_general(a,b,(((ca,),(cb,)),((),())),preferred_element_type=f32)

def split2(x):
    hi=x.astype(bf16); return hi,(x-hi.astype(f32)).astype(bf16)

def split3(x):
    hi=x.astype(bf16); r=x-hi.astype(f32); mid=r.astype(bf16); return hi,mid,(r-mid.astype(f32)).astype(bf16)

def mm3(a,b,ca=1,cb=0):
    ah,al=split2(a); bh,bl=split2(b)
    return mm(jnp.concatenate([ah,ah,al],axis=ca),jnp.concatenate([bh,bl,bh],axis=cb),ca,cb)

def tri_sum(tri,x):
    a,b,c=split3(x); w=x.shape[1]
    p=mm(tri,jnp.concatenate([a,b,c],axis=1))
    return p[:,:w]+p[:,w:2*w]+p[:,2*w:]

def spread(x,ee):
    a,b=split2(x)
    return mm(jnp.concatenate([a,b],axis=1),ee)

def iotas():
    return lax.broadcasted_iota(jnp.int32,(Q,Q),0),lax.broadcasted_iota(jnp.int32,(Q,Q),1)

def softplus(z):
    return jnp.maximum(z,0.0)+jnp.log(1.0+jnp.exp(-jnp.abs(z)))

def sig(z):
    return 1.0/(1.0+jnp.exp(-z))

def halves(x):
    lane=lax.broadcasted_iota(jnp.int32,x.shape,1)
    lo=jnp.where(lane<HW,x,0.0); hi=jnp.where(lane<HW,0.0,x)
    return jnp.concatenate([lo.astype(bf16),hi.astype(bf16)],axis=0)

def spread_matrix(shape):
    r=lax.broadcasted_iota(jnp.int32,shape,0)%128; c=lax.broadcasted_iota(jnp.int32,shape,1)//HW
    return jnp.where(r==c,1.0,0.0).astype(bf16)

def sum_matrix(shape):
    r=lax.broadcasted_iota(jnp.int32,shape,0)%VW//HW; c=lax.broadcasted_iota(jnp.int32,shape,1)
    return jnp.where(r==c,1.0,0.0).astype(bf16)

def halves2(x):
    lane=lax.broadcasted_iota(jnp.int32,x.shape,1)
    h,l=split2(jnp.concatenate([jnp.where(lane<HW,x,0.0),jnp.where(lane<HW,0.0,x)],axis=0))
    return h,l

def fwd_kernel(c0,nc,first_ref,raw_ref,par_ref,*rest):
    y_ref,act_ref,sl_ref,sp_ref,wt_ref,lt_ref,s_ref,t_ref,ext,ee_ref=rest[-10:]
    ck_ref=par_ref
    i=pl.program_id(0)
    @pl.when(i==0)
    def _():
        ee_ref[...]=spread_matrix(ee_ref.shape)
        if c0:
            s_ref[...]=rest[0][...]; t_ref[...]=rest[1][...]
        else:
            s_ref[...]=jnp.zeros_like(s_ref); t_ref[...]=jnp.zeros_like(t_ref)
    c=c0+i
    start=(first_ref[c//(SPAN//Q)]==1)&(c%(SPAN//Q)==0)
    @pl.when(start)
    def _():
        s_ref[...]=jnp.zeros_like(s_ref); t_ref[...]=jnp.zeros_like(t_ref)
    ext[0:8,:]=t_ref[...]
    x=raw_ref[:,:CW]
    ext[8:8+Q,:]=x
    t_ref[...]=raw_ref[Q-8:Q,:CW]
    pre=par_ref[4:5,:]+ck_ref[3:4,:]*x
    for j in (1,2,3):
        pre=pre+ck_ref[3-j:4-j,:]*ext[8-j:8-j+Q,:]
    sg=sig(pre)
    act=pre*sg
    act_ref[...]=act
    sl_ref[...]=sg*(1.0+pre-act)
    v=act[:,:VW]; b=act[:,VW:VW+NS].astype(bf16); cc=act[:,VW+NS:].astype(bf16)
    dt=softplus(raw_ref[:,CW:]+par_ref[5:6,:128])
    a=-dt*jnp.exp(par_ref[6:7,:128])
    row,col=iotas()
    low=row>=col; up=row<=col
    tri=jnp.where(low,1.0,0.0).astype(bf16)
    cum=tri_sum(tri,a)
    cum_t=cum.T
    last=cum[Q-1:Q,:]
    ee=ee_ref[...]
    sprd=spread(jnp.concatenate([dt,jnp.exp(cum),jnp.exp(last-cum)],axis=0),ee)
    dte,ecum,etail=sprd[:Q],sprd[Q:2*Q],sprd[2*Q:]
    x=v*dte
    g=mm(cc,b,1,1)
    gt=mm(b,cc,1,1)
    parts=[]
    for p in range(VW//128):
        ws=[]
        for h in (2*p,2*p+1):
            d=jnp.where(low,cum[:,h:h+1]-cum_t[h:h+1,:],NEG)
            ws.append((jnp.exp(d)*g).astype(bf16))
            lt=jnp.exp(jnp.where(up,cum_t[h:h+1,:]-cum[:,h:h+1],NEG))
            lt_ref[:,h*Q:(h+1)*Q]=lt
            wt_ref[:,h*Q:(h+1)*Q]=(lt*gt).astype(bf16)
        parts.append(mm(jnp.concatenate(ws,axis=1),halves(x[:,128*p:128*p+128])))
    s=s_ref[...]
    sp_ref[0]=s
    y_ref[...]=jnp.concatenate(parts,axis=1)+ecum*mm(cc,s.astype(bf16))+par_ref[7:8,:VW]*v
    s_ref[...]=ecum[Q-1:Q,:]*s+mm(b,(x*etail).astype(bf16),0,0)

def bwd_kernel(c0,nc,nall,first_ref,raw_ref,act_ref,sl_ref,y_ref,dy_ref,sp_ref,wt_ref,lt_ref,par_ref,*rest):
    out_ref,ds_ref,sn_ref,h_ref,acc_ref,acs_ref,ext,ee_ref,hh_ref=rest[-9:]
    ck_ref=par_ref
    i=pl.program_id(0)
    @pl.when(i==0)
    def _():
        ee_ref[...]=spread_matrix(ee_ref.shape)
        hh_ref[...]=sum_matrix(hh_ref.shape)
        for k,ref in enumerate((ds_ref,sn_ref,h_ref,acc_ref,acs_ref)):
            ref[...]=jnp.zeros_like(ref) if c0+nc==nall else rest[k][...]
    c=c0+nc-1-i
    nxt=jnp.minimum(c+1,nall-1)
    start=(first_ref[nxt//(SPAN//Q)]==1)&(nxt%(SPAN//Q)==0)
    @pl.when(start)
    def _():
        ds_ref[...]=jnp.zeros_like(ds_ref); h_ref[...]=jnp.zeros_like(h_ref)
    act=act_ref[...]
    v=act[:,:VW]; bf=act[:,VW:VW+NS]; cf=act[:,VW+NS:]
    b=bf.astype(bf16); cc=cf.astype(bf16)
    z=raw_ref[:,CW:]+par_ref[5:6,:128]
    dt=softplus(z)
    edl=jnp.exp(par_ref[6:7,:128])
    a=-dt*edl
    row,col=iotas()
    low=row>=col; up=row<=col
    cum=tri_sum(jnp.where(low,1.0,0.0).astype(bf16),a)
    last=cum[Q-1:Q,:]
    ee=ee_ref[...]
    sprd=spread(jnp.concatenate([dt,jnp.exp(cum),jnp.exp(last-cum)],axis=0),ee)
    dte,ecum,etail=sprd[:Q],sprd[Q:2*Q],sprd[2*Q:]
    x=v*dte
    xb=x.astype(bf16)
    dy=dy_ref[...].astype(f32)
    dyb=dy.astype(bf16)
    dgt=jnp.zeros((Q,Q),f32)
    parts=[]
    for p in range(VW//128):
        cols=slice(128*p,128*p+128)
        dyh,dyl=split2(dy[:,cols])
        xh,xl=halves2(x[:,cols])
        dw=mm(jnp.concatenate([xh,xl,xh],axis=1),jnp.concatenate([dyh,dyh,dyl],axis=1),1,1)
        for k in (0,1):
            h=2*p+k
            dgt=dgt+lt_ref[:,h*Q:(h+1)*Q]*dw[k*Q:(k+1)*Q]
        parts.append(mm(wt_ref[:,2*Q*p:2*Q*(p+1)],halves(dy[:,cols])))
    ds=ds_ref[...]
    dsb=ds.astype(bf16)
    s=sp_ref[0]
    dxd=jnp.concatenate(parts,axis=1)
    bds=mm(b,dsb)
    dx=dxd+etail*bds
    xe=(x*etail).astype(bf16)
    dye=dy*ecum
    db=mm3(dgt,cf)+mm3(x*etail,ds,1,1)
    dc=mm3(dgt,bf,0,0)+mm3(dye,s,1,1)
    kk=jnp.sum(dsb.astype(f32)*sn_ref[...],axis=0,keepdims=True)
    rh,rl=split2(dyb.astype(f32)*(y_ref[...]-par_ref[7:8,:VW]*v)-xb.astype(f32)*dxd-xe.astype(f32)*bds)
    kh,kl=split2(jnp.concatenate([kk,jnp.zeros((7,VW),f32)],axis=0))
    hs=mm(jnp.concatenate([rh,rl,(v*dx).astype(bf16),jnp.concatenate([kh,kl],axis=0)],axis=0),hh_ref[...])
    dcum,q,k0=hs[:Q]+hs[Q:2*Q],hs[2*Q:3*Q],hs[3*Q:3*Q+1]+hs[3*Q+8:3*Q+9]
    da=k0+tri_sum(jnp.where(up,1.0,0.0).astype(bf16),dcum)
    dst=(q-da*edl)*sig(z)
    ds_ref[...]=ecum[Q-1:Q,:]*ds+mm3(cf,dye,0,0)
    sn_ref[...]=s
    acs_ref[0:1,:]+=jnp.sum(da*a,axis=0,keepdims=True)
    acs_ref[1:2,:]+=jnp.sum(dst,axis=0,keepdims=True)
    dv=dte*dx+par_ref[7:8,:VW]*dy
    acc_ref[5:6,:VW]+=jnp.sum(dy*v,axis=0,keepdims=True)
    dpre=jnp.concatenate([dv,db,dc],axis=1)*sl_ref[...]
    ext[0:Q,:]=dpre
    ext[Q:Q+8,:]=h_ref[...]
    h_ref[...]=dpre[0:8,:]
    xr=raw_ref[:,:CW]
    draw=ck_ref[3:4,:]*dpre
    acc_ref[3:4,:]+=jnp.sum(dpre*xr,axis=0,keepdims=True)
    acc_ref[4:5,:]+=jnp.sum(dpre,axis=0,keepdims=True)
    for j in (1,2,3):
        sh=ext[j:j+Q,:]
        draw=draw+ck_ref[3-j:4-j,:]*sh
        acc_ref[3-j:4-j,:]+=jnp.sum(sh*xr,axis=0,keepdims=True)
    out_ref[:,:CW]=draw.astype(bf16)
    out_ref[:,CW:]=dst.astype(bf16)

def sd(shape,dt=f32): return jax.ShapeDtypeStruct(shape,dt)

def hbm(shape,dt=f32): return pltpu.HBM(shape,dt)

def vmem(shape,dt=f32): return pltpu.VMEM(shape,dt)

def near_by(x): return pltpu.with_memory_space_constraint(x,pltpu.VMEM)

def stay(x): return pltpu.with_memory_space_constraint(x,pltpu.HBM)

def whole(shape): return pl.BlockSpec(shape,lambda i,*_: (0,)*len(shape))

def once(shape): return pl.BlockSpec(shape,lambda i,*_: (0,)*len(shape),pipeline_mode=pl.Buffered(1))

HL=VW//HW

def ssd_fwd(c0,nc,nall,first,raw,par,carry):
    rb=lambda w: pl.BlockSpec((Q,w),lambda i,*_: (c0+i,0))
    any_spec=pl.BlockSpec(memory_space=pl.ANY)
    held=[whole((NS,VW)),whole((8,CW))]
    return pl.pallas_call(partial(fwd_kernel,c0,nc),
        out_shape=(vmem((nall*Q,VW)),hbm((nall*Q,CW)),hbm((nall*Q,CW)),hbm((nall,NS,VW)),hbm((nall*Q,HL*Q),bf16),hbm((nall*Q,HL*Q)),sd((NS,VW)),sd((8,CW))),
        grid_spec=pltpu.PrefetchScalarGridSpec(num_scalar_prefetch=1,grid=(nc,),
            in_specs=[rb(RW),once((8,CW))]+(held+[any_spec]*6 if carry else []),
            out_specs=(rb(VW),rb(CW),rb(CW),pl.BlockSpec((1,NS,VW),lambda i,*_: (c0+i,0,0)),rb(HL*Q),rb(HL*Q),*held),
            scratch_shapes=[pltpu.VMEM((Q+8,CW),f32),pltpu.VMEM((256,VW),bf16)]),
        input_output_aliases={5+k:k for k in range(6)} if carry else {},
        compiler_params=pltpu.CompilerParams(vmem_limit_bytes=FWD_LIMIT),
        cost_estimate=pl.CostEstimate(flops=int(1.5e9*nc/8),bytes_accessed=30_000_000*nc//8,transcendentals=3_000_000*nc//8),
        name=f"ssd_forward_{c0}")(first,stay(raw),par,*(carry[6:]+(near_by(carry[0]),)+tuple(stay(x) for x in carry[1:6]) if carry else ()))

def ssd_bwd(c0,nc,nall,first,raw,act,sl,y,dy,sp,wt,lt,par,carry):
    rv=lambda w: pl.BlockSpec((Q,w),lambda i,*_: (c0+nc-1-i,0))
    any_spec=pl.BlockSpec(memory_space=pl.ANY)
    held=[whole((NS,VW)),whole((NS,VW)),whole((8,CW)),whole((8,CW)),whole((8,128))]
    return pl.pallas_call(partial(bwd_kernel,c0,nc,nall),
        out_shape=(vmem((nall*Q,RW),bf16),hbm((NS,VW)),hbm((NS,VW)),sd((8,CW)),sd((8,CW)),sd((8,128))),
        grid_spec=pltpu.PrefetchScalarGridSpec(num_scalar_prefetch=1,grid=(nc,),
            in_specs=[rv(RW),rv(CW),rv(CW),rv(VW),rv(VW),pl.BlockSpec((1,NS,VW),lambda i,*_: (c0+nc-1-i,0,0)),rv(HL*Q),rv(HL*Q),once((8,CW))]
                     +(held+[any_spec] if carry else []),
            out_specs=(rv(RW),*held),
            scratch_shapes=[pltpu.VMEM((Q+8,CW),f32),pltpu.VMEM((256,VW),bf16),pltpu.VMEM((VW,128),bf16)]),
        input_output_aliases={15:0} if carry else {},
        compiler_params=pltpu.CompilerParams(vmem_limit_bytes=BACK_LIMIT),
        cost_estimate=pl.CostEstimate(flops=int(3e9*nc/8),bytes_accessed=60_000_000*nc//8,transcendentals=4_000_000*nc//8),
        name=f"ssd_backward_{c0}")(first,stay(raw),stay(act),stay(sl),near_by(y),near_by(dy),stay(sp),stay(wt),stay(lt),par,*((stay(carry[1]),stay(carry[2]))+carry[3:]+(near_by(carry[0]),) if carry else ()))


D = 1536
H = 48
E = 3072
TOK_DEV = 1024
SEQ_DEV = 4
EPSILON = 1e-05
FWD_PARTS = ((0, 4), (4, 4))
BACK_PARTS = ((5, 3), (2, 3), (0, 2))


def contract(left, right, left_dim, right_dim, out=f32):
    return lax.dot_general(
        left, right, (((left_dim,), (right_dim,)), ((), ())), preferred_element_type=f32
    ).astype(out)


def span_layout(seq_lengths, seq_device, seq_offset, device):
    span_index = jnp.arange(SEQ_DEV, dtype=jnp.int32)
    needed = (seq_lengths + SPAN - 1) // SPAN
    owned_seq = (seq_device == device) & (seq_lengths > 0)
    relative = span_index[None, :] - seq_offset[:, None]
    inside = owned_seq[:, None] & (relative >= 0) & (relative < needed[:, None])
    live_rows = jnp.sum(
        jnp.where(inside, jnp.clip(seq_lengths[:, None] - relative * SPAN, 0, SPAN), 0), axis=0
    )
    seq_first = jnp.any(inside & (relative == 0), axis=0)
    return live_rows, seq_first.astype(jnp.int32)


def ring_order(count):
    if count == 8:
        return [0, 2, 4, 6, 7, 5, 3, 1]
    return list(range(count))


def lay(cols, rows, off_ref, refs, out):
    for k, (c0, w) in enumerate(cols):
        out[pl.ds(pl.multiple_of(off_ref[k] * rows, 16), rows), c0 : c0 + w] = refs[k][...]


def row_sums(x):
    a, b = split2(x)
    ones = jnp.ones((8, x.shape[1]), bf16)
    return mm(ones, a, 1, 1) + mm(ones, b, 1, 1)


def project_kernel(cols, rows, nx, off_ref, *refs):
    n = len(cols)
    xs = refs[n : n + nx]
    w_ref, x_ref, xt_ref, raw_ref = refs[n + nx :]
    i = pl.program_id(0)

    @pl.when(i == 0)
    def _():
        w_ref[:, CW:] = jnp.zeros((w_ref.shape[0], RW - CW), bf16)
        lay(cols, rows, off_ref, refs, w_ref)

    for k in range(nx):

        @pl.when(i == k)
        def _(k=k):
            x_ref[...] = xs[k][...]

    xt_ref[...] = x_ref[...].T
    raw_ref[...] = mm(x_ref[...], w_ref[...])


def project(pieces, offsets, xs, total):
    rows, n = pieces[0][0].shape[0], len(pieces)
    cols = [(c0, x.shape[1]) for x, c0 in pieces]
    width = RW
    q, depth = xs[0].shape
    nx = len(xs)
    at = lambda w: pl.BlockSpec((q, w), lambda i, off: (off[n + i], 0))
    return pl.pallas_call(
        partial(project_kernel, cols, rows, nx),
        out_shape=(hbm((total, width), bf16), sd((q * nx, depth), bf16), sd((depth, q * nx), bf16), hbm((q * nx, width))),
        grid_spec=pltpu.PrefetchScalarGridSpec(
            num_scalar_prefetch=1,
            grid=(nx,),
            in_specs=[once(x.shape) for x, _ in pieces] + [once(x.shape) for x in xs],
            out_specs=(whole((total, width)), at(depth), pl.BlockSpec((depth, q), lambda i, off: (0, off[n + i])), at(width)),
        ),
        compiler_params=pltpu.CompilerParams(vmem_limit_bytes=22 << 20),
        cost_estimate=pl.CostEstimate(flops=2 * q * nx * total * width, bytes_accessed=30_000_000, transcendentals=0),
        name="project",
    )(offsets, *[x for x, _ in pieces], *xs)


def cotangent_kernel(cols, rows, nx, off_ref, *refs):
    n = len(cols)
    xs = refs[n : n + nx]
    normed_ref, ssd_ref, gain_ref, w_ref, gr_ref, by_ref, sum_ref, yr_ref, x_ref = refs[n + nx :]
    i = pl.program_id(0)

    @pl.when(i == 0)
    def _():
        lay(cols, rows, off_ref, refs, w_ref)

    for k in range(nx):

        @pl.when(i == k)
        def _(k=k):
            x_ref[...] = xs[k][...]

    by = mm(x_ref[...], w_ref[:, VW:])
    gr = mm(normed_ref[...], w_ref[:, :VW])
    by_ref[...] = by
    gr_ref[...] = gr
    gated = ssd_ref[...] * (gr * sig(gr))
    scaled = gated * gain_ref[...]
    yr_ref[...] = scaled.astype(bf16)
    square = row_sums(gated * gated)
    cross = row_sums(by * scaled)
    top = lax.broadcasted_iota(jnp.int32, square.shape, 0) == 0
    sum_ref[0] = jnp.where(top, square, cross)


def cotangent(pieces, offsets, xs, normed, ssd, gain, total):
    rows, n = pieces[0][0].shape[0], len(pieces)
    cols = [(c0, x.shape[1]) for x, c0 in pieces]
    width = max(c0 + w for c0, w in cols)
    q, depth = xs[0].shape
    nx = len(xs)
    at = lambda w: pl.BlockSpec((q, w), lambda i, off: (off[n + i], 0))
    return pl.pallas_call(
        partial(cotangent_kernel, cols, rows, nx),
        out_shape=(
            vmem((total, width), bf16),
            sd((q * nx, VW)),
            sd((q * nx, VW)),
            sd((nx, 8, q)),
            sd((q * nx, VW), bf16),
        ),
        grid_spec=pltpu.PrefetchScalarGridSpec(
            num_scalar_prefetch=1,
            grid=(nx,),
            in_specs=[once(x.shape) for x, _ in pieces]
            + [once(x.shape) for x in xs]
            + [at(depth), at(VW), once((1, VW))],
            out_specs=(
                whole((total, width)),
                at(VW),
                at(VW),
                pl.BlockSpec((1, 8, q), lambda i, off: (off[n + i], 0, 0)),
                at(VW),
            ),
            scratch_shapes=[pltpu.VMEM((q, depth), bf16)],
        ),
        compiler_params=pltpu.CompilerParams(vmem_limit_bytes=30 << 20),
        cost_estimate=pl.CostEstimate(flops=2 * q * nx * total * width, bytes_accessed=30_000_000, transcendentals=800_000),
        name="cotangent",
    )(offsets, *[x for x, _ in pieces], *xs, normed, near_by(ssd), gain)


def turn_kernel(nx, off_ref, *refs):
    i = pl.program_id(0)
    for k in range(nx):

        @pl.when(i == k)
        def _(k=k):
            refs[nx][...] = refs[k][...].T


def turn(offsets, xs):
    q, depth = xs[0].shape
    nx = len(xs)
    n = offsets.shape[0] - nx
    return pl.pallas_call(
        partial(turn_kernel, nx),
        out_shape=sd((depth, q * nx), bf16),
        grid_spec=pltpu.PrefetchScalarGridSpec(
            num_scalar_prefetch=1,
            grid=(nx,),
            in_specs=[once(x.shape) for x in xs],
            out_specs=pl.BlockSpec((depth, q), lambda i, off: (0, off[n + i])),
        ),
        compiler_params=pltpu.CompilerParams(vmem_limit_bytes=8 << 20),
        cost_estimate=pl.CostEstimate(flops=0, bytes_accessed=10_000_000, transcendentals=0),
        name="turn",
    )(offsets, *xs)


def gate_kernel(sum_ref, by_ref, gr_ref, ssd_ref, gain_ref, ny_ref, bg_ref, dy_ref, gg_ref):
    @pl.when(pl.program_id(0) == 0)
    def _():
        gg_ref[...] = jnp.zeros_like(gg_ref)

    sums = sum_ref[0].T
    inv = lax.rsqrt(sums[:, 0:1] / E + EPSILON)
    gr, ssd, by, gain = gr_ref[...], ssd_ref[...], by_ref[...], gain_ref[...]
    sg = sig(gr)
    gate = gr * sg
    unit = ssd * gate * inv
    ny_ref[...] = (unit * gain).astype(bf16)
    gg_ref[0:1, :] += jnp.sum(by * unit, axis=0, keepdims=True)
    back = inv * (by * gain - unit * (inv * sums[:, 1:2] / E))
    bg_ref[...] = (back * ssd * (sg * (1.0 + gr - gate))).astype(bf16)
    dy_ref[...] = back * gate


def gate_back(sums, by, gate_raw, ssd, gain):
    t, width = by.shape
    n, _, q = sums.shape
    rb = pl.BlockSpec((q, width), lambda i: (i, 0))
    return pl.pallas_call(
        gate_kernel,
        out_shape=(sd((t, width), bf16), sd((t, width), bf16), vmem((t, width)), sd((8, width))),
        grid=(n,),
        in_specs=[pl.BlockSpec((1, 8, q), lambda i: (i, 0, 0)), rb, rb, rb, once((1, width))],
        out_specs=(rb, rb, rb, whole((8, width))),
        compiler_params=pltpu.CompilerParams(vmem_limit_bytes=12 << 20),
        cost_estimate=pl.CostEstimate(flops=20_000_000, bytes_accessed=15_000_000, transcendentals=800_000),
        name="gate_back",
    )(sums, by, gate_raw, near_by(ssd), gain)


def normed_kernel(
    half, at_ref, first_ref, gate_ref, w_ref, g_ref, x_ref, h_ref, m_ref, s_ref, mk_ref, mn_ref, ma_ref, mb_ref, away_ref, keep_ref, ng_ref, o_ref, scale_ref
):
    i = pl.program_id(0)

    @pl.when(i == 0)
    def _():
        ng_ref[...] = jnp.zeros_like(ng_ref)
        inv = lax.rsqrt(s_ref[0, 0:1, :] / E + EPSILON) * m_ref[...]
        scale_ref[...] = jnp.broadcast_to(inv, (8, inv.shape[1])).T

    n = o_ref.shape[0]
    scale = scale_ref[pl.ds(pl.multiple_of(i * n, 8), n), 0:1]
    far = jnp.where(i < half, ma_ref[...].astype(f32), mb_ref[...].astype(f32))
    mixed = mk_ref[0].astype(f32) + mn_ref[0].astype(f32) + far
    o_ref[...] = h_ref[...] + scale * mixed
    back = mm(first_ref[...], w_ref[...], 1, 1) + mm(gate_ref[...], g_ref[...], 1, 1)
    ng_ref[0:1, :] += jnp.sum(back * x_ref[...].astype(f32), axis=0, keepdims=True)

    @pl.when(i < half)
    def _():
        away_ref[0] = back.astype(bf16)

    @pl.when(i >= half)
    def _():
        keep_ref[0] = back.astype(bf16)


def back_normed_rows(at, q, first, gate, w, gate_w, normed, hidden, mask, sums, keep, near, far):
    depth = normed.shape[1]
    n = at.shape[0]
    half = n // 2
    rb = lambda c: pl.BlockSpec((q, c), lambda i, at: (at[i], 0))
    part = lambda c: pl.BlockSpec((q // n, c), lambda i, at: (i, 0))
    second = pl.BlockSpec((1, q // n, depth), lambda i, at: (1, i, 0))
    return pl.pallas_call(
        partial(normed_kernel, half),
        out_shape=(sd((half, q, depth), bf16), sd((half, q, depth), bf16), sd((8, depth)), sd((q, depth))),
        grid_spec=pltpu.PrefetchScalarGridSpec(
            num_scalar_prefetch=1,
            grid=(n,),
            in_specs=[rb(RW), rb(VW), once(w.shape), once((depth, VW)), rb(depth)]
            + [part(depth), whole((1, q)), pl.BlockSpec((1, 8, q), lambda i, at: (at[n - 1], 0, 0)), second, second]
            + [
                pl.BlockSpec((q // n, depth), lambda i, at: (jnp.minimum(i, half - 1), 0)),
                pl.BlockSpec((q // n, depth), lambda i, at: (jnp.maximum(i - half, 0), 0)),
            ],
            out_specs=(
                pl.BlockSpec((1, q, depth), lambda i, at: (jnp.minimum(i, half - 1), 0, 0)),
                pl.BlockSpec((1, q, depth), lambda i, at: (jnp.maximum(i - half, 0), 0, 0)),
                whole((8, depth)),
                part(depth),
            ),
            scratch_shapes=[pltpu.VMEM((q, 8), f32)],
        ),
        compiler_params=pltpu.CompilerParams(vmem_limit_bytes=22 << 20),
        cost_estimate=pl.CostEstimate(flops=2 * n * q * depth * (RW + VW), bytes_accessed=60_000_000, transcendentals=0),
        name="back_normed",
    )(at, near_by(first), gate, w, near_by(gate_w), normed, hidden, mask, sums, keep, near, *far)


def mixer_kernel(half, at_ref, x_ref, w_ref, away_ref, keep_ref):
    r = mm(x_ref[...], w_ref[...], 1, 1).astype(bf16)
    i = pl.program_id(0)

    @pl.when(i < half)
    def _():
        away_ref[0] = r

    @pl.when(i >= half)
    def _():
        keep_ref[0] = r


def mixer_blocks(at, q, x, w):
    n, depth, width = at.shape[0], w.shape[0], x.shape[1]
    half = n // 2
    return pl.pallas_call(
        partial(mixer_kernel, half),
        out_shape=(sd((half, q, depth), bf16), sd((half, q, depth), bf16)),
        grid_spec=pltpu.PrefetchScalarGridSpec(
            num_scalar_prefetch=1,
            grid=(n,),
            in_specs=[
                pl.BlockSpec((q, width), lambda i, at: (at[i], 0)),
                pl.BlockSpec((depth, width), lambda i, at: (0, 1), pipeline_mode=pl.Buffered(1)),
            ],
            out_specs=(
                pl.BlockSpec((1, q, depth), lambda i, at: (jnp.minimum(i, half - 1), 0, 0)),
                pl.BlockSpec((1, q, depth), lambda i, at: (jnp.maximum(i - half, 0), 0, 0)),
            ),
        ),
        compiler_params=pltpu.CompilerParams(vmem_limit_bytes=12 << 20),
        cost_estimate=pl.CostEstimate(flops=2 * n * q * depth * width, bytes_accessed=20_000_000, transcendentals=0),
        name="mixer_rows",
    )(at, x, near_by(w))


def grad_kernel(per, rows, at_ref, xt_ref, back_ref, out_ref):
    i = pl.program_id(0)
    r = mm(xt_ref[...], back_ref[...]).astype(bf16)
    for d in range(per):
        out_ref[pl.ds(at_ref[i * per + d], 1)] = r[d * rows : (d + 1) * rows][None]


def weight_grad(at, xt, back, n_dp):
    depth, t = xt.shape
    rows, width = depth // n_dp, back.shape[1]
    steps = 2
    return pl.pallas_call(
        partial(grad_kernel, n_dp // steps, rows),
        out_shape=sd((n_dp, rows, width), bf16),
        grid_spec=pltpu.PrefetchScalarGridSpec(
            num_scalar_prefetch=1,
            grid=(steps,),
            in_specs=[pl.BlockSpec((depth // steps, t), lambda i, at: (i, 0)), once(back.shape)],
            out_specs=whole((n_dp, rows, width)),
        ),
        compiler_params=pltpu.CompilerParams(vmem_limit_bytes=20 << 20),
        cost_estimate=pl.CostEstimate(flops=2 * depth * t * width, bytes_accessed=8_000_000, transcendentals=0),
        name="weight_grad",
    )(at, xt, near_by(back))


def far_pair_kernel(at_ref, xt_ref, back_ref, zt_ref, y_ref, f_ref, b_ref):
    f_ref[...] = mm(xt_ref[...], back_ref[...]).astype(bf16)
    b_ref[...] = mm(zt_ref[...], y_ref[...]).astype(bf16)


def far_value_kernel(mid, at_ref, xt_ref, back_ref, f_ref, b_ref):
    r = mm(xt_ref[...], back_ref[...]).astype(bf16)
    f_ref[...] = r[:, :mid]
    b_ref[...] = r[:, mid:]


def far_grad(at, rows, pairs, mid=0):
    depth, t = pairs[0][0].shape
    block = pl.BlockSpec((rows, t), lambda i, at: (at[0], 0))
    specs, args = [], []
    for xt, back in pairs:
        specs += [block, once(back.shape)]
        args += [xt, back]
    widths = (mid, pairs[0][1].shape[1] - mid) if mid else tuple(b.shape[1] for _, b in pairs)
    return pl.pallas_call(
        partial(far_value_kernel, mid) if mid else far_pair_kernel,
        out_shape=tuple(sd((rows, w), bf16) for w in widths),
        grid_spec=pltpu.PrefetchScalarGridSpec(
            num_scalar_prefetch=1,
            grid=(1,),
            in_specs=specs,
            out_specs=tuple(whole((rows, w)) for w in widths),
        ),
        compiler_params=pltpu.CompilerParams(vmem_limit_bytes=12 << 20),
        cost_estimate=pl.CostEstimate(flops=2 * rows * t * sum(widths), bytes_accessed=4_000_000, transcendentals=0),
        name="far_grad",
    )(at, *args)


def pair_grad_kernel(per, rows, at_ref, xt_ref, back_ref, zt_ref, y_ref, out_ref):
    i = pl.program_id(0)
    for k, r in enumerate((mm(xt_ref[...], back_ref[...]), mm(zt_ref[...], y_ref[...]))):
        r = r.astype(bf16)
        for d in range(per):
            out_ref[pl.ds(at_ref[i * per + d], 1), :, k * VW : (k + 1) * VW] = r[d * rows : (d + 1) * rows][None]


def pair_grad(at, xt, back, zt, y, n_dp):
    depth, t = xt.shape
    rows, steps = depth // n_dp, 4
    rb = pl.BlockSpec((depth // steps, t), lambda i, at: (i, 0))
    return pl.pallas_call(
        partial(pair_grad_kernel, n_dp // steps, rows),
        out_shape=sd((n_dp, rows, 2 * VW), bf16),
        grid_spec=pltpu.PrefetchScalarGridSpec(
            num_scalar_prefetch=1,
            grid=(steps,),
            in_specs=[rb, once(back.shape), rb, once(y.shape)],
            out_specs=whole((n_dp, rows, 2 * VW)),
        ),
        compiler_params=pltpu.CompilerParams(vmem_limit_bytes=22 << 20),
        cost_estimate=pl.CostEstimate(flops=4 * depth * t * VW, bytes_accessed=14_000_000, transcendentals=0),
        name="pair_grad",
    )(at, xt, back, zt, y)


def finish_kernel(
    x_ref, f_ref, b_ref, g_ref, small_ref, gv_ref, steps_ref, taps_ref, bias_ref, gain_ref, sb_ref, dl_ref, skip_ref
):
    value = x_ref[...].astype(f32) + f_ref[...].astype(f32) + b_ref[...].astype(f32)
    gv_ref[:, 0, :] = g_ref[...]
    gv_ref[:, 1, :] = value[:, :VW]
    heads = sb_ref.shape[0]
    steps_ref[...] = value[:, CW:].T[:heads, :]
    taps_ref[...] = small_ref[0:4, :VW]
    bias_ref[...] = small_ref[4, :VW]
    gain_ref[...] = small_ref[6, :VW]
    dl_ref[...] = small_ref[6, VW : VW + heads]
    sb_ref[...] = small_ref[6, VW + 128 : VW + 128 + heads]
    parts = jnp.concatenate(split3(small_ref[0:8, :VW]), axis=0)
    sums = mm(parts, sum_matrix((VW, 128)))
    skip_ref[...] = (sums[5:6] + sums[13:14] + sums[21:22])[0, :heads]


def finish(x, f, b, pair_out, small, heads):
    rows, width = x.shape
    full = whole((rows, width))
    outs = ((rows, 2, VW), (heads, rows), (4, VW), (VW,), (VW,), (heads,), (heads,), (heads,))
    return pl.pallas_call(
        finish_kernel,
        out_shape=tuple(sd(o) for o in outs),
        grid=(1,),
        in_specs=[full, full, full, pl.BlockSpec((rows, VW), lambda i: (0, 0)), whole(small.shape)],
        out_specs=tuple(whole(o) for o in outs),
        compiler_params=pltpu.CompilerParams(vmem_limit_bytes=16 << 20),
        cost_estimate=pl.CostEstimate(flops=1_000_000, bytes_accessed=5_000_000, transcendentals=0),
        name="finish",
    )(stay(x), stay(f), stay(b), stay(pair_out), small)


class Ring:
    def __init__(self, count):
        self.count = count
        self.half = count // 2
        self.order = ring_order(count)
        at = {d: i for i, d in enumerate(self.order)}
        self.table = [[self.order[(at[d] + k) % count] for k in range(count)] for d in range(count)]
        self.ahead = [(self.order[i], self.order[(i + 1) % count]) for i in range(count)]
        self.back = [(b, a) for a, b in self.ahead]

    def rows_of(self, table):
        return jnp.asarray(table, jnp.int32)[lax.axis_index("dp")]

    def hop(self, f, b):
        return lax.ppermute(f, "dp", self.ahead), lax.ppermute(b, "dp", self.back)


class Gather:
    def __init__(self, ring, x, c0=0):
        self.ring, self.mid, self.c0 = ring, x.shape[1] // 2 // 128 * 128, c0
        self.pieces, self.f, self.b, self.s = [(x, c0)], x, x, 0

    def ready(self):
        if self.s == self.ring.half - 1:
            return [self.f[:, : self.mid], self.b[:, self.mid :]]
        return [self.f, self.b]

    def step(self, f, b):
        self.s += 1
        self.f, self.b = self.ring.hop(f, b)
        self.pieces += [(self.f, self.c0), (self.b, self.c0 + (self.mid if self.s == self.ring.half else 0))]

    @staticmethod
    def offsets(ring):
        ahead = [0]
        for s in range(1, ring.half + 1):
            ahead += [ring.count - s, s]
        return [[ring.table[d][k] for k in ahead] for d in range(ring.count)]


class Scatter:
    def __init__(self, ring, first):
        self.ring, self.first, self.x, self.s = ring, list(first), None, ring.half

    def ready(self):
        x, s = self.x, self.s
        if s == self.ring.half:
            return self.first
        f, b = self.f, self.b
        if s == self.ring.half - 1:
            f = jnp.pad(f, ((0, 0), (0, x.shape[2] - f.shape[1])))
            b = jnp.pad(b, ((0, 0), (x.shape[2] - b.shape[1], 0)))
        f = x[s].astype(f32) + f.astype(f32)
        b = x[self.ring.count - s].astype(f32) + b.astype(f32)
        return [f.astype(bf16), b.astype(bf16)]

    def step(self, f, b):
        self.f, self.b = self.ring.hop(f, b)
        self.s -= 1

    def total(self, columns=slice(None)):
        return self.x[0, :, columns].astype(f32) + self.f[:, columns].astype(f32) + self.b[:, columns].astype(f32)


def swap(x, axis, count, bits):
    return lax.ppermute(x, axis, [(i, i ^ bits) for i in range(count)])


def tensor_order(count):
    keys = [0]
    bit = count // 2
    while bit:
        keys += [k ^ bit for k in keys]
        bit //= 2
    return keys


def pick(x, index, axis=0):
    return lax.dynamic_index_in_dim(x, index, axis, keepdims=False)


def groups_of(count):
    bits = [1 << k for k in range(count.bit_length() - 1)]
    first = len(bits) % 2
    return ([bits[:first]] if first else []) + [bits[k : k + 2] for k in range(first, len(bits), 2)]


def others(bits):
    return [bits[0]] if len(bits) == 1 else [bits[0], bits[1], bits[0] | bits[1]]


class Spread:
    def __init__(self, x, axis, count):
        self.x, self.axis, self.count, self.groups = x, axis, count, groups_of(count)

    def step(self, x):
        bits = self.groups.pop(0)
        self.x = sum((swap(x, self.axis, self.count, k) for k in others(bits)), x)


def together(*lists):
    flat = lax.optimization_barrier(tuple(x for xs in lists for x in xs))
    out, at = [], 0
    for xs in lists:
        out.append(list(flat[at : at + len(xs)]))
        at += len(xs)
    return out


def body(
    n_dp,
    n_tensor,
    hidden_in,
    norm_gain,
    gate_value_weight,
    state_proj_weight,
    step_weight,
    conv_value_kernel,
    conv_value_bias,
    conv_state_kernel,
    conv_state_bias,
    step_bias,
    decay_log,
    skip_scale,
    gate_norm_gain,
    out_weight,
    out_cotangent,
    seq_lengths,
    seq_device,
    seq_offset,
):
    quarter = hidden_in.shape[0]
    heads = step_weight.shape[1]
    rows = gate_value_weight.shape[0]
    me, dp = lax.axis_index("tensor"), lax.axis_index("dp")
    ring = Ring(n_dp)
    plan = [
        [ring.table[d].index(k) for k in range(n_dp)] + [ring.table[d][ring.half]] + Gather.offsets(ring)[d]
        for d in range(n_dp)
    ]
    plan = ring.rows_of(plan)
    ring_at, far_at = plan[:n_dp], plan[n_dp : n_dp + 1]
    order = me ^ jnp.asarray([3, 1, 2, 0], jnp.int32)
    offsets = jnp.concatenate([plan[n_dp + 1 :], me ^ jnp.asarray(tensor_order(n_tensor), jnp.int32)])
    to_core = lambda x: swap(x, "tensor", n_tensor, 1)
    to_far = lambda x: swap(x, "tensor", n_tensor, 2)

    live_rows, seq_first = span_layout(seq_lengths, seq_device, seq_offset, dp)
    row = me * quarter + jnp.arange(quarter, dtype=jnp.int32)
    local_live = jnp.sum(
        jnp.where((row // SPAN)[:, None] == jnp.arange(SEQ_DEV)[None, :], live_rows[None, :], 0), axis=1
    )
    local_mask = (row % SPAN < local_live).astype(f32)

    pad_to = lambda x, w: jnp.pad(x, (0, w - x.shape[0]))[None]
    params = jnp.concatenate(
        [
            jnp.concatenate([conv_value_kernel, conv_state_kernel], axis=0).T,
            jnp.concatenate([conv_value_bias, conv_state_bias])[None],
            pad_to(step_bias, CW),
            pad_to(decay_log, CW),
            pad_to(jnp.repeat(skip_scale, HW), CW),
        ],
        axis=0,
    )
    gain = gate_norm_gain[None]
    zeros = lambda *s: jnp.zeros(s, f32)

    first_own = jnp.concatenate(
        [gate_value_weight[:, 1, :], state_proj_weight, jnp.pad(step_weight, ((0, 0), (0, 16 - heads)))], axis=1
    )
    first_own, hidden, later = lax.optimization_barrier((first_own, hidden_in, gate_value_weight))
    inv_rms = lax.rsqrt(jnp.mean(hidden * hidden, axis=-1) + EPSILON)
    scaled = hidden * inv_rms[:, None]
    normed_local = (scaled * norm_gain[None, :]).astype(bf16)
    first = Gather(ring, first_own)
    first.step(*first.ready())
    far = to_far(normed_local)
    out_own = jnp.concatenate([later[:, 0, :], out_weight], axis=1)
    back_local = (local_mask[:, None] * out_cotangent).astype(bf16)
    (out_own, offsets, ring_at, far_at, order, seq_first, params, back_local) = lax.optimization_barrier(
        (out_own, offsets, ring_at, far_at, order, seq_first, params, back_local)
    )
    out = Gather(ring, out_own)
    for s in range(1, ring.half):
        extra = []
        if s == min(2, ring.half - 1):
            extra = [[normed_local, far]]
        elif s == ring.half - 1:
            extra = [[back_local] + normed_parts[2:]]
        sends = together(first.ready(), *extra)
        first.step(*sends.pop(0))
        if s == min(2, ring.half - 1):
            [a, far] = sends.pop(0)
            normed_parts = [a, far, to_core(a), to_core(far)]
        elif s == ring.half - 1:
            [back_local, *normed_parts[2:]] = sends.pop(0)
            back_far = to_far(back_local)
    ps, os = together([x for x, _ in first.pieces] + normed_parts, out.ready())
    out.step(*os)
    n = len(first.pieces)
    first_w, normed, normed_t, raw = project(
        [(x, c0) for x, (_, c0) in zip(ps, first.pieces)], offsets, ps[n:], D
    )
    chunks = TOK_DEV // Q
    carry = ()
    for k, (c0, n) in enumerate(FWD_PARTS):
        held, os, bs = together([carry[6]] if carry else [raw], out.ready(), [back_local, back_far] if k == 0 else [])
        out.step(*os)
        if k:
            carry = carry[:6] + (held[0],) + carry[7:]
        else:
            raw = held[0]
            back_parts = bs + [to_core(x) for x in bs]
        carry = tuple(ssd_fwd(c0, n, chunks, seq_first, raw, params, carry))
    held, os, back_parts = together([carry[0]], out.ready(), back_parts)
    carry = (held[0],) + carry[1:]
    out.step(*os)
    back_t = turn(offsets, back_parts)
    while out.s < ring.half:
        out.step(*out.ready())
    ssd, act, slope, states, weights_t, decays_t = carry[:6]

    out_w, gate_raw, back_y, sums, gated = cotangent(
        out.pieces, offsets, back_parts, normed, ssd, gain, D
    )
    total = Spread(sums, "tensor", n_tensor)
    while total.groups:
        total.step(total.x)
    sums = total.x
    mixer = mixer_blocks(order, quarter, gated, out_w)
    sums, mixer_away, mixer_keep = lax.optimization_barrier((sums, *mixer))
    normed_y, back_gate, back_ssd, gain_grad = gate_back(sums, back_y, gate_raw, ssd, gain)
    pair_sum = Scatter(ring, far_grad(far_at, rows, [(normed_t, back_gate), (back_t, normed_y)]))
    ps, [away, mixer_keep, back_gate, normed_y] = together(
        pair_sum.ready(), [mixer_away, mixer_keep, back_gate, normed_y]
    )
    pair_sum.step(*ps)
    mixer_near = to_core(away)
    pair_sum.x = pair_grad(ring_at, normed_t, back_gate, back_t, normed_y, n_dp)
    [pair_sum.f, pair_sum.b, pair_sum.x, mixer_near], = together([pair_sum.f, pair_sum.b, pair_sum.x, mixer_near])

    half_rows = quarter // 2
    away = (mixer_keep[0].astype(f32) + mixer_near[0].astype(f32)).astype(bf16)
    away = [away[:half_rows], away[half_rows:]]
    carry, held, mixer_far = (), [back_ssd], []
    for k, (c0, n) in enumerate(BACK_PARTS):
        ps = pair_sum.ready() if pair_sum.s else []
        held, ps, ms = together(held, ps, away[k : k + 1])
        if carry:
            carry = carry[:1] + (held[0],) + carry[2:]
        else:
            back_ssd = held[0]
        if pair_sum.s:
            pair_sum.step(*ps)
        ms = [to_far(x) for x in ms]
        carry = tuple(
            ssd_bwd(
                c0, n, chunks, seq_first, raw, act, slope, ssd, back_ssd, states, weights_t, decays_t, params, carry
            )
        )
        last = k == len(BACK_PARTS) - 1
        held, [pair_sum.f, pair_sum.b], ms = together([carry[0 if last else 1]], [pair_sum.f, pair_sum.b], ms)
        mixer_far += ms
    carry = (held[0],) + carry[1:]
    while pair_sum.s:
        pair_sum.step(*pair_sum.ready())
    back_first, _, _, _, acc, acs = carry
    value_sum = Scatter(ring, far_grad(far_at, rows, [(normed_t, back_first)], RW // 2 // 128 * 128))
    vs, [back_first] = together(value_sum.ready(), [back_first])
    value_sum.step(*vs)
    value_sum.x = weight_grad(ring_at, normed_t, back_first, n_dp)
    [value_sum.f, value_sum.b, value_sum.x, back_first], = together(
        [value_sum.f, value_sum.b, value_sum.x, back_first]
    )
    vs, [back_first] = together(value_sum.ready(), [back_first])
    value_sum.step(*vs)
    away, keep, ng, output = back_normed_rows(
        order, quarter, back_first, back_gate, first_w, out_w, normed, hidden_in, local_mask[None], sums, mixer_keep, mixer_near, mixer_far
    )
    [value_sum.f, value_sum.b, away, keep, ng], = together([value_sum.f, value_sum.b, away, keep, ng])
    shared = jnp.concatenate([acc[:5, VW:], (ng[0] / norm_gain).reshape(6, 256), zeros(5, 256)], axis=0)
    shared = Spread(shared, "tensor", n_tensor)
    vs, cs, ps = together(value_sum.ready(), [away], [shared.x])
    value_sum.step(*vs)
    near = to_core(cs[0])
    away = (keep[0].astype(f32) + near[0].astype(f32)).astype(bf16)
    got = to_far(away[:half_rows])
    shared.step(ps[0])
    [value_sum.f, value_sum.b, near, away, got, shared.x], = together(
        [value_sum.f, value_sum.b, near, away, got, shared.x]
    )
    own = jnp.concatenate(
        [acc[:6], jnp.concatenate([gain_grad[0], acs[0], acs[1]])[None], zeros(1, CW)], axis=0
    )
    while shared.groups:
        shared.step(shared.x)
    small = Spread(jnp.concatenate([own, shared.x.reshape(4, CW)], axis=0), "dp", n_dp)
    vs, cs, ps = together(value_sum.ready(), [away[half_rows:]], [small.x])
    value_sum.step(*vs)
    cs = [got, to_far(cs[0])]
    small.step(ps[0])
    while value_sum.s:
        value_sum.step(*value_sum.ready())
    [value_sum.f, value_sum.b, small.x], cs = together([value_sum.f, value_sum.b, small.x], cs)
    state_grad = value_sum.total(slice(VW, CW)).reshape(n_tensor, rows // n_tensor, 2 * NS)
    ps, ss = together([small.x], [pick(state_grad, me ^ k) for k in range(n_tensor)])
    state_out = sum((swap(ss[k], "tensor", n_tensor, k) for k in range(1, n_tensor)), ss[0])
    small.x = ps[0]
    while small.groups:
        small.step(small.x)
    small = small.x
    pair_out = pair_sum.total()
    gv_out, step_out, taps, bias, gains, steps, decays, skips = finish(
        value_sum.x[0], value_sum.f, value_sum.b, pair_out, small, heads
    )
    back_rows = keep[1].astype(f32) + near[1].astype(f32) + jnp.concatenate(cs, axis=0).astype(f32)
    back_scaled = back_rows * norm_gain[None, :]
    hidden_gradient = out_cotangent + inv_rms[:, None] * (
        back_scaled - scaled * jnp.mean(back_scaled * scaled, axis=-1)[:, None]
    )
    shared = small[8:].reshape(16, 256)
    index = dp * n_tensor + me
    all_count = n_dp * n_tensor
    kern_share = 2 * NS // all_count
    state_kernel_out = lax.dynamic_slice(shared, (0, index * kern_share), (5, kern_share))
    norm_out = lax.dynamic_slice(shared[5:11].reshape(D), (index * (D // all_count),), (D // all_count,))
    return (
        output,
        hidden_gradient,
        norm_out,
        gv_out,
        state_out,
        step_out.T,
        taps.T,
        bias,
        state_kernel_out[:4].T,
        state_kernel_out[4],
        steps,
        decays,
        skips,
        gains,
        pair_out[:, VW:],
    )


def solution(mesh):
    in_specs = (
        P(("dp", "tensor"), None),
        P(),
        P("dp", None, "tensor"),
        P("dp", None),
        P("dp", "tensor"),
        P("tensor", None),
        P("tensor"),
        P(),
        P(),
        P("tensor"),
        P("tensor"),
        P("tensor"),
        P("tensor"),
        P("dp", "tensor"),
        P(("dp", "tensor"), None),
        P(),
        P(),
        P(),
    )
    out_specs = (
        P(("dp", "tensor"), None),
        P(("dp", "tensor"), None),
        P(("dp", "tensor")),
        P("dp", None, "tensor"),
        P(("dp", "tensor"), None),
        P("dp", "tensor"),
        P("tensor", None),
        P("tensor"),
        P(("dp", "tensor"), None),
        P(("dp", "tensor")),
        P("tensor"),
        P("tensor"),
        P("tensor"),
        P("tensor"),
        P("dp", "tensor"),
    )
    return jax.shard_map(
        partial(body, mesh.shape["dp"], mesh.shape["tensor"]),
        mesh=mesh,
        in_specs=in_specs,
        out_specs=out_specs,
        check_vma=False,
    )
```

```python
from functools import partial

import jax, jax.numpy as jnp
from jax import lax
from jax.experimental import pallas as pl
from jax.experimental.pallas import tpu as pltpu
from jax.sharding import PartitionSpec as P
f32=jnp.float32; bf16=jnp.bfloat16
Q=128
NS=128
VW=768
HW=64
CW=1024
RW=1152
SPAN=256
FWD_LIMIT=12<<20
BACK_LIMIT=16<<20
NEG=-1e30

def mm(a,b,ca=1,cb=0):
    return lax.dot_general(a,b,(((ca,),(cb,)),((),())),preferred_element_type=f32)

def split2(x):
    hi=x.astype(bf16); return hi,(x-hi.astype(f32)).astype(bf16)

def split3(x):
    hi=x.astype(bf16); r=x-hi.astype(f32); mid=r.astype(bf16); return hi,mid,(r-mid.astype(f32)).astype(bf16)

def mm3(a,b,ca=1,cb=0):
    ah,al=split2(a); bh,bl=split2(b)
    return mm(jnp.concatenate([ah,ah,al],axis=ca),jnp.concatenate([bh,bl,bh],axis=cb),ca,cb)

def tri_sum(tri,x):
    a,b,c=split3(x); w=x.shape[1]
    p=mm(tri,jnp.concatenate([a,b,c],axis=1))
    return p[:,:w]+p[:,w:2*w]+p[:,2*w:]

def spread(x,ee):
    a,b=split2(x)
    return mm(jnp.concatenate([a,b],axis=1),ee)

def iotas():
    return lax.broadcasted_iota(jnp.int32,(Q,Q),0),lax.broadcasted_iota(jnp.int32,(Q,Q),1)

def softplus(z):
    return jnp.maximum(z,0.0)+jnp.log(1.0+jnp.exp(-jnp.abs(z)))

def sig(z):
    return 1.0/(1.0+jnp.exp(-z))

def halves(x):
    lane=lax.broadcasted_iota(jnp.int32,x.shape,1)
    lo=jnp.where(lane<HW,x,0.0); hi=jnp.where(lane<HW,0.0,x)
    return jnp.concatenate([lo.astype(bf16),hi.astype(bf16)],axis=0)

def spread_matrix(shape):
    r=lax.broadcasted_iota(jnp.int32,shape,0)%128; c=lax.broadcasted_iota(jnp.int32,shape,1)//HW
    return jnp.where(r==c,1.0,0.0).astype(bf16)

def sum_matrix(shape):
    r=lax.broadcasted_iota(jnp.int32,shape,0)%VW//HW; c=lax.broadcasted_iota(jnp.int32,shape,1)
    return jnp.where(r==c,1.0,0.0).astype(bf16)

def halves2(x):
    lane=lax.broadcasted_iota(jnp.int32,x.shape,1)
    h,l=split2(jnp.concatenate([jnp.where(lane<HW,x,0.0),jnp.where(lane<HW,0.0,x)],axis=0))
    return h,l

def fwd_kernel(c0,nc,first_ref,raw_ref,par_ref,*rest):
    y_ref,act_ref,sl_ref,sp_ref,wt_ref,lt_ref,s_ref,t_ref,ext,ee_ref=rest[-10:]
    ck_ref=par_ref
    i=pl.program_id(0)
    @pl.when(i==0)
    def _():
        ee_ref[...]=spread_matrix(ee_ref.shape)
        if c0:
            s_ref[...]=rest[0][...]; t_ref[...]=rest[1][...]
        else:
            s_ref[...]=jnp.zeros_like(s_ref); t_ref[...]=jnp.zeros_like(t_ref)
    c=c0+i
    start=(first_ref[c//(SPAN//Q)]==1)&(c%(SPAN//Q)==0)
    @pl.when(start)
    def _():
        s_ref[...]=jnp.zeros_like(s_ref); t_ref[...]=jnp.zeros_like(t_ref)
    ext[0:8,:]=t_ref[...]
    x=raw_ref[:,:CW]
    ext[8:8+Q,:]=x
    t_ref[...]=raw_ref[Q-8:Q,:CW]
    pre=par_ref[4:5,:]+ck_ref[3:4,:]*x
    for j in (1,2,3):
        pre=pre+ck_ref[3-j:4-j,:]*ext[8-j:8-j+Q,:]
    sg=sig(pre)
    act=pre*sg
    act_ref[...]=act
    sl_ref[...]=sg*(1.0+pre-act)
    v=act[:,:VW]; b=act[:,VW:VW+NS].astype(bf16); cc=act[:,VW+NS:].astype(bf16)
    dt=softplus(raw_ref[:,CW:]+par_ref[5:6,:128])
    a=-dt*jnp.exp(par_ref[6:7,:128])
    row,col=iotas()
    low=row>=col; up=row<=col
    tri=jnp.where(low,1.0,0.0).astype(bf16)
    cum=tri_sum(tri,a)
    cum_t=cum.T
    last=cum[Q-1:Q,:]
    ee=ee_ref[...]
    sprd=spread(jnp.concatenate([dt,jnp.exp(cum),jnp.exp(last-cum)],axis=0),ee)
    dte,ecum,etail=sprd[:Q],sprd[Q:2*Q],sprd[2*Q:]
    x=v*dte
    g=mm(cc,b,1,1)
    gt=mm(b,cc,1,1)
    parts=[]
    for p in range(VW//128):
        ws=[]
        for h in (2*p,2*p+1):
            d=jnp.where(low,cum[:,h:h+1]-cum_t[h:h+1,:],NEG)
            ws.append((jnp.exp(d)*g).astype(bf16))
            lt=jnp.exp(jnp.where(up,cum_t[h:h+1,:]-cum[:,h:h+1],NEG))
            lt_ref[:,h*Q:(h+1)*Q]=lt
            wt_ref[:,h*Q:(h+1)*Q]=(lt*gt).astype(bf16)
        parts.append(mm(jnp.concatenate(ws,axis=1),halves(x[:,128*p:128*p+128])))
    s=s_ref[...]
    sp_ref[0]=s
    y_ref[...]=jnp.concatenate(parts,axis=1)+ecum*mm(cc,s.astype(bf16))+par_ref[7:8,:VW]*v
    s_ref[...]=ecum[Q-1:Q,:]*s+mm(b,(x*etail).astype(bf16),0,0)

def bwd_kernel(c0,nc,nall,first_ref,raw_ref,act_ref,sl_ref,y_ref,dy_ref,sp_ref,wt_ref,lt_ref,par_ref,*rest):
    out_ref,ds_ref,sn_ref,h_ref,acc_ref,acs_ref,ext,ee_ref,hh_ref=rest[-9:]
    ck_ref=par_ref
    i=pl.program_id(0)
    @pl.when(i==0)
    def _():
        ee_ref[...]=spread_matrix(ee_ref.shape)
        hh_ref[...]=sum_matrix(hh_ref.shape)
        for k,ref in enumerate((ds_ref,sn_ref,h_ref,acc_ref,acs_ref)):
            ref[...]=jnp.zeros_like(ref) if c0+nc==nall else rest[k][...]
    c=c0+nc-1-i
    nxt=jnp.minimum(c+1,nall-1)
    start=(first_ref[nxt//(SPAN//Q)]==1)&(nxt%(SPAN//Q)==0)
    @pl.when(start)
    def _():
        ds_ref[...]=jnp.zeros_like(ds_ref); h_ref[...]=jnp.zeros_like(h_ref)
    act=act_ref[...]
    v=act[:,:VW]; bf=act[:,VW:VW+NS]; cf=act[:,VW+NS:]
    b=bf.astype(bf16); cc=cf.astype(bf16)
    z=raw_ref[:,CW:]+par_ref[5:6,:128]
    dt=softplus(z)
    edl=jnp.exp(par_ref[6:7,:128])
    a=-dt*edl
    row,col=iotas()
    low=row>=col; up=row<=col
    cum=tri_sum(jnp.where(low,1.0,0.0).astype(bf16),a)
    last=cum[Q-1:Q,:]
    ee=ee_ref[...]
    sprd=spread(jnp.concatenate([dt,jnp.exp(cum),jnp.exp(last-cum)],axis=0),ee)
    dte,ecum,etail=sprd[:Q],sprd[Q:2*Q],sprd[2*Q:]
    x=v*dte
    xb=x.astype(bf16)
    dy=dy_ref[...].astype(f32)
    dyb=dy.astype(bf16)
    dgt=jnp.zeros((Q,Q),f32)
    parts=[]
    for p in range(VW//128):
        cols=slice(128*p,128*p+128)
        dyh,dyl=split2(dy[:,cols])
        xh,xl=halves2(x[:,cols])
        dw=mm(jnp.concatenate([xh,xl,xh],axis=1),jnp.concatenate([dyh,dyh,dyl],axis=1),1,1)
        for k in (0,1):
            h=2*p+k
            dgt=dgt+lt_ref[:,h*Q:(h+1)*Q]*dw[k*Q:(k+1)*Q]
        parts.append(mm(wt_ref[:,2*Q*p:2*Q*(p+1)],halves(dy[:,cols])))
    ds=ds_ref[...]
    dsb=ds.astype(bf16)
    s=sp_ref[0]
    dxd=jnp.concatenate(parts,axis=1)
    bds=mm(b,dsb)
    dx=dxd+etail*bds
    xe=(x*etail).astype(bf16)
    dye=dy*ecum
    db=mm3(dgt,cf)+mm3(x*etail,ds,1,1)
    dc=mm3(dgt,bf,0,0)+mm3(dye,s,1,1)
    kk=jnp.sum(dsb.astype(f32)*sn_ref[...],axis=0,keepdims=True)
    rh,rl=split2(dyb.astype(f32)*(y_ref[...]-par_ref[7:8,:VW]*v)-xb.astype(f32)*dxd-xe.astype(f32)*bds)
    kh,kl=split2(jnp.concatenate([kk,jnp.zeros((7,VW),f32)],axis=0))
    hs=mm(jnp.concatenate([rh,rl,(v*dx).astype(bf16),jnp.concatenate([kh,kl],axis=0)],axis=0),hh_ref[...])
    dcum,q,k0=hs[:Q]+hs[Q:2*Q],hs[2*Q:3*Q],hs[3*Q:3*Q+1]+hs[3*Q+8:3*Q+9]
    da=k0+tri_sum(jnp.where(up,1.0,0.0).astype(bf16),dcum)
    dst=(q-da*edl)*sig(z)
    ds_ref[...]=ecum[Q-1:Q,:]*ds+mm3(cf,dye,0,0)
    sn_ref[...]=s
    acs_ref[0:1,:]+=jnp.sum(da*a,axis=0,keepdims=True)
    acs_ref[1:2,:]+=jnp.sum(dst,axis=0,keepdims=True)
    dv=dte*dx+par_ref[7:8,:VW]*dy
    acc_ref[5:6,:VW]+=jnp.sum(dy*v,axis=0,keepdims=True)
    dpre=jnp.concatenate([dv,db,dc],axis=1)*sl_ref[...]
    ext[0:Q,:]=dpre
    ext[Q:Q+8,:]=h_ref[...]
    h_ref[...]=dpre[0:8,:]
    xr=raw_ref[:,:CW]
    draw=ck_ref[3:4,:]*dpre
    acc_ref[3:4,:]+=jnp.sum(dpre*xr,axis=0,keepdims=True)
    acc_ref[4:5,:]+=jnp.sum(dpre,axis=0,keepdims=True)
    for j in (1,2,3):
        sh=ext[j:j+Q,:]
        draw=draw+ck_ref[3-j:4-j,:]*sh
        acc_ref[3-j:4-j,:]+=jnp.sum(sh*xr,axis=0,keepdims=True)
    out_ref[:,:CW]=draw.astype(bf16)
    out_ref[:,CW:]=dst.astype(bf16)

def sd(shape,dt=f32): return jax.ShapeDtypeStruct(shape,dt)

def hbm(shape,dt=f32): return pltpu.HBM(shape,dt)

def vmem(shape,dt=f32): return pltpu.VMEM(shape,dt)

def near_by(x): return pltpu.with_memory_space_constraint(x,pltpu.VMEM)

def stay(x): return pltpu.with_memory_space_constraint(x,pltpu.HBM)

def whole(shape): return pl.BlockSpec(shape,lambda i,*_: (0,)*len(shape))

def once(shape): return pl.BlockSpec(shape,lambda i,*_: (0,)*len(shape),pipeline_mode=pl.Buffered(1))

HL=VW//HW

def ssd_fwd(c0,nc,nall,first,raw,par,carry):
    rb=lambda w: pl.BlockSpec((Q,w),lambda i,*_: (c0+i,0))
    any_spec=pl.BlockSpec(memory_space=pl.ANY)
    held=[whole((NS,VW)),whole((8,CW))]
    return pl.pallas_call(partial(fwd_kernel,c0,nc),
        out_shape=(vmem((nall*Q,VW)),hbm((nall*Q,CW)),hbm((nall*Q,CW)),hbm((nall,NS,VW)),hbm((nall*Q,HL*Q),bf16),hbm((nall*Q,HL*Q)),sd((NS,VW)),sd((8,CW))),
        grid_spec=pltpu.PrefetchScalarGridSpec(num_scalar_prefetch=1,grid=(nc,),
            in_specs=[rb(RW),once((8,CW))]+(held+[any_spec]*6 if carry else []),
            out_specs=(rb(VW),rb(CW),rb(CW),pl.BlockSpec((1,NS,VW),lambda i,*_: (c0+i,0,0)),rb(HL*Q),rb(HL*Q),*held),
            scratch_shapes=[pltpu.VMEM((Q+8,CW),f32),pltpu.VMEM((256,VW),bf16)]),
        input_output_aliases={5+k:k for k in range(6)} if carry else {},
        compiler_params=pltpu.CompilerParams(vmem_limit_bytes=FWD_LIMIT),
        cost_estimate=pl.CostEstimate(flops=int(1.5e9*nc/8),bytes_accessed=30_000_000*nc//8,transcendentals=3_000_000*nc//8),
        name=f"ssd_forward_{c0}")(first,stay(raw),par,*(carry[6:]+(near_by(carry[0]),)+tuple(stay(x) for x in carry[1:6]) if carry else ()))

def ssd_bwd(c0,nc,nall,first,raw,act,sl,y,dy,sp,wt,lt,par,carry):
    rv=lambda w: pl.BlockSpec((Q,w),lambda i,*_: (c0+nc-1-i,0))
    any_spec=pl.BlockSpec(memory_space=pl.ANY)
    held=[whole((NS,VW)),whole((NS,VW)),whole((8,CW)),whole((8,CW)),whole((8,128))]
    return pl.pallas_call(partial(bwd_kernel,c0,nc,nall),
        out_shape=(vmem((nall*Q,RW),bf16),hbm((NS,VW)),hbm((NS,VW)),sd((8,CW)),sd((8,CW)),sd((8,128))),
        grid_spec=pltpu.PrefetchScalarGridSpec(num_scalar_prefetch=1,grid=(nc,),
            in_specs=[rv(RW),rv(CW),rv(CW),rv(VW),rv(VW),pl.BlockSpec((1,NS,VW),lambda i,*_: (c0+nc-1-i,0,0)),rv(HL*Q),rv(HL*Q),once((8,CW))]
                     +(held+[any_spec] if carry else []),
            out_specs=(rv(RW),*held),
            scratch_shapes=[pltpu.VMEM((Q+8,CW),f32),pltpu.VMEM((256,VW),bf16),pltpu.VMEM((VW,128),bf16)]),
        input_output_aliases={15:0} if carry else {},
        compiler_params=pltpu.CompilerParams(vmem_limit_bytes=BACK_LIMIT),
        cost_estimate=pl.CostEstimate(flops=int(3e9*nc/8),bytes_accessed=60_000_000*nc//8,transcendentals=4_000_000*nc//8),
        name=f"ssd_backward_{c0}")(first,stay(raw),stay(act),stay(sl),near_by(y),near_by(dy),stay(sp),stay(wt),stay(lt),par,*((stay(carry[1]),stay(carry[2]))+carry[3:]+(near_by(carry[0]),) if carry else ()))


D = 1536
H = 48
E = 3072
TOK_DEV = 1024
SEQ_DEV = 4
EPSILON = 1e-05
FWD_PARTS = ((0, 4), (4, 4))
BACK_PARTS = ((5, 3), (2, 3), (0, 2))


def contract(left, right, left_dim, right_dim, out=f32):
    return lax.dot_general(
        left, right, (((left_dim,), (right_dim,)), ((), ())), preferred_element_type=f32
    ).astype(out)


def span_layout(seq_lengths, seq_device, seq_offset, device):
    span_index = jnp.arange(SEQ_DEV, dtype=jnp.int32)
    needed = (seq_lengths + SPAN - 1) // SPAN
    owned_seq = (seq_device == device) & (seq_lengths > 0)
    relative = span_index[None, :] - seq_offset[:, None]
    inside = owned_seq[:, None] & (relative >= 0) & (relative < needed[:, None])
    live_rows = jnp.sum(
        jnp.where(inside, jnp.clip(seq_lengths[:, None] - relative * SPAN, 0, SPAN), 0), axis=0
    )
    seq_first = jnp.any(inside & (relative == 0), axis=0)
    return live_rows, seq_first.astype(jnp.int32)


def ring_order(count):
    if count == 8:
        return [0, 2, 4, 6, 7, 5, 3, 1]
    return list(range(count))


def lay(cols, rows, off_ref, refs, out):
    for k, (c0, w) in enumerate(cols):
        out[pl.ds(pl.multiple_of(off_ref[k] * rows, 16), rows), c0 : c0 + w] = refs[k][...]


def row_sums(x):
    a, b = split2(x)
    ones = jnp.ones((8, x.shape[1]), bf16)
    return mm(ones, a, 1, 1) + mm(ones, b, 1, 1)


def project_kernel(cols, rows, nx, off_ref, *refs):
    n = len(cols)
    xs = refs[n : n + nx]
    w_ref, x_ref, xt_ref, raw_ref = refs[n + nx :]
    i = pl.program_id(0)

    @pl.when(i == 0)
    def _():
        w_ref[:, CW:] = jnp.zeros((w_ref.shape[0], RW - CW), bf16)
        lay(cols, rows, off_ref, refs, w_ref)

    for k in range(nx):

        @pl.when(i == k)
        def _(k=k):
            x_ref[...] = xs[k][...]

    xt_ref[...] = x_ref[...].T
    raw_ref[...] = mm(x_ref[...], w_ref[...])


def project(pieces, offsets, xs, total):
    rows, n = pieces[0][0].shape[0], len(pieces)
    cols = [(c0, x.shape[1]) for x, c0 in pieces]
    width = RW
    q, depth = xs[0].shape
    nx = len(xs)
    at = lambda w: pl.BlockSpec((q, w), lambda i, off: (off[n + i], 0))
    return pl.pallas_call(
        partial(project_kernel, cols, rows, nx),
        out_shape=(hbm((total, width), bf16), sd((q * nx, depth), bf16), sd((depth, q * nx), bf16), hbm((q * nx, width))),
        grid_spec=pltpu.PrefetchScalarGridSpec(
            num_scalar_prefetch=1,
            grid=(nx,),
            in_specs=[once(x.shape) for x, _ in pieces] + [once(x.shape) for x in xs],
            out_specs=(whole((total, width)), at(depth), pl.BlockSpec((depth, q), lambda i, off: (0, off[n + i])), at(width)),
        ),
        compiler_params=pltpu.CompilerParams(vmem_limit_bytes=22 << 20),
        cost_estimate=pl.CostEstimate(flops=2 * q * nx * total * width, bytes_accessed=30_000_000, transcendentals=0),
        name="project",
    )(offsets, *[x for x, _ in pieces], *xs)


def cotangent_kernel(cols, rows, nx, off_ref, *refs):
    n = len(cols)
    xs = refs[n : n + nx]
    normed_ref, ssd_ref, gain_ref, w_ref, gr_ref, by_ref, sum_ref, yr_ref, x_ref = refs[n + nx :]
    i = pl.program_id(0)

    @pl.when(i == 0)
    def _():
        lay(cols, rows, off_ref, refs, w_ref)

    for k in range(nx):

        @pl.when(i == k)
        def _(k=k):
            x_ref[...] = xs[k][...]

    by = mm(x_ref[...], w_ref[:, VW:])
    gr = mm(normed_ref[...], w_ref[:, :VW])
    by_ref[...] = by
    gr_ref[...] = gr
    gated = ssd_ref[...] * (gr * sig(gr))
    scaled = gated * gain_ref[...]
    yr_ref[...] = scaled.astype(bf16)
    square = row_sums(gated * gated)
    cross = row_sums(by * scaled)
    top = lax.broadcasted_iota(jnp.int32, square.shape, 0) == 0
    sum_ref[0] = jnp.where(top, square, cross)


def cotangent(pieces, offsets, xs, normed, ssd, gain, total):
    rows, n = pieces[0][0].shape[0], len(pieces)
    cols = [(c0, x.shape[1]) for x, c0 in pieces]
    width = max(c0 + w for c0, w in cols)
    q, depth = xs[0].shape
    nx = len(xs)
    at = lambda w: pl.BlockSpec((q, w), lambda i, off: (off[n + i], 0))
    return pl.pallas_call(
        partial(cotangent_kernel, cols, rows, nx),
        out_shape=(
            vmem((total, width), bf16),
            sd((q * nx, VW)),
            sd((q * nx, VW)),
            sd((nx, 8, q)),
            sd((q * nx, VW), bf16),
        ),
        grid_spec=pltpu.PrefetchScalarGridSpec(
            num_scalar_prefetch=1,
            grid=(nx,),
            in_specs=[once(x.shape) for x, _ in pieces]
            + [once(x.shape) for x in xs]
            + [at(depth), at(VW), once((1, VW))],
            out_specs=(
                whole((total, width)),
                at(VW),
                at(VW),
                pl.BlockSpec((1, 8, q), lambda i, off: (off[n + i], 0, 0)),
                at(VW),
            ),
            scratch_shapes=[pltpu.VMEM((q, depth), bf16)],
        ),
        compiler_params=pltpu.CompilerParams(vmem_limit_bytes=30 << 20),
        cost_estimate=pl.CostEstimate(flops=2 * q * nx * total * width, bytes_accessed=30_000_000, transcendentals=800_000),
        name="cotangent",
    )(offsets, *[x for x, _ in pieces], *xs, normed, near_by(ssd), gain)


def turn_kernel(nx, off_ref, *refs):
    i = pl.program_id(0)
    for k in range(nx):

        @pl.when(i == k)
        def _(k=k):
            refs[nx][...] = refs[k][...].T


def turn(offsets, xs):
    q, depth = xs[0].shape
    nx = len(xs)
    n = offsets.shape[0] - nx
    return pl.pallas_call(
        partial(turn_kernel, nx),
        out_shape=sd((depth, q * nx), bf16),
        grid_spec=pltpu.PrefetchScalarGridSpec(
            num_scalar_prefetch=1,
            grid=(nx,),
            in_specs=[once(x.shape) for x in xs],
            out_specs=pl.BlockSpec((depth, q), lambda i, off: (0, off[n + i])),
        ),
        compiler_params=pltpu.CompilerParams(vmem_limit_bytes=8 << 20),
        cost_estimate=pl.CostEstimate(flops=0, bytes_accessed=10_000_000, transcendentals=0),
        name="turn",
    )(offsets, *xs)


def gate_kernel(sum_ref, by_ref, gr_ref, ssd_ref, gain_ref, ny_ref, bg_ref, dy_ref, gg_ref):
    @pl.when(pl.program_id(0) == 0)
    def _():
        gg_ref[...] = jnp.zeros_like(gg_ref)

    sums = sum_ref[0].T
    inv = lax.rsqrt(sums[:, 0:1] / E + EPSILON)
    gr, ssd, by, gain = gr_ref[...], ssd_ref[...], by_ref[...], gain_ref[...]
    sg = sig(gr)
    gate = gr * sg
    unit = ssd * gate * inv
    ny_ref[...] = (unit * gain).astype(bf16)
    gg_ref[0:1, :] += jnp.sum(by * unit, axis=0, keepdims=True)
    back = inv * (by * gain - unit * (inv * sums[:, 1:2] / E))
    bg_ref[...] = (back * ssd * (sg * (1.0 + gr - gate))).astype(bf16)
    dy_ref[...] = back * gate


def gate_back(sums, by, gate_raw, ssd, gain):
    t, width = by.shape
    n, _, q = sums.shape
    rb = pl.BlockSpec((q, width), lambda i: (i, 0))
    return pl.pallas_call(
        gate_kernel,
        out_shape=(sd((t, width), bf16), sd((t, width), bf16), vmem((t, width)), sd((8, width))),
        grid=(n,),
        in_specs=[pl.BlockSpec((1, 8, q), lambda i: (i, 0, 0)), rb, rb, rb, once((1, width))],
        out_specs=(rb, rb, rb, whole((8, width))),
        compiler_params=pltpu.CompilerParams(vmem_limit_bytes=12 << 20),
        cost_estimate=pl.CostEstimate(flops=20_000_000, bytes_accessed=15_000_000, transcendentals=800_000),
        name="gate_back",
    )(sums, by, gate_raw, near_by(ssd), gain)


def normed_kernel(
    half, at_ref, first_ref, gate_ref, w_ref, g_ref, x_ref, h_ref, m_ref, s_ref, mk_ref, mn_ref, ma_ref, mb_ref, away_ref, keep_ref, ng_ref, o_ref, scale_ref
):
    i = pl.program_id(0)

    @pl.when(i == 0)
    def _():
        ng_ref[...] = jnp.zeros_like(ng_ref)
        inv = lax.rsqrt(s_ref[0, 0:1, :] / E + EPSILON) * m_ref[...]
        scale_ref[...] = jnp.broadcast_to(inv, (8, inv.shape[1])).T

    n = o_ref.shape[0]
    scale = scale_ref[pl.ds(pl.multiple_of(i * n, 8), n), 0:1]
    far = jnp.where(i < half, ma_ref[...].astype(f32), mb_ref[...].astype(f32))
    mixed = mk_ref[0].astype(f32) + mn_ref[0].astype(f32) + far
    o_ref[...] = h_ref[...] + scale * mixed
    back = mm(first_ref[...], w_ref[...], 1, 1) + mm(gate_ref[...], g_ref[...], 1, 1)
    ng_ref[0:1, :] += jnp.sum(back * x_ref[...].astype(f32), axis=0, keepdims=True)

    @pl.when(i < half)
    def _():
        away_ref[0] = back.astype(bf16)

    @pl.when(i >= half)
    def _():
        keep_ref[0] = back.astype(bf16)


def back_normed_rows(at, q, first, gate, w, gate_w, normed, hidden, mask, sums, keep, near, far):
    depth = normed.shape[1]
    n = at.shape[0]
    half = n // 2
    rb = lambda c: pl.BlockSpec((q, c), lambda i, at: (at[i], 0))
    part = lambda c: pl.BlockSpec((q // n, c), lambda i, at: (i, 0))
    second = pl.BlockSpec((1, q // n, depth), lambda i, at: (1, i, 0))
    return pl.pallas_call(
        partial(normed_kernel, half),
        out_shape=(sd((half, q, depth), bf16), sd((half, q, depth), bf16), sd((8, depth)), sd((q, depth))),
        grid_spec=pltpu.PrefetchScalarGridSpec(
            num_scalar_prefetch=1,
            grid=(n,),
            in_specs=[rb(RW), rb(VW), once(w.shape), once((depth, VW)), rb(depth)]
            + [part(depth), whole((1, q)), pl.BlockSpec((1, 8, q), lambda i, at: (at[n - 1], 0, 0)), second, second]
            + [
                pl.BlockSpec((q // n, depth), lambda i, at: (jnp.minimum(i, half - 1), 0)),
                pl.BlockSpec((q // n, depth), lambda i, at: (jnp.maximum(i - half, 0), 0)),
            ],
            out_specs=(
                pl.BlockSpec((1, q, depth), lambda i, at: (jnp.minimum(i, half - 1), 0, 0)),
                pl.BlockSpec((1, q, depth), lambda i, at: (jnp.maximum(i - half, 0), 0, 0)),
                whole((8, depth)),
                part(depth),
            ),
            scratch_shapes=[pltpu.VMEM((q, 8), f32)],
        ),
        compiler_params=pltpu.CompilerParams(vmem_limit_bytes=22 << 20),
        cost_estimate=pl.CostEstimate(flops=2 * n * q * depth * (RW + VW), bytes_accessed=60_000_000, transcendentals=0),
        name="back_normed",
    )(at, near_by(first), gate, w, near_by(gate_w), normed, hidden, mask, sums, keep, near, *far)


def mixer_kernel(half, at_ref, x_ref, w_ref, away_ref, keep_ref):
    r = mm(x_ref[...], w_ref[...], 1, 1).astype(bf16)
    i = pl.program_id(0)

    @pl.when(i < half)
    def _():
        away_ref[0] = r

    @pl.when(i >= half)
    def _():
        keep_ref[0] = r


def mixer_blocks(at, q, x, w):
    n, depth, width = at.shape[0], w.shape[0], x.shape[1]
    half = n // 2
    return pl.pallas_call(
        partial(mixer_kernel, half),
        out_shape=(sd((half, q, depth), bf16), sd((half, q, depth), bf16)),
        grid_spec=pltpu.PrefetchScalarGridSpec(
            num_scalar_prefetch=1,
            grid=(n,),
            in_specs=[
                pl.BlockSpec((q, width), lambda i, at: (at[i], 0)),
                pl.BlockSpec((depth, width), lambda i, at: (0, 1), pipeline_mode=pl.Buffered(1)),
            ],
            out_specs=(
                pl.BlockSpec((1, q, depth), lambda i, at: (jnp.minimum(i, half - 1), 0, 0)),
                pl.BlockSpec((1, q, depth), lambda i, at: (jnp.maximum(i - half, 0), 0, 0)),
            ),
        ),
        compiler_params=pltpu.CompilerParams(vmem_limit_bytes=12 << 20),
        cost_estimate=pl.CostEstimate(flops=2 * n * q * depth * width, bytes_accessed=20_000_000, transcendentals=0),
        name="mixer_rows",
    )(at, x, near_by(w))


def grad_kernel(per, rows, at_ref, xt_ref, back_ref, out_ref):
    i = pl.program_id(0)
    r = mm(xt_ref[...], back_ref[...]).astype(bf16)
    for d in range(per):
        out_ref[pl.ds(at_ref[i * per + d], 1)] = r[d * rows : (d + 1) * rows][None]


def weight_grad(at, xt, back, n_dp):
    depth, t = xt.shape
    rows, width = depth // n_dp, back.shape[1]
    steps = 2
    return pl.pallas_call(
        partial(grad_kernel, n_dp // steps, rows),
        out_shape=sd((n_dp, rows, width), bf16),
        grid_spec=pltpu.PrefetchScalarGridSpec(
            num_scalar_prefetch=1,
            grid=(steps,),
            in_specs=[pl.BlockSpec((depth // steps, t), lambda i, at: (i, 0)), once(back.shape)],
            out_specs=whole((n_dp, rows, width)),
        ),
        compiler_params=pltpu.CompilerParams(vmem_limit_bytes=20 << 20),
        cost_estimate=pl.CostEstimate(flops=2 * depth * t * width, bytes_accessed=8_000_000, transcendentals=0),
        name="weight_grad",
    )(at, xt, near_by(back))


def far_pair_kernel(at_ref, xt_ref, back_ref, zt_ref, y_ref, f_ref, b_ref):
    f_ref[...] = mm(xt_ref[...], back_ref[...]).astype(bf16)
    b_ref[...] = mm(zt_ref[...], y_ref[...]).astype(bf16)


def far_value_kernel(mid, at_ref, xt_ref, back_ref, f_ref, b_ref):
    r = mm(xt_ref[...], back_ref[...]).astype(bf16)
    f_ref[...] = r[:, :mid]
    b_ref[...] = r[:, mid:]


def far_grad(at, rows, pairs, mid=0):
    depth, t = pairs[0][0].shape
    block = pl.BlockSpec((rows, t), lambda i, at: (at[0], 0))
    specs, args = [], []
    for xt, back in pairs:
        specs += [block, once(back.shape)]
        args += [xt, back]
    widths = (mid, pairs[0][1].shape[1] - mid) if mid else tuple(b.shape[1] for _, b in pairs)
    return pl.pallas_call(
        partial(far_value_kernel, mid) if mid else far_pair_kernel,
        out_shape=tuple(sd((rows, w), bf16) for w in widths),
        grid_spec=pltpu.PrefetchScalarGridSpec(
            num_scalar_prefetch=1,
            grid=(1,),
            in_specs=specs,
            out_specs=tuple(whole((rows, w)) for w in widths),
        ),
        compiler_params=pltpu.CompilerParams(vmem_limit_bytes=12 << 20),
        cost_estimate=pl.CostEstimate(flops=2 * rows * t * sum(widths), bytes_accessed=4_000_000, transcendentals=0),
        name="far_grad",
    )(at, *args)


def pair_grad_kernel(per, rows, at_ref, xt_ref, back_ref, zt_ref, y_ref, out_ref):
    i = pl.program_id(0)
    for k, r in enumerate((mm(xt_ref[...], back_ref[...]), mm(zt_ref[...], y_ref[...]))):
        r = r.astype(bf16)
        for d in range(per):
            out_ref[pl.ds(at_ref[i * per + d], 1), :, k * VW : (k + 1) * VW] = r[d * rows : (d + 1) * rows][None]


def pair_grad(at, xt, back, zt, y, n_dp):
    depth, t = xt.shape
    rows, steps = depth // n_dp, 4
    rb = pl.BlockSpec((depth // steps, t), lambda i, at: (i, 0))
    return pl.pallas_call(
        partial(pair_grad_kernel, n_dp // steps, rows),
        out_shape=sd((n_dp, rows, 2 * VW), bf16),
        grid_spec=pltpu.PrefetchScalarGridSpec(
            num_scalar_prefetch=1,
            grid=(steps,),
            in_specs=[rb, once(back.shape), rb, once(y.shape)],
            out_specs=whole((n_dp, rows, 2 * VW)),
        ),
        compiler_params=pltpu.CompilerParams(vmem_limit_bytes=22 << 20),
        cost_estimate=pl.CostEstimate(flops=4 * depth * t * VW, bytes_accessed=14_000_000, transcendentals=0),
        name="pair_grad",
    )(at, xt, back, zt, y)


def finish_kernel(
    x_ref, f_ref, b_ref, g_ref, small_ref, gv_ref, steps_ref, taps_ref, bias_ref, gain_ref, sb_ref, dl_ref, skip_ref
):
    value = x_ref[...].astype(f32) + f_ref[...].astype(f32) + b_ref[...].astype(f32)
    gv_ref[:, 0, :] = g_ref[...]
    gv_ref[:, 1, :] = value[:, :VW]
    heads = sb_ref.shape[0]
    steps_ref[...] = value[:, CW:].T[:heads, :]
    taps_ref[...] = small_ref[0:4, :VW]
    bias_ref[...] = small_ref[4, :VW]
    gain_ref[...] = small_ref[6, :VW]
    dl_ref[...] = small_ref[6, VW : VW + heads]
    sb_ref[...] = small_ref[6, VW + 128 : VW + 128 + heads]
    parts = jnp.concatenate(split3(small_ref[0:8, :VW]), axis=0)
    sums = mm(parts, sum_matrix((VW, 128)))
    skip_ref[...] = (sums[5:6] + sums[13:14] + sums[21:22])[0, :heads]


def finish(x, f, b, pair_out, small, heads):
    rows, width = x.shape
    full = whole((rows, width))
    outs = ((rows, 2, VW), (heads, rows), (4, VW), (VW,), (VW,), (heads,), (heads,), (heads,))
    return pl.pallas_call(
        finish_kernel,
        out_shape=tuple(sd(o) for o in outs),
        grid=(1,),
        in_specs=[full, full, full, pl.BlockSpec((rows, VW), lambda i: (0, 0)), whole(small.shape)],
        out_specs=tuple(whole(o) for o in outs),
        compiler_params=pltpu.CompilerParams(vmem_limit_bytes=16 << 20),
        cost_estimate=pl.CostEstimate(flops=1_000_000, bytes_accessed=5_000_000, transcendentals=0),
        name="finish",
    )(stay(x), stay(f), stay(b), stay(pair_out), small)


class Ring:
    def __init__(self, count):
        self.count = count
        self.half = count // 2
        self.order = ring_order(count)
        at = {d: i for i, d in enumerate(self.order)}
        self.table = [[self.order[(at[d] + k) % count] for k in range(count)] for d in range(count)]
        self.ahead = [(self.order[i], self.order[(i + 1) % count]) for i in range(count)]
        self.back = [(b, a) for a, b in self.ahead]

    def rows_of(self, table):
        return jnp.asarray(table, jnp.int32)[lax.axis_index("dp")]

    def hop(self, f, b):
        return lax.ppermute(f, "dp", self.ahead), lax.ppermute(b, "dp", self.back)


class Gather:
    def __init__(self, ring, x, c0=0):
        self.ring, self.mid, self.c0 = ring, x.shape[1] // 2 // 128 * 128, c0
        self.pieces, self.f, self.b, self.s = [(x, c0)], x, x, 0

    def ready(self):
        if self.s == self.ring.half - 1:
            return [self.f[:, : self.mid], self.b[:, self.mid :]]
        return [self.f, self.b]

    def step(self, f, b):
        self.s += 1
        self.f, self.b = self.ring.hop(f, b)
        self.pieces += [(self.f, self.c0), (self.b, self.c0 + (self.mid if self.s == self.ring.half else 0))]

    @staticmethod
    def offsets(ring):
        ahead = [0]
        for s in range(1, ring.half + 1):
            ahead += [ring.count - s, s]
        return [[ring.table[d][k] for k in ahead] for d in range(ring.count)]


class Scatter:
    def __init__(self, ring, first):
        self.ring, self.first, self.x, self.s = ring, list(first), None, ring.half

    def ready(self):
        x, s = self.x, self.s
        if s == self.ring.half:
            return self.first
        f, b = self.f, self.b
        if s == self.ring.half - 1:
            f = jnp.pad(f, ((0, 0), (0, x.shape[2] - f.shape[1])))
            b = jnp.pad(b, ((0, 0), (x.shape[2] - b.shape[1], 0)))
        f = x[s].astype(f32) + f.astype(f32)
        b = x[self.ring.count - s].astype(f32) + b.astype(f32)
        return [f.astype(bf16), b.astype(bf16)]

    def step(self, f, b):
        self.f, self.b = self.ring.hop(f, b)
        self.s -= 1

    def total(self, columns=slice(None)):
        return self.x[0, :, columns].astype(f32) + self.f[:, columns].astype(f32) + self.b[:, columns].astype(f32)


def swap(x, axis, count, bits):
    return lax.ppermute(x, axis, [(i, i ^ bits) for i in range(count)])


def tensor_order(count):
    keys = [0]
    bit = count // 2
    while bit:
        keys += [k ^ bit for k in keys]
        bit //= 2
    return keys


def pick(x, index, axis=0):
    return lax.dynamic_index_in_dim(x, index, axis, keepdims=False)


def groups_of(count):
    bits = [1 << k for k in range(count.bit_length() - 1)]
    first = len(bits) % 2
    return ([bits[:first]] if first else []) + [bits[k : k + 2] for k in range(first, len(bits), 2)]


def others(bits):
    return [bits[0]] if len(bits) == 1 else [bits[0], bits[1], bits[0] | bits[1]]


class Spread:
    def __init__(self, x, axis, count):
        self.x, self.axis, self.count, self.groups = x, axis, count, groups_of(count)

    def step(self, x):
        bits = self.groups.pop(0)
        self.x = sum((swap(x, self.axis, self.count, k) for k in others(bits)), x)


def together(*lists):
    flat = lax.optimization_barrier(tuple(x for xs in lists for x in xs))
    out, at = [], 0
    for xs in lists:
        out.append(list(flat[at : at + len(xs)]))
        at += len(xs)
    return out


def body(
    n_dp,
    n_tensor,
    hidden_in,
    norm_gain,
    gate_value_weight,
    state_proj_weight,
    step_weight,
    conv_value_kernel,
    conv_value_bias,
    conv_state_kernel,
    conv_state_bias,
    step_bias,
    decay_log,
    skip_scale,
    gate_norm_gain,
    out_weight,
    out_cotangent,
    seq_lengths,
    seq_device,
    seq_offset,
):
    quarter = hidden_in.shape[0]
    heads = step_weight.shape[1]
    rows = gate_value_weight.shape[0]
    me, dp = lax.axis_index("tensor"), lax.axis_index("dp")
    ring = Ring(n_dp)
    plan = [
        [ring.table[d].index(k) for k in range(n_dp)] + [ring.table[d][ring.half]] + Gather.offsets(ring)[d]
        for d in range(n_dp)
    ]
    plan = ring.rows_of(plan)
    ring_at, far_at = plan, plan[n_dp : n_dp + 1]
    order = me ^ jnp.asarray([3, 1, 2, 0], jnp.int32)
    offsets = jnp.concatenate([plan[n_dp + 1 :], me ^ jnp.asarray(tensor_order(n_tensor), jnp.int32)])
    to_core = lambda x: swap(x, "tensor", n_tensor, 1)
    to_far = lambda x: swap(x, "tensor", n_tensor, 2)

    live_rows, seq_first = span_layout(seq_lengths, seq_device, seq_offset, dp)
    row = me * quarter + jnp.arange(quarter, dtype=jnp.int32)
    local_live = jnp.sum(
        jnp.where((row // SPAN)[:, None] == jnp.arange(SEQ_DEV)[None, :], live_rows[None, :], 0), axis=1
    )
    local_mask = (row % SPAN < local_live).astype(f32)

    pad_to = lambda x, w: jnp.pad(x, (0, w - x.shape[0]))[None]
    params = jnp.concatenate(
        [
            jnp.concatenate([conv_value_kernel, conv_state_kernel], axis=0).T,
            jnp.concatenate([conv_value_bias, conv_state_bias])[None],
            pad_to(step_bias, CW),
            pad_to(decay_log, CW),
            pad_to(jnp.repeat(skip_scale, HW), CW),
        ],
        axis=0,
    )
    gain = gate_norm_gain[None]
    zeros = lambda *s: jnp.zeros(s, f32)

    first_own = jnp.concatenate(
        [gate_value_weight[:, 1, :], state_proj_weight, jnp.pad(step_weight, ((0, 0), (0, 16 - heads)))], axis=1
    )
    first_own, hidden, later = lax.optimization_barrier((first_own, hidden_in, gate_value_weight))
    inv_rms = lax.rsqrt(jnp.mean(hidden * hidden, axis=-1) + EPSILON)
    scaled = hidden * inv_rms[:, None]
    normed_local = (scaled * norm_gain[None, :]).astype(bf16)
    first = Gather(ring, first_own)
    first.step(*first.ready())
    far = to_far(normed_local)
    out_own = jnp.concatenate([later[:, 0, :], out_weight], axis=1)
    back_local = (local_mask[:, None] * out_cotangent).astype(bf16)
    (out_own, offsets, ring_at, far_at, order, seq_first, params, back_local) = lax.optimization_barrier(
        (out_own, offsets, ring_at, far_at, order, seq_first, params, back_local)
    )
    out = Gather(ring, out_own)
    for s in range(1, ring.half):
        extra = []
        if s == min(2, ring.half - 1):
            extra = [[normed_local, far]]
        elif s == ring.half - 1:
            extra = [[back_local] + normed_parts[2:]]
        sends = together(first.ready(), *extra)
        first.step(*sends.pop(0))
        if s == min(2, ring.half - 1):
            [a, far] = sends.pop(0)
            normed_parts = [a, far, to_core(a), to_core(far)]
        elif s == ring.half - 1:
            [back_local, *normed_parts[2:]] = sends.pop(0)
            back_far = to_far(back_local)
    ps, os = together([x for x, _ in first.pieces] + normed_parts, out.ready())
    out.step(*os)
    n = len(first.pieces)
    first_w, normed, normed_t, raw = project(
        [(x, c0) for x, (_, c0) in zip(ps, first.pieces)], offsets, ps[n:], D
    )
    chunks = TOK_DEV // Q
    carry = ()
    for k, (c0, n) in enumerate(FWD_PARTS):
        held, os, bs = together([carry[6]] if carry else [raw], out.ready(), [back_local, back_far] if k == 0 else [])
        out.step(*os)
        if k:
            carry = carry[:6] + (held[0],) + carry[7:]
        else:
            raw = held[0]
            back_parts = bs + [to_core(x) for x in bs]
        carry = tuple(ssd_fwd(c0, n, chunks, seq_first, raw, params, carry))
    held, os, back_parts = together([carry[0]], out.ready(), back_parts)
    carry = (held[0],) + carry[1:]
    out.step(*os)
    back_t = turn(offsets, back_parts)
    while out.s < ring.half:
        out.step(*out.ready())
    ssd, act, slope, states, weights_t, decays_t = carry[:6]

    out_w, gate_raw, back_y, sums, gated = cotangent(
        out.pieces, offsets, back_parts, normed, ssd, gain, D
    )
    total = Spread(sums, "tensor", n_tensor)
    while total.groups:
        total.step(total.x)
    sums = total.x
    mixer = mixer_blocks(order, quarter, gated, out_w)
    sums, mixer_away, mixer_keep = lax.optimization_barrier((sums, *mixer))
    normed_y, back_gate, back_ssd, gain_grad = gate_back(sums, back_y, gate_raw, ssd, gain)
    pair_sum = Scatter(ring, far_grad(far_at, rows, [(normed_t, back_gate), (back_t, normed_y)]))
    ps, [away, mixer_keep, back_gate, normed_y] = together(
        pair_sum.ready(), [mixer_away, mixer_keep, back_gate, normed_y]
    )
    pair_sum.step(*ps)
    mixer_near = to_core(away)
    pair_sum.x = pair_grad(ring_at, normed_t, back_gate, back_t, normed_y, n_dp)
    [pair_sum.f, pair_sum.b, pair_sum.x, mixer_near], = together([pair_sum.f, pair_sum.b, pair_sum.x, mixer_near])

    half_rows = quarter // 2
    away = (mixer_keep[0].astype(f32) + mixer_near[0].astype(f32)).astype(bf16)
    away = [away[:half_rows], away[half_rows:]]
    carry, held, mixer_far = (), [back_ssd], []
    for k, (c0, n) in enumerate(BACK_PARTS):
        ps = pair_sum.ready() if pair_sum.s else []
        held, ps, ms = together(held, ps, away[k : k + 1])
        if carry:
            carry = carry[:1] + (held[0],) + carry[2:]
        else:
            back_ssd = held[0]
        if pair_sum.s:
            pair_sum.step(*ps)
        ms = [to_far(x) for x in ms]
        carry = tuple(
            ssd_bwd(
                c0, n, chunks, seq_first, raw, act, slope, ssd, back_ssd, states, weights_t, decays_t, params, carry
            )
        )
        last = k == len(BACK_PARTS) - 1
        held, [pair_sum.f, pair_sum.b], ms = together([carry[0 if last else 1]], [pair_sum.f, pair_sum.b], ms)
        mixer_far += ms
    carry = (held[0],) + carry[1:]
    while pair_sum.s:
        pair_sum.step(*pair_sum.ready())
    back_first, _, _, _, acc, acs = carry
    value_sum = Scatter(ring, far_grad(far_at, rows, [(normed_t, back_first)], RW // 2 // 128 * 128))
    vs, [back_first] = together(value_sum.ready(), [back_first])
    value_sum.step(*vs)
    value_sum.x = weight_grad(ring_at, normed_t, back_first, n_dp)
    [value_sum.f, value_sum.b, value_sum.x, back_first], = together(
        [value_sum.f, value_sum.b, value_sum.x, back_first]
    )
    vs, [back_first] = together(value_sum.ready(), [back_first])
    value_sum.step(*vs)
    away, keep, ng, output = back_normed_rows(
        order, quarter, back_first, back_gate, first_w, out_w, normed, hidden_in, local_mask[None], sums, mixer_keep, mixer_near, mixer_far
    )
    [value_sum.f, value_sum.b, away, keep, ng], = together([value_sum.f, value_sum.b, away, keep, ng])
    shared = jnp.concatenate([acc[:5, VW:], (ng[0] / norm_gain).reshape(6, 256), zeros(5, 256)], axis=0)
    shared = Spread(shared, "tensor", n_tensor)
    vs, cs, ps = together(value_sum.ready(), [away], [shared.x])
    value_sum.step(*vs)
    near = to_core(cs[0])
    away = (keep[0].astype(f32) + near[0].astype(f32)).astype(bf16)
    got = to_far(away[:half_rows])
    shared.step(ps[0])
    [value_sum.f, value_sum.b, near, away, got, shared.x], = together(
        [value_sum.f, value_sum.b, near, away, got, shared.x]
    )
    own = jnp.concatenate(
        [acc[:6], jnp.concatenate([gain_grad[0], acs[0], acs[1]])[None], zeros(1, CW)], axis=0
    )
    while shared.groups:
        shared.step(shared.x)
    small = Spread(jnp.concatenate([own, shared.x.reshape(4, CW)], axis=0), "dp", n_dp)
    vs, cs, ps = together(value_sum.ready(), [away[half_rows:]], [small.x])
    value_sum.step(*vs)
    cs = [got, to_far(cs[0])]
    small.step(ps[0])
    while value_sum.s:
        value_sum.step(*value_sum.ready())
    [value_sum.f, value_sum.b, small.x], cs = together([value_sum.f, value_sum.b, small.x], cs)
    state_grad = value_sum.total(slice(VW, CW)).reshape(n_tensor, rows // n_tensor, 2 * NS)
    ps, ss = together([small.x], [pick(state_grad, me ^ k) for k in range(n_tensor)])
    state_out = sum((swap(ss[k], "tensor", n_tensor, k) for k in range(1, n_tensor)), ss[0])
    small.x = ps[0]
    while small.groups:
        small.step(small.x)
    small = small.x
    pair_out = pair_sum.total()
    gv_out, step_out, taps, bias, gains, steps, decays, skips = finish(
        value_sum.x[0], value_sum.f, value_sum.b, pair_out, small, heads
    )
    back_rows = keep[1].astype(f32) + near[1].astype(f32) + jnp.concatenate(cs, axis=0).astype(f32)
    back_scaled = back_rows * norm_gain[None, :]
    hidden_gradient = out_cotangent + inv_rms[:, None] * (
        back_scaled - scaled * jnp.mean(back_scaled * scaled, axis=-1)[:, None]
    )
    shared = small[8:].reshape(16, 256)
    index = dp * n_tensor + me
    all_count = n_dp * n_tensor
    kern_share = 2 * NS // all_count
    state_kernel_out = lax.dynamic_slice(shared, (0, index * kern_share), (5, kern_share))
    norm_out = lax.dynamic_slice(shared[5:11].reshape(D), (index * (D // all_count),), (D // all_count,))
    return (
        output,
        hidden_gradient,
        norm_out,
        gv_out,
        state_out,
        step_out.T,
        taps.T,
        bias,
        state_kernel_out[:4].T,
        state_kernel_out[4],
        steps,
        decays,
        skips,
        gains,
        pair_out[:, VW:],
    )


def solution(mesh):
    in_specs = (
        P(("dp", "tensor"), None),
        P(),
        P("dp", None, "tensor"),
        P("dp", None),
        P("dp", "tensor"),
        P("tensor", None),
        P("tensor"),
        P(),
        P(),
        P("tensor"),
        P("tensor"),
        P("tensor"),
        P("tensor"),
        P("dp", "tensor"),
        P(("dp", "tensor"), None),
        P(),
        P(),
        P(),
    )
    out_specs = (
        P(("dp", "tensor"), None),
        P(("dp", "tensor"), None),
        P(("dp", "tensor")),
        P("dp", None, "tensor"),
        P(("dp", "tensor"), None),
        P("dp", "tensor"),
        P("tensor", None),
        P("tensor"),
        P(("dp", "tensor"), None),
        P(("dp", "tensor")),
        P("tensor"),
        P("tensor"),
        P("tensor"),
        P("tensor"),
        P("dp", "tensor"),
    )
    return jax.shard_map(
        partial(body, mesh.shape["dp"], mesh.shape["tensor"]),
        mesh=mesh,
        in_specs=in_specs,
        out_specs=out_specs,
        check_vma=False,
    )
```
